32 devices in a mesh: dp: 2 (over x), seq: 16 (over z, y, core).
Axes of the slice: x: 2, y: 2, z: 4, core: 2. Of those that a mesh axis runs over, the one named last changes fastest.
Arguments:
- token_ids: int32 [2, 2048], P('dp', 'seq'), may hold values from 0 to 11
- embed_table: float32 [12, 768], replicated, may hold values from -6 to 6
- gain_one: float32 [768], replicated, may hold values from 0.1 to 1.9
- bias_one: float32 [768], replicated, may hold values from -1.75 to 1.75
- in_weight: float32 [768, 2304], P(('dp', 'seq')), may hold values from -0.21875 to 0.21875
- in_bias: float32 [2304], replicated, may hold values from -1.75 to 1.75
- short_taps: float32 [3, 2304], replicated, may hold values from -3.5 to 3.5
- short_bias: float32 [2304], replicated, may hold values from -1.75 to 1.75
- freq_weight: float32 [33, 64], replicated, may hold values from -6 to 6
- freq_bias: float32 [64], replicated, may hold values from -3.140625 to 3.140625
- inner_weight: float32 [64, 64], replicated, may hold values from -3 to 3
- inner_bias: float32 [64], replicated, may hold values from -3.140625 to 3.140625
- filter_weight: float32 [1536, 64], P(('dp', 'seq')), may hold values from -0.046875 to 0.046875
- skip_scale: float32 [2, 768], replicated, may hold values from -6 to 6
- out_weight: float32 [768, 768], P(('dp', 'seq')), may hold values from -0.21875 to 0.21875
- out_bias: float32 [768], replicated, may hold values from -1.75 to 1.75
- gain_two: float32 [768], replicated, may hold values from 0.1 to 1.9
- bias_two: float32 [768], replicated, may hold values from -1.75 to 1.75
- up_weight: float32 [768, 3072], P(('dp', 'seq')), may hold values from -0.21875 to 0.21875
- up_bias: float32 [3072], replicated, may hold values from -1.75 to 1.75
- down_weight: float32 [3072, 768], P(('dp', 'seq')), may hold values from -0.21875 to 0.21875
- down_bias: float32 [768], replicated, may hold values from -1.75 to 1.75
- cotangent: bfloat16 [2, 2048, 768], P('dp', 'seq'), may hold values from -6 to 6
Outputs:
- block_out: float32 [2, 2048, 768], P('dp', 'seq')
- grad_embed: float32 [12, 768], replicated
- grad_gain_one: float32 [768], replicated
- grad_bias_one: float32 [768], replicated
- grad_in_weight: float32 [768, 2304], P(('dp', 'seq'))
- grad_in_bias: float32 [2304], replicated
- grad_short_taps: float32 [3, 2304], replicated
- grad_short_bias: float32 [2304], replicated
- grad_freq_weight: float32 [33, 64], replicated
- grad_freq_bias: float32 [64], replicated
- grad_inner_weight: float32 [64, 64], replicated
- grad_inner_bias: float32 [64], replicated
- grad_filter_weight: float32 [1536, 64], P(('dp', 'seq'))
- grad_skip_scale: float32 [2, 768], replicated
- grad_out_weight: float32 [768, 768], P(('dp', 'seq'))
- grad_out_bias: float32 [768], replicated
- grad_gain_two: float32 [768], replicated
- grad_bias_two: float32 [768], replicated
- grad_up_weight: float32 [768, 3072], P(('dp', 'seq'))
- grad_up_bias: float32 [3072], replicated
- grad_down_weight: float32 [3072, 768], P(('dp', 'seq'))
- grad_down_bias: float32 [768], replicated
The draws below stay inside these ranges and needn't reach their ends.
All inputs are finite; a program needn't handle non-finite values.
Results may differ from the reference program's by a relative error of at most 0.012.
Values may be sent and summed in bfloat16 or wider, within the bound.
A program may use at most 192 MiB of HBM per device.

```python
import math
import jax
import jax.numpy as jnp
from jax import lax

D = 768
FF = 3072
VOCAB = 12
FEAT = 33
ORDER = 64
SEQS = 2
SEQLEN = 2048


def touch_ends(values, own_key, low, top_value):
    place = [jax.random.randint(jax.random.fold_in(own_key, axis), (), 0, length) for axis, length in enumerate(values.shape)]
    longest = values.shape.index(max(values.shape))
    beside = place[:longest] + [(place[longest] + 1) % values.shape[longest]] + place[longest + 1:]
    return values.at[tuple(place)].set(low).at[tuple(beside)].set(top_value)


def level_of(stream_key, shape, cuts, least, largest):
    factor_of, own = 1.0, jax.random.fold_in(stream_key, 6)
    for position, shards_of in cuts:
        heights = jnp.exp(jax.random.uniform(jax.random.fold_in(own, position), (shards_of,), jnp.float32, least / len(cuts), largest / len(cuts)))
        factor_of = factor_of * jnp.repeat(heights, shape[position] // shards_of).reshape([-1 if axis == position else 1 for axis in range(len(shape))])
    return factor_of


def noise(own_key, shape, deviation, limit, cuts=(), kind=jnp.bfloat16):
    gain = level_of(own_key, shape, cuts, -0.22, 0.18) if cuts else 1.0
    result = jax.random.normal(own_key, shape, jnp.float32) * deviation * gain
    return jnp.minimum(jnp.maximum(result, -limit), limit).astype(kind)


def setup_inputs(seed: int = 0) -> dict:
    streams_of = jax.random.split(jax.random.key(seed), 24)
    return {
        "token_ids": touch_ends(jax.random.randint(streams_of[0], (SEQS, SEQLEN), 0, VOCAB), jax.random.fold_in(streams_of[0], 1), 0, VOCAB - 1).astype(jnp.int32),
        "embed_table": noise(streams_of[1], (VOCAB, D), 1.0, 6.0, (), jnp.float32),
        "gain_one": jnp.clip(1.0 + 0.18 * jax.random.normal(streams_of[2], (D,), jnp.float32), 0.1, 1.9),
        "bias_one": noise(streams_of[3], (D,), 0.3, 1.75, (), jnp.float32),
        "in_weight": noise(streams_of[4], (D, 3 * D), D ** -0.5, 0.21875, ((0, 32),), jnp.float32),
        "in_bias": noise(streams_of[5], (3 * D,), 0.3, 1.75, (), jnp.float32),
        "short_taps": noise(streams_of[6], (3, 3 * D), 0.6, 3.5, (), jnp.float32),
        "short_bias": noise(streams_of[7], (3 * D,), 0.3, 1.75, (), jnp.float32),
        "freq_weight": noise(streams_of[8], (FEAT, ORDER), 1.0, 6.0, (), jnp.float32),
        "freq_bias": jnp.clip(jax.random.uniform(streams_of[9], (ORDER,), jnp.float32, -3.140625, 3.140625), -3.140625, 3.140625),
        "inner_weight": noise(streams_of[10], (ORDER, ORDER), 0.5, 3.0, (), jnp.float32),
        "inner_bias": jnp.clip(jax.random.uniform(streams_of[11], (ORDER,), jnp.float32, -3.140625, 3.140625), -3.140625, 3.140625),
        "filter_weight": noise(streams_of[12], (2 * D, ORDER), (ORDER * SEQLEN // 8) ** -0.5, 0.046875, ((0, 32),), jnp.float32),
        "skip_scale": noise(streams_of[13], (2, D), 1.0, 6.0, (), jnp.float32),
        "out_weight": noise(streams_of[14], (D, D), D ** -0.5, 0.21875, ((0, 32),), jnp.float32),
        "out_bias": noise(streams_of[15], (D,), 0.3, 1.75, (), jnp.float32),
        "gain_two": jnp.clip(1.0 + 0.18 * jax.random.normal(streams_of[16], (D,), jnp.float32), 0.1, 1.9),
        "bias_two": noise(streams_of[17], (D,), 0.3, 1.75, (), jnp.float32),
        "up_weight": noise(streams_of[18], (D, FF), D ** -0.5, 0.21875, ((0, 32),), jnp.float32),
        "up_bias": noise(streams_of[19], (FF,), 0.3, 1.75, (), jnp.float32),
        "down_weight": noise(streams_of[20], (FF, D), (FF // 4) ** -0.5, 0.21875, ((0, 32),), jnp.float32),
        "down_bias": noise(streams_of[21], (D,), 0.3, 1.75, (), jnp.float32),
        "cotangent": noise(streams_of[22], (SEQS, SEQLEN, D), 1.0, 6.0, ((0, 2), (1, 16))),
    }


@jax.custom_vjp
def low(v):
    return lax.optimization_barrier(v.astype(jnp.bfloat16)).astype(jnp.float32)

@jax.custom_vjp
def low_back(v):
    return v

def low_keep(v):
    return (low(v), None)

def low_pass(kept, grad):
    return (grad,)

def back_keep(v):
    return (v, None)

def back_low(kept, grad):
    return (low(grad),)
low.defvjp(low_keep, low_pass)
low_back.defvjp(back_keep, back_low)
epsilon = 1e-05
slow_rate = -math.log(0.01) / 1.5
fast_rate = -math.log(0.01) / 0.3
decay_shift = 0.05

def matmul(left_side, right_side):
    return jnp.dot(left_side, right_side, precision=lax.Precision.HIGHEST, preferred_element_type=jnp.float32)

def layer_norm(values, scales, offsets):
    center = values - lax.optimization_barrier(jnp.mean(values, axis=-1, keepdims=True))
    inverse = lax.rsqrt(lax.optimization_barrier(jnp.mean(center * center, axis=-1, keepdims=True)) + epsilon)
    return center * inverse * scales + offsets

def long_conv(signal, kernel):
    length = signal.shape[0]
    spectrum = jnp.fft.rfft(signal, n=2 * length, axis=0) * jnp.fft.rfft(kernel, n=2 * length, axis=0)
    return jnp.fft.irfft(spectrum, n=2 * length, axis=0)[:length]

def filter_inputs():
    count = (FEAT - 1) // 2
    position_phase = jnp.arange(SEQLEN, dtype=jnp.float32) / SEQLEN
    levels = 0.0001 + jnp.arange(count, dtype=jnp.float32) * ((count - 1 - 0.0001) / (count - 1))
    angles = 2.0 * math.pi * position_phase[:, None] * levels[None, :]
    features = jnp.concatenate([position_phase[:, None], jnp.cos(angles), -jnp.sin(angles)], axis=1)
    channel = jnp.arange(D, dtype=jnp.float32) / (D - 1)
    decay_rate = slow_rate + (fast_rate - slow_rate) * channel
    decay = jnp.exp(-position_phase[:, None] * decay_rate[None, :]) + decay_shift
    return (features, decay)

def forward(params, token_row):
    embed_table, gain_one, bias_one, in_weight, in_bias, short_taps, short_bias, freq_weight, freq_bias, inner_weight, inner_bias, filter_weight, skip_scale, out_weight, out_bias, gain_two, bias_two, up_weight, up_bias, down_weight, down_bias = params
    hidden = jnp.take(embed_table, token_row, axis=0)
    normed = low(layer_norm(hidden, gain_one, bias_one))
    projected = low_back(matmul(normed, low(in_weight))) + in_bias
    padded = jnp.concatenate([jnp.zeros((2, 3 * D), jnp.float32), projected], axis=0)
    mixed = short_taps[0] * padded[:-2] + short_taps[1] * padded[1:-1] + short_taps[2] * padded[2:] + short_bias
    gate_outer = mixed[:, :D]
    gate_inner = mixed[:, D:2 * D]
    value_part = mixed[:, 2 * D:]
    features, decay = filter_inputs()
    first_act = jnp.sin(matmul(features, freq_weight) + freq_bias)
    second_act = jnp.sin(matmul(first_act, inner_weight) + inner_bias)
    kernels = matmul(second_act, low(filter_weight).T)
    first_conv = long_conv(value_part, kernels[:, :D] * decay) + skip_scale[0] * value_part
    gated = gate_inner * first_conv
    second_conv = long_conv(gated, kernels[:, D:] * decay) + skip_scale[1] * gated
    mixer = low(gate_outer * second_conv)
    residual = hidden + low_back(matmul(mixer, low(out_weight))) + out_bias
    normed_two = low(layer_norm(residual, gain_two, bias_two))
    lifted = low_back(matmul(normed_two, low(up_weight))) + up_bias
    activated = low(jax.nn.gelu(lifted, approximate=False))
    return residual + low_back(matmul(activated, low(down_weight))) + down_bias

def reference(token_ids, embed_table, gain_one, bias_one, in_weight, in_bias, short_taps, short_bias, freq_weight, freq_bias, inner_weight, inner_bias, filter_weight, skip_scale, out_weight, out_bias, gain_two, bias_two, up_weight, up_bias, down_weight, down_bias, cotangent):
    params = (embed_table, gain_one, bias_one, in_weight, in_bias, short_taps, short_bias, freq_weight, freq_bias, inner_weight, inner_bias, filter_weight, skip_scale, out_weight, out_bias, gain_two, bias_two, up_weight, up_bias, down_weight, down_bias)

    def one_sequence(totals, inputs):
        token_row, seed_row = inputs
        output, pullback = jax.vjp(lambda *weights: forward(weights, token_row), *params)
        gradients = pullback(seed_row.astype(jnp.float32))
        return (tuple((running + update for running, update in zip(totals, gradients))), output)
    initial = tuple((jnp.zeros_like(tensor) for tensor in params))
    sums, outputs = lax.scan(one_sequence, initial, (token_ids, cotangent))
    return (outputs, sums[0], sums[1], sums[2], sums[3], sums[4], sums[5], sums[6], sums[7], sums[8], sums[9], sums[10], sums[11], sums[12], sums[13], sums[14], sums[15], sums[16], sums[17], sums[18], sums[19], sums[20])
```

```python
import math
from types import SimpleNamespace

import jax
import jax.numpy as jnp
import ml_dtypes
import numpy as np
from jax import lax
from jax.experimental import pallas as pl
from jax.experimental.pallas import tpu as pltpu
from jax.sharding import PartitionSpec as P

epsilon = 1e-05
slow_rate = -math.log(0.01) / 1.5
fast_rate = -math.log(0.01) / 0.3
decay_shift = 0.05
highest = lax.Precision.HIGHEST


def exact_dot(left_side, right_side):
    return jnp.dot(left_side, right_side, precision=highest, preferred_element_type=jnp.float32)


def narrow_dot(left_side, right_side):
    return jnp.dot(left_side, right_side, preferred_element_type=jnp.float32)


def rows_inner(left_side, right_side, accuracy=None):
    return lax.dot_general(
        left_side,
        right_side,
        (((0,), (0,)), ((), ())),
        precision=accuracy,
        preferred_element_type=jnp.float32,
    )


def against_rows(left_side, right_side, accuracy=None):
    return lax.dot_general(
        left_side,
        right_side,
        (((1,), (1,)), ((), ())),
        precision=accuracy,
        preferred_element_type=jnp.float32,
    )


def normalize(values):
    center = values - jnp.mean(values, axis=-1, keepdims=True)
    inverse = lax.rsqrt(jnp.mean(center * center, axis=-1, keepdims=True) + epsilon)
    return (center * inverse, inverse)


def norm_back(upstream, unit_vals, inverse):
    return inverse * (
        upstream
        - jnp.mean(upstream, axis=-1, keepdims=True)
        - unit_vals * jnp.mean(upstream * unit_vals, axis=-1, keepdims=True)
    )


def angle_table(row_count, column_count, modulus):
    product = (
        jnp.arange(row_count, dtype=jnp.int32)[:, None]
        * jnp.arange(column_count, dtype=jnp.int32)[None, :]
        % modulus
    )
    angles = 2.0 * math.pi / modulus * product.astype(jnp.float32)
    return (jnp.cos(angles), jnp.sin(angles))


def forward_transform(signal, tables):
    cos_section, sin_section, cos_twist, sin_twist, cos_last, sin_last = tables
    real_first = jnp.einsum("kn,...nm->...km", cos_section, signal, precision=highest)
    imag_first = -jnp.einsum("kn,...nm->...km", sin_section, signal, precision=highest)
    real_turn = real_first * cos_twist + imag_first * sin_twist
    imag_turn = imag_first * cos_twist - real_first * sin_twist
    real_out = exact_dot(real_turn, cos_last) + exact_dot(imag_turn, sin_last)
    imag_out = exact_dot(imag_turn, cos_last) - exact_dot(real_turn, sin_last)
    return (real_out, imag_out)


def inverse_transform(real_spec, imag_spec, tables):
    cos_section, sin_section, cos_twist, sin_twist, cos_last, sin_last = tables
    real_turn = exact_dot(real_spec, cos_last) - exact_dot(imag_spec, sin_last)
    imag_turn = exact_dot(imag_spec, cos_last) + exact_dot(real_spec, sin_last)
    real_first = real_turn * cos_twist - imag_turn * sin_twist
    imag_first = imag_turn * cos_twist + real_turn * sin_twist
    signal = jnp.einsum("kn,...km->...nm", cos_section, real_first, precision=highest) - jnp.einsum(
        "kn,...km->...nm", sin_section, imag_first, precision=highest
    )
    return signal / (cos_twist.shape[0] * cos_twist.shape[1])


def multiply(real_one, imag_one, real_two, imag_two):
    return (real_one * real_two - imag_one * imag_two, real_one * imag_two + imag_one * real_two)


def multiply_conj(real_one, imag_one, real_two, imag_two):
    return (real_one * real_two + imag_one * imag_two, imag_one * real_two - real_one * imag_two)


def to_channels(rows_in):
    return lax.all_to_all(rows_in.T, "seq", split_axis=0, concat_axis=1, tiled=True)


def to_rows(columns):
    return lax.all_to_all(columns, "seq", split_axis=1, concat_axis=0, tiled=True).T


def gather_all(pieces):
    shapes = [piece.shape for piece in pieces]
    flat = jnp.concatenate([piece.astype(jnp.bfloat16).reshape(-1) for piece in pieces])
    whole = lax.all_gather(flat, ("dp", "seq"), axis=0, tiled=False)
    result, start = [], 0
    for shape in shapes:
        size = math.prod(shape)
        result.append(whole[:, start : start + size].reshape((-1,) + shape[1:]))
        start += size
    return result


def per_device(
    token_ids,
    embed_table,
    gain_one,
    bias_one,
    in_weight,
    in_bias,
    short_taps,
    short_bias,
    freq_weight,
    freq_bias,
    inner_weight,
    inner_bias,
    filter_weight,
    skip_scale,
    out_weight,
    out_bias,
    gain_two,
    bias_two,
    up_weight,
    up_bias,
    down_weight,
    down_bias,
    cotangent,
):
    tokens = token_ids[0]
    row_count = tokens.shape[0]
    vocab, model_width = embed_table.shape
    seq_parts = lax.axis_size("seq")
    seq_index = lax.axis_index("seq")
    dp_index = lax.axis_index("dp")
    local_width = model_width // seq_parts
    length = row_count * seq_parts
    freq_rows = 2 * seq_parts
    low_rows = seq_index * local_width

    def own_channels(table):
        parts = table.reshape(table.shape[0], -1, model_width)
        return lax.dynamic_slice_in_dim(parts, low_rows, local_width, 2)

    in_full, out_full, up_full, down_full, filter_full, tokens_full = gather_all(
        (in_weight, out_weight, up_weight, down_weight, filter_weight, token_ids)
    )
    sequence = lax.dynamic_slice_in_dim(
        tokens_full.reshape(-1, length), dp_index, 1, 0
    )[0].astype(jnp.int32)
    cos_section, sin_section = angle_table(freq_rows, seq_parts, freq_rows)
    cos_twist, sin_twist = angle_table(freq_rows, row_count, freq_rows * row_count)
    cos_last, sin_last = angle_table(row_count, row_count, row_count)
    tables = (cos_section, sin_section, cos_twist, sin_twist, cos_last, sin_last)

    unit_one, inverse_one = normalize(embed_table)
    normed = (unit_one * gain_one + bias_one).astype(jnp.bfloat16)
    table = narrow_dot(normed, in_full) + in_bias
    local_table = own_channels(table)
    local_taps = own_channels(short_taps)
    local_bias = own_channels(short_bias[None])[0]
    local_skip = own_channels(skip_scale)[:, 0, :, None]
    ids = jnp.arange(vocab, dtype=jnp.int32)[:, None]
    padded = jnp.concatenate([jnp.full((2,), -1, jnp.int32), sequence])
    shifted = jnp.concatenate(
        [(padded[None, j : j + length] == ids).astype(jnp.float32) for j in range(3)], axis=0
    )
    weights = (local_taps[:, None] * local_table[None]).reshape(3 * vocab, 3 * local_width)
    mixed = rows_inner(weights, shifted, highest) + local_bias.reshape(-1, 1)
    gate_outer = mixed[:local_width]
    gate_inner = mixed[local_width : 2 * local_width]
    value_part = mixed[2 * local_width :]

    count = (freq_weight.shape[0] - 1) // 2
    position_phase = jnp.arange(length, dtype=jnp.float32) / length
    levels = 0.0001 + jnp.arange(count, dtype=jnp.float32) * ((count - 1 - 0.0001) / (count - 1))
    angles = 2.0 * math.pi * position_phase[None, :] * levels[:, None]
    features = jnp.concatenate([position_phase[None, :], jnp.cos(angles), -jnp.sin(angles)], axis=0)
    first_pre = rows_inner(freq_weight, features, highest) + freq_bias[:, None]
    first_act = jnp.sin(first_pre)
    second_pre = rows_inner(inner_weight, first_act, highest) + inner_bias[:, None]
    second_act = jnp.sin(second_pre)
    channel = (low_rows + jnp.arange(local_width, dtype=jnp.int32)).astype(jnp.float32) / (
        model_width - 1
    )
    decay_rate = slow_rate + (fast_rate - slow_rate) * channel
    decay = jnp.exp(-position_phase[None, :] * decay_rate[:, None]) + decay_shift
    local_filter = lax.dynamic_slice_in_dim(
        filter_full.reshape(2, model_width, -1), low_rows, local_width, 1
    ).astype(jnp.float32).reshape(2 * local_width, -1)
    kernels = exact_dot(local_filter, second_act).reshape(2, local_width, length) * decay

    def forth(signal):
        shape = signal.shape[:-1] + (seq_parts, row_count)
        return forward_transform(signal.reshape(shape), tables)

    def back(real_spec, imag_spec):
        result = inverse_transform(real_spec, imag_spec, tables)
        return result.reshape(result.shape[:-2] + (length,))

    kernel_real, kernel_imag = forth(kernels)
    value_real, value_imag = forth(value_part)
    first_conv = (
        back(*multiply(value_real, value_imag, kernel_real[0], kernel_imag[0]))
        + local_skip[0] * value_part
    )
    gated = gate_inner * first_conv
    gated_real, gated_imag = forth(gated)
    second_conv = (
        back(*multiply(gated_real, gated_imag, kernel_real[1], kernel_imag[1]))
        + local_skip[1] * gated
    )
    mixer = to_rows((gate_outer * second_conv).astype(jnp.bfloat16))

    onehot = (tokens[:, None] == ids[:, 0][None, :]).astype(jnp.float32)
    hidden = exact_dot(onehot, embed_table)
    residual = hidden + narrow_dot(mixer, out_full) + out_bias
    unit_two, inverse_two = normalize(residual)
    normed_two = (unit_two * gain_two + bias_two).astype(jnp.bfloat16)
    lifted = narrow_dot(normed_two, up_full) + up_bias
    normal_cdf = 0.5 * (1.0 + lax.erf(lifted * (1.0 / math.sqrt(2.0))))
    activated = (lifted * normal_cdf).astype(jnp.bfloat16)
    block_out = residual + narrow_dot(activated, down_full) + down_bias
    seed_low = cotangent[0]
    seed = seed_low.astype(jnp.float32)
    grad_down_bias = jnp.sum(seed, axis=0)
    grad_down = rows_inner(activated, seed_low)
    grad_activated = against_rows(seed_low, down_full)
    normal_pdf = jnp.exp(-0.5 * lifted * lifted) * (1.0 / math.sqrt(2.0 * math.pi))
    grad_lifted = grad_activated * (normal_cdf + lifted * normal_pdf)
    grad_up_bias = jnp.sum(grad_lifted, axis=0)
    lifted_low = grad_lifted.astype(jnp.bfloat16)
    grad_up = rows_inner(normed_two, lifted_low)
    grad_normed_two = against_rows(lifted_low, up_full)
    grad_gain_two = jnp.sum(grad_normed_two * unit_two, axis=0)
    grad_bias_two = jnp.sum(grad_normed_two, axis=0)
    grad_residual = seed + norm_back(grad_normed_two * gain_two, unit_two, inverse_two)
    grad_out_bias = jnp.sum(grad_residual, axis=0)
    residual_low = grad_residual.astype(jnp.bfloat16)
    grad_out = rows_inner(mixer, residual_low)
    grad_mixer = to_channels(against_rows(residual_low, out_full).astype(jnp.bfloat16)).astype(
        jnp.float32
    )
    embed_sum = rows_inner(onehot, grad_residual, highest)

    grad_outer = grad_mixer * second_conv
    grad_second = grad_mixer * gate_outer
    skip_second = jnp.sum(grad_second * gated, axis=1)
    back_real, back_imag = forth(grad_second)
    grad_gated = grad_second * local_skip[1] + back(
        *multiply_conj(back_real, back_imag, kernel_real[1], kernel_imag[1])
    )
    kernel_grad_two = back(*multiply_conj(back_real, back_imag, gated_real, gated_imag))
    grad_inner_gate = grad_gated * first_conv
    grad_first = grad_gated * gate_inner
    skip_first = jnp.sum(grad_first * value_part, axis=1)
    early_real, early_imag = forth(grad_first)
    grad_value = grad_first * local_skip[0] + back(
        *multiply_conj(early_real, early_imag, kernel_real[0], kernel_imag[0])
    )
    kernel_grad_one = back(*multiply_conj(early_real, early_imag, value_real, value_imag))
    grad_mixed = jnp.concatenate([grad_outer, grad_inner_gate, grad_value], axis=0)
    id_sums = against_rows(shifted, grad_mixed, highest).reshape(3, vocab, 3, local_width)
    local_sums = jnp.sum(id_sums * local_taps[:, None], axis=0)
    local_taps_grad = jnp.sum(id_sums * local_table[None], axis=1)
    local_short_bias = jnp.sum(id_sums[2], axis=0, keepdims=True)
    local_small = jnp.concatenate(
        [
            local_sums,
            local_taps_grad,
            local_short_bias,
            jnp.pad(jnp.stack([skip_first, skip_second])[:, None], ((0, 0), (0, 2), (0, 0))),
        ],
        axis=0,
    )
    wide_small = lax.dynamic_update_slice_in_dim(
        jnp.zeros((local_small.shape[0], 3, model_width), jnp.float32), local_small, low_rows, 2
    )

    raw_grads = (jnp.stack([kernel_grad_one, kernel_grad_two]) * decay).reshape(
        2 * local_width, length
    )
    grad_local_filter = against_rows(raw_grads, second_act, highest).reshape(2, local_width, -1)
    grad_second_act = rows_inner(local_filter, raw_grads, highest)
    grad_second_pre = grad_second_act * jnp.cos(second_pre)
    grad_inner_weight = against_rows(first_act, grad_second_pre, highest)
    grad_inner_bias = jnp.sum(grad_second_pre, axis=1)
    grad_first_pre = exact_dot(inner_weight, grad_second_pre) * jnp.cos(first_pre)
    grad_freq_weight = against_rows(features, grad_first_pre, highest)
    grad_freq_bias = jnp.sum(grad_first_pre, axis=1)
    sum_filter = lax.psum_scatter(grad_local_filter, "dp", scatter_dimension=0, tiled=False)

    devices = lax.axis_size("dp") * seq_parts
    up_rows = model_width // devices
    pieces = jnp.concatenate(
        [
            grad_up.reshape(devices, -1, model_width),
            grad_down.reshape(devices, -1, model_width),
            grad_out.reshape(devices, -1, model_width),
        ],
        axis=1,
    )
    summed = lax.psum_scatter(pieces, ("dp", "seq"), scatter_dimension=0, tiled=False)
    up_size = up_rows * up_weight.shape[1] // model_width
    sum_up = summed[:up_size].reshape(up_weight.shape)
    sum_down = summed[up_size : up_size + down_weight.shape[0]]
    sum_out = summed[up_size + down_weight.shape[0] :]

    (
        wide_small,
        embed_sum,
        sum_freq_weight,
        sum_freq_bias,
        sum_inner_weight,
        sum_inner_bias,
        sum_out_bias,
        sum_gain_two,
        sum_bias_two,
        sum_up_bias,
        sum_down_bias,
    ) = lax.psum(
        (
            wide_small,
            embed_sum,
            grad_freq_weight,
            grad_freq_bias,
            grad_inner_weight,
            grad_inner_bias,
            grad_out_bias,
            grad_gain_two,
            grad_bias_two,
            grad_up_bias,
            grad_down_bias,
        ),
        ("dp", "seq"),
    )
    total_ids = wide_small[:vocab].reshape(vocab, 3 * model_width)
    sum_taps = wide_small[vocab : vocab + 3].reshape(3, 3 * model_width)
    sum_short_bias = wide_small[vocab + 3].reshape(3 * model_width)
    sum_skip = wide_small[vocab + 4 :, 0]
    sum_in_bias = jnp.sum(total_ids, axis=0)
    own_row = (dp_index * seq_parts + seq_index) * up_rows
    own_normed = lax.dynamic_slice_in_dim(normed, own_row, up_rows, 1).astype(jnp.float32)
    sum_in = rows_inner(own_normed, total_ids, highest)
    grad_normed = against_rows(total_ids, in_full.astype(jnp.float32), highest)
    sum_gain_one = jnp.sum(grad_normed * unit_one, axis=0)
    sum_bias_one = jnp.sum(grad_normed, axis=0)
    sum_embed = embed_sum + norm_back(grad_normed * gain_one, unit_one, inverse_one)
    return (
        block_out[None],
        sum_embed,
        sum_gain_one,
        sum_bias_one,
        sum_in,
        sum_in_bias,
        sum_taps,
        sum_short_bias,
        sum_freq_weight,
        sum_freq_bias,
        sum_inner_weight,
        sum_inner_bias,
        sum_filter,
        sum_skip,
        sum_out,
        sum_out_bias,
        sum_gain_two,
        sum_bias_two,
        sum_up,
        sum_up_bias,
        sum_down,
        sum_down_bias,
    )


F32, BF16 = jnp.float32, jnp.bfloat16
ROWS, PARTS, LOCAL, WIDTH, HIDDEN, SPLIT, IDS = 128, 16, 48, 768, 3072, 768, 16
GROUPS, LANE_CH = 3, 16
BINS = PARTS + 1
SPEC = BINS * LANE_CH
LENGTH = ROWS * PARTS


def tables_of(feature_count):
    b = np.arange(ROWS)
    grid = 2 * np.pi * ((b[:, None] * b[None, :]) % ROWS) / ROWS
    cos, sin = np.cos(grid), np.sin(grid)
    forth = np.block([[cos, -sin], [sin, cos]])
    high = forth.astype(ml_dtypes.bfloat16)
    low = (forth - high.astype(np.float64)).astype(ml_dtypes.bfloat16)
    mats = np.stack([high, low, high.T, low.T])
    k = np.arange(BINS)
    turn = 2 * np.pi * k[:, None] * b[None, :] / (2 * LENGTH)
    scale = np.where((k == 0) | (k == PARTS), 1.0, 2.0)[:, None] / (2 * LENGTH)
    twist = np.zeros((72, ROWS))
    twist[0:17], twist[17:34] = np.cos(turn), np.sin(turn)
    twist[34:51], twist[51:68] = np.cos(turn) * scale, np.sin(turn) * scale
    count = (feature_count - 1) // 2
    phase = np.arange(LENGTH, dtype=np.float32) / np.float32(LENGTH)
    levels = np.float32(0.0001) + np.arange(count, dtype=np.float32) * np.float32(
        (count - 1 - 0.0001) / (count - 1)
    )
    angle = np.float32(2.0 * math.pi) * phase[None, :] * levels[:, None]
    feats = np.zeros((40, LENGTH), np.float32)
    feats[0] = phase
    feats[1 : 1 + count] = np.cos(angle.astype(np.float64))
    feats[1 + count : 1 + 2 * count] = -np.sin(angle.astype(np.float64))
    feats[1 + 2 * count] = 1.0
    return mats, twist.astype(np.float32), feats


def times_turn(value, quarter_count, k, m):
    re, im = value
    c, s = math.cos(math.pi * k / m), math.sin(math.pi * k / m)
    if im is None:
        return (re * c, re * (-s))
    return (re * c + im * s, im * c - re * s)


def real_spectrum(xs):
    m = len(xs)
    if m == 1:
        return [(xs[0], None), (xs[0], None)]
    even, odd = real_spectrum(xs[0::2]), real_spectrum(xs[1::2])
    bins = [None] * (m + 1)
    bins[0] = (even[0][0] + odd[0][0], None)
    bins[m] = (even[0][0] - odd[0][0], None)
    half = m // 2
    bins[half] = (even[half][0], -odd[half][0])
    for k in range(1, half):
        er, ei = even[k]
        tr, ti = times_turn(odd[k], None, k, m)
        bins[k] = (er + tr, ei + ti)
        bins[m - k] = (er - tr, ti - ei)
    return bins


def real_signal(bins):
    m = len(bins) - 1
    if m == 1:
        return [bins[0][0] + bins[1][0]]
    half = m // 2
    even, odd = [None] * (half + 1), [None] * (half + 1)
    even[0] = (bins[0][0] + bins[m][0], None)
    odd[0] = (bins[0][0] - bins[m][0], None)
    even[half] = (bins[half][0], None)
    odd[half] = (-bins[half][1], None)
    for k in range(1, half):
        (ar, ai), (br, bi) = bins[k], bins[m - k]
        even[k] = (ar + br, ai - bi)
        dr, di = ar - br, ai + bi
        c, s = math.cos(math.pi * k / m), math.sin(math.pi * k / m)
        odd[k] = (dr * c - di * s, di * c + dr * s)
    first, second = real_signal(even), real_signal(odd)
    out = [None] * m
    out[0::2], out[1::2] = first, second
    return out


def sin_cos(x):
    n = jnp.floor(x * (1.0 / math.pi) + 0.5)
    r = x - n * 3.140625
    r = r - n * 9.67025756835937500000e-4
    r = r - n * 6.2771141529083251953e-7
    r = r - n * 1.2154201256553420762e-10
    flip = 1.0 - 2.0 * (n - 2.0 * jnp.floor(n * 0.5))
    q = r * r
    s = -2.50507477628578072866e-8
    s = s * q + 2.75573136213857245213e-6
    s = s * q - 1.98412698295895385996e-4
    s = s * q + 8.33333333332211858878e-3
    s = s * q - 1.66666666666666307295e-1
    s = (s * q) * r + r
    c = 2.08757008419747316778e-9
    c = c * q - 2.75573141792967388112e-7
    c = c * q + 2.48015872888517045348e-5
    c = c * q - 1.38888888888730564116e-3
    c = c * q + 4.16666666666665929218e-2
    c = c * q - 0.5
    c = c * q + 1.0
    return s * flip, c * flip


def dot32(a, b, ca, cb, precision=lax.Precision.HIGH):
    return lax.dot_general(
        a, b, (((ca,), (cb,)), ((), ())), precision=precision, preferred_element_type=F32
    )


def dot16(a, b, ca, cb):
    return lax.dot_general(a, b, (((ca,), (cb,)), ((), ())), preferred_element_type=F32)


def start_push(src, dst, send, recv, dp, seq):
    pltpu.make_async_remote_copy(
        src_ref=src,
        dst_ref=dst,
        send_sem=send,
        recv_sem=recv,
        device_id=(dp, seq),
        device_id_type=pl.DeviceIdType.MESH,
    ).start()


def wait_for(ref, sem):
    pltpu.make_async_copy(ref, ref, sem).wait()


def step_kernel(*refs):
    it = iter(refs)

    def take(count):
        return [next(it) for _ in range(count)]

    sources = take(len(INPUTS))
    sinks = take(len(OUTPUTS))
    v = SimpleNamespace(**dict(zip(SCRATCH, take(len(SCRATCH)))))
    sem_s, sem_r, sem_l, sem_o = take(4)
    src = SimpleNamespace(**dict(zip(INPUTS, sources)))
    out = SimpleNamespace(**dict(zip(OUTPUTS, sinks)))
    tok_v, emb_v, par_v, inw_v, mlp_v, filt_v = v.tok, v.emb, v.par, v.inw, v.mlp, v.filt
    outw_v, upw_v, downw_v, mats_v, twist_v, feats_v = v.outw, v.upw, v.downw, v.mats, v.twist, v.feats
    dp, seq = lax.axis_index("dp"), lax.axis_index("seq")
    me = dp * PARTS + seq
    z, yc = lax.div(seq, 4), lax.rem(seq, 4)
    y, core = lax.div(yc, 2), lax.rem(yc, 2)
    chip = dp * 2 + y
    twin = seq + 1 - 2 * core
    other_core = 1 - core
    other_dp = 1 - dp

    def tile(index, size):
        return pl.ds(pl.multiple_of(index * size, size), size)

    def everyone(k):
        d = lax.rem(me + k, 2 * PARTS)
        return d, lax.div(d, PARTS), lax.rem(d, PARTS)

    def of_seq(k):
        return lax.rem(seq + k, PARTS)

    def of_plane(k):
        xx, yy = lax.rem(dp + lax.div(k, 2), 2), lax.rem(y + lax.rem(k, 2), 2)
        return xx * 2 + yy, xx, z * 4 + yy * 2 + core

    def of_line(k):
        zz = lax.rem(z + k, 4)
        return zz, zz * 4 + yc

    def of_eight(k):
        j = lax.rem(dp * 4 + yc + k, 8)
        return j, lax.div(j, 4), z * 4 + lax.rem(j, 4)

    def loop(low, high, body):
        def step(k, carry):
            body(k)
            return carry

        lax.fori_loop(low, high, step, 0)

    firsts = np.cumsum([0] + list(FAMILIES.values())).tolist()
    fam = SimpleNamespace(**dict(zip(FAMILIES, firsts)))

    def s_of(first, index):
        return sem_s.at[first + index]

    def r_of(first, index):
        return sem_r.at[first + index]

    barrier = pltpu.get_barrier_semaphore()

    def greet(k):
        _, d, s = everyone(k)
        pl.semaphore_signal(barrier, inc=1, device_id=(d, s), device_id_type=pl.DeviceIdType.MESH)

    loop(1, 2 * PARTS, greet)
    loads = []

    def load(source, target):
        copy = pltpu.make_async_copy(source, target, sem_l.at[len(loads)])
        copy.start()
        loads.append(copy)

    def wait_load(*which):
        for i in which:
            loads[i].wait()

    load(src.embed_table, emb_v)
    load(src.gain_one, par_v.at[0])
    load(src.bias_one, par_v.at[1])
    load(src.in_weight, inw_v)
    load(src.token_ids, tok_v)
    load(src.filter_weight, filt_v)
    LOAD_WEIGHTS = len(loads)
    load(src.up_weight, upw_v)
    load(src.out_weight, outw_v)
    load(src.cotangent, v.seed_all.at[chip])
    LOAD_NET = len(loads)
    load(src.freq_weight, mlp_v.at[0:33, :])
    load(src.freq_bias, mlp_v.at[33])
    load(src.inner_weight, mlp_v.at[40:104, :])
    load(src.inner_bias, mlp_v.at[104])
    load(src.feats, feats_v)
    LOAD_TAIL = len(loads)
    load(src.mats, mats_v)
    load(src.twist, twist_v)
    for p in range(3):
        at = pl.ds(p * WIDTH, WIDTH)
        load(src.in_bias.at[at], par_v.at[2 + p])
        load(src.short_bias.at[at], par_v.at[14 + p])
        for t in range(3):
            load(src.short_taps.at[t : t + 1, at], par_v.at[5 + 3 * t + p : 6 + 3 * t + p, :])
    load(src.skip_scale, par_v.at[17:19, :])
    load(src.out_bias, par_v.at[19])
    load(src.gain_two, par_v.at[20])
    load(src.bias_two, par_v.at[21])
    load(src.down_bias, par_v.at[22])
    for r in range(4):
        load(src.up_bias.at[pl.ds(r * WIDTH, WIDTH)], par_v.at[23 + r])
    load(src.down_weight, downw_v)
    LOAD_END = len(loads)

    wait_load(*range(LOAD_WEIGHTS))
    lanes16 = lax.broadcasted_iota(jnp.int32, (IDS, WIDTH), 0)
    embed = jnp.concatenate([emb_v[...], jnp.zeros((4, WIDTH), F32)], axis=0)
    center = embed - jnp.mean(embed, axis=-1, keepdims=True)
    inverse_one = lax.rsqrt(jnp.mean(center * center, axis=-1, keepdims=True) + epsilon)
    unit_one = center * inverse_one
    normed = (unit_one * par_v[0:1, :] + par_v[1:2, :]).astype(BF16).astype(F32)
    normed = jnp.where(lanes16 < 12, normed, 0.0)
    normed_t = v.normed_t
    normed_t[...] = normed.T
    in_low = inw_v[...].astype(BF16).astype(F32)
    partial = dot32(normed_t[tile(me, 24), :], in_low, 0, 0, None)
    p_send, p_recv = v.p_send, v.p_recv
    for i in range(PARTS):
        block = [partial[:, p * WIDTH + i * LOCAL : p * WIDTH + (i + 1) * LOCAL] for p in range(3)]
        p_send[i] = jnp.concatenate(block, axis=1).astype(BF16)
    filt_all, tok_all = v.filt_all, v.tok_all
    filt_all[dp] = filt_v[...].astype(BF16)
    tok_all[seq] = tok_v[...]
    p_recv[seq] = p_send[seq]
    mlp_v[34:40, :] = jnp.zeros((6, 64), F32)
    mlp_v[105:112, :] = jnp.zeros((7, 64), F32)

    pl.semaphore_wait(barrier, 2 * PARTS - 1)

    def push_p(k):
        s = of_seq(k)
        start_push(p_send.at[s], p_recv.at[seq], s_of(fam.p, k), r_of(fam.p, seq), dp, s)
        start_push(tok_v, tok_all.at[seq], s_of(fam.tok, k), r_of(fam.tok, seq), dp, s)

    loop(1, PARTS, push_p)
    start_push(filt_all.at[dp], filt_all.at[dp], s_of(fam.filt, 0), r_of(fam.filt, 0), other_dp, seq)

    wait_load(*range(LOAD_WEIGHTS, LOAD_NET))
    up_send, up_all, out_all, seed_all = v.up_send, v.up_all, v.out_all, v.seed_all
    out_all[core, chip, z] = outw_v[...].astype(BF16)

    def push_out(k):
        zz, s = of_line(k)
        mine = out_all.at[core, chip, z]
        start_push(mine, mine, s_of(fam.outz, k), r_of(fam.outz, z), dp, s)

    loop(1, 4, push_out)

    def shard_of(q, c, zz):
        return (q // 2) * PARTS + zz * 4 + (q % 2) * 2 + c

    for q in range(4):
        cut = [
            upw_v[:, 96 * shard_of(q, c, zz) : 96 * (shard_of(q, c, zz) + 1)]
            for c in range(2)
            for zz in range(4)
        ]
        up_send[q] = jnp.concatenate(cut, axis=1).astype(BF16)
    up_all[core, z, chip] = up_send[chip]

    def push_up(k):
        q, d, s = of_plane(k)
        start_push(
            up_send.at[q], up_all.at[core, z, chip], s_of(fam.up, k), r_of(fam.up, chip), d, s
        )

    loop(1, 4, push_up)

    def push_seed(k):
        q, d, s = of_plane(k)
        mine = seed_all.at[chip]
        start_push(mine, mine, s_of(fam.seed, k), r_of(fam.seed, chip), d, s)

    loop(1, 4, push_seed)

    act1, cos1, act2, cos2 = v.act1, v.cos1, v.act2, v.cos2
    wait_load(*range(LOAD_NET, LOAD_TAIL))
    mlp = mlp_v[...]
    freq_t = mlp[0:40].T
    inner_bias = mlp[104:112].T[:, 0:1]
    inner = mlp[40:104]

    def network(i):
        at = tile(i, 256)
        s1, c1 = sin_cos(dot32(freq_t, feats_v[:, at], 1, 0, lax.Precision.HIGHEST))
        act1[0:64, at] = s1
        cos1[:, at] = c1
        act1[64:72, at] = jnp.where(
            lax.broadcasted_iota(jnp.int32, (8, 256), 0) == 0, 1.0, 0.0
        ).astype(F32)
        s2, c2 = sin_cos(dot32(inner, s1, 0, 0, lax.Precision.HIGHEST) + inner_bias)
        act2[:, at] = s2
        cos2[:, at] = c2

    loop(0, LENGTH // 256, network)
    def wait_up(k):
        q, _, _ = of_plane(k)
        wait_for(up_all.at[0, 0, 0], r_of(fam.up, q))

    loop(1, 4, wait_up)

    def push_up_line(k):
        zz, s = of_line(k)
        mine = up_all.at[core, z]
        start_push(mine, mine, s_of(fam.upz, k), r_of(fam.upz, z), dp, s)

    loop(1, 4, push_up_line)

    def twin_push(name, index, ref, target=None):
        start_push(ref, ref if target is None else target, s_of(name, index), r_of(name, index), dp, twin)

    twin_push(fam.upt, z, up_all.at[core, z])

    def wait_line(k):
        zz, _ = of_line(k)
        wait_for(out_all.at[0, 0, 0], r_of(fam.outz, zz))

    loop(1, 4, wait_line)

    def push_out_plane(k):
        q, d, s = of_plane(k)
        mine = out_all.at[core, chip]
        start_push(mine, mine, s_of(fam.outp, k), r_of(fam.outp, chip), d, s)

    loop(1, 4, push_out_plane)
    twin_push(fam.outt, chip, out_all.at[core, chip])

    wait_load(*range(LOAD_TAIL, LOAD_END))
    par_t = v.par_t
    for i in range(WIDTH // 128):
        par_t[128 * i : 128 * (i + 1), :] = par_v[:, 128 * i : 128 * (i + 1)].T
    own_par = par_t[tile(seq, LOCAL), :]

    def wait_p(k):
        s = of_seq(k)
        wait_for(p_recv.at[s], r_of(fam.p, s))

    loop(1, PARTS, wait_p)
    table = p_recv[0].astype(F32)
    for s in range(1, PARTS):
        table = table + p_recv[s].astype(F32)
    px_send, px_recv = v.px_send, v.px_recv
    px_send[...] = jnp.concatenate([table, jnp.zeros((IDS, 256 - 3 * LOCAL), F32)], axis=1)
    start_push(px_send, px_recv, s_of(fam.px, 0), r_of(fam.px, 0), other_dp, seq)

    kern, hi_ref, lo_ref = v.kern, v.hi, v.lo
    spec_k1, spec_k2, spec_v, spec_g = v.spec_k1, v.spec_k2, v.spec_v, v.spec_g
    wait_for(filt_all.at[0], r_of(fam.filt, 0))
    filt = jnp.concatenate([filt_all[0], filt_all[1]], axis=0).astype(F32)
    for i in range(LENGTH // 256):
        both = dot32(filt, act2[:, 256 * i : 256 * (i + 1)], 1, 0)
        for h in range(2):
            for f in range(2):
                kern[f, 2 * i + h] = both[f * LOCAL : (f + 1) * LOCAL, 128 * h : 128 * (h + 1)]
    lane = lax.broadcasted_iota(jnp.int32, (LANE_CH, ROWS), 1).astype(F32)

    def decay_of(g):
        row = lax.broadcasted_iota(jnp.int32, (LANE_CH, ROWS), 0) + (seq * LOCAL + g * LANE_CH)
        rate = slow_rate + (fast_rate - slow_rate) * (row.astype(F32) * (1.0 / (WIDTH - 1)))
        return lambda a: jnp.exp((lane + float(a * ROWS)) * (rate * (-1.0 / LENGTH))) + decay_shift

    def put(row0, k, re, im):
        rows = pl.ds(row0 + k * LANE_CH, LANE_CH)
        for part, value in ((0, re), (1, im)):
            at = pl.ds(part * ROWS, ROWS)
            high = value.astype(BF16)
            hi_ref[rows, at] = high
            lo_ref[rows, at] = (value - high.astype(F32)).astype(BF16)

    def forth(row0, values):
        for k, (re, im) in enumerate(real_spectrum(values)):
            c, s = twist_v[k : k + 1, :], twist_v[17 + k : 18 + k, :]
            if im is None:
                put(row0, k, re * c, re * (-s))
            else:
                put(row0, k, re * c + im * s, im * c - re * s)

    def dft(rows, which):
        high, low = hi_ref[0:rows, :], lo_ref[0:rows, :]
        m_high, m_low = mats_v[which], mats_v[which + 1]
        return dot16(high, m_high, 1, 0) + dot16(low, m_high, 1, 0) + dot16(high, m_low, 1, 0)

    def put_product(row0, spec, other, conj):
        a_re, a_im = spec[:, 0:ROWS], spec[:, ROWS:]
        b_re, b_im = other[:, 0:ROWS], other[:, ROWS:]
        if conj:
            re, im = a_re * b_re + a_im * b_im, a_im * b_re - a_re * b_im
        else:
            re, im = a_re * b_re - a_im * b_im, a_re * b_im + a_im * b_re
        rows = pl.ds(row0, SPEC)
        for part, value in ((0, re), (1, im)):
            at = pl.ds(part * ROWS, ROWS)
            high = value.astype(BF16)
            hi_ref[rows, at] = high
            lo_ref[rows, at] = (value - high.astype(F32)).astype(BF16)

    def back(turned, row0):
        bins = []
        for k in range(BINS):
            part = turned[row0 + k * LANE_CH : row0 + (k + 1) * LANE_CH]
            re, im = part[:, 0:ROWS], part[:, ROWS:]
            c, s = twist_v[34 + k : 35 + k, :], twist_v[51 + k : 52 + k, :]
            if k in (0, PARTS):
                bins.append((re * c - im * s, None))
            else:
                bins.append((re * c - im * s, im * c + re * s))
        return real_signal(bins)

    def kernel_spectra(g):
        at = tile(g, LANE_CH)
        decay = decay_of(g)
        damp = [decay(a) for a in range(PARTS)]
        forth(0, [kern[0, a, at, :] * damp[a] for a in range(PARTS)])
        forth(SPEC, [kern[1, a, at, :] * damp[a] for a in range(PARTS)])
        spec = dft(2 * SPEC, 0)
        spec_k1[g] = spec[0:SPEC]
        spec_k2[g] = spec[SPEC:]

    loop(0, GROUPS, kernel_spectra)

    table_t, onehot, mix = v.table_t, v.onehot, v.mix
    wait_for(px_recv, r_of(fam.px, 0))
    wide_t = (px_send[...] + px_recv[...]).T
    table_t[...] = jnp.concatenate(
        [wide_t[p * LOCAL : (p + 1) * LOCAL] + own_par[:, 2 + p : 3 + p] for p in range(3)], axis=0
    )

    def wait_tok(k):
        s = of_seq(k)
        wait_for(tok_v, r_of(fam.tok, s))

    loop(1, PARTS, wait_tok)
    id_rows = lax.broadcasted_iota(jnp.int32, (IDS, ROWS), 0)
    for a in range(PARTS):
        now = tok_all[a]
        if a == 0:
            long = jnp.concatenate([jnp.full((1, ROWS), -1, jnp.int32), now], axis=1)
        else:
            long = jnp.concatenate([tok_all[a - 1], now], axis=1)
        for t in range(3):
            moved = long[:, ROWS - 2 + t : 2 * ROWS - 2 + t]
            onehot[t * IDS : (t + 1) * IDS, a * ROWS : (a + 1) * ROWS] = (
                id_rows == moved
            ).astype(F32)

    def taps_of(t):
        return jnp.concatenate(
            [own_par[:, 5 + 3 * t + p : 6 + 3 * t + p] for p in range(3)], axis=0
        )

    short = jnp.concatenate([taps_of(t) * table_t[...] for t in range(3)], axis=1)
    short_bias = jnp.concatenate([own_par[:, 14 + p : 15 + p] for p in range(3)], axis=0)
    for i in range(LENGTH // 256):
        both = dot32(short, onehot[:, 256 * i : 256 * (i + 1)], 1, 0) + short_bias
        for h in range(2):
            for p in range(3):
                mix[p, 2 * i + h] = both[p * LOCAL : (p + 1) * LOCAL, 128 * h : 128 * (h + 1)]

    first_s, gated_s, second_s = v.first, v.gated, v.second
    mix_send, mix_recv = v.mix_send, v.mix_recv
    gm_send, gm_recv = v.gm_send, v.gm_recv

    def exchange(name, send, recv, g):
        at = tile(g, LANE_CH)

        def push(k):
            s = of_seq(k)
            start_push(
                send.at[s, at, :],
                recv.at[seq, at, :],
                s_of(name, g * PARTS + k),
                r_of(name, g * PARTS + seq),
                dp,
                s,
            )

        loop(1, PARTS, push)

    def exchanged(name, recv, g):
        def wait(k):
            s = of_seq(k)
            wait_for(recv.at[0, 0:LANE_CH, :], r_of(name, g * PARTS + s))

        loop(1, PARTS, wait)

    def operator(g):
        at = tile(g, LANE_CH)
        skips = par_t[pl.ds(pl.multiple_of(seq * LOCAL + g * LANE_CH, LANE_CH), LANE_CH), :]
        skip0, skip1 = skips[:, 17:18], skips[:, 18:19]
        forth(0, [mix[2, a, at, :] for a in range(PARTS)])
        spec = dft(SPEC, 0)
        spec_v[g] = spec
        put_product(0, spec, spec_k1[g], False)
        signal = back(dft(SPEC, 2), 0)
        gated = []
        for a in range(PARTS):
            conv = signal[a] + skip0 * mix[2, a, at, :]
            first_s[a, at, :] = conv
            gate = mix[1, a, at, :] * conv
            gated_s[a, at, :] = gate
            gated.append(gate)
        forth(0, gated)
        spec = dft(SPEC, 0)
        spec_g[g] = spec
        put_product(0, spec, spec_k2[g], False)
        signal = back(dft(SPEC, 2), 0)
        for a in range(PARTS):
            conv = signal[a] + skip1 * gated_s[a, at, :]
            second_s[a, at, :] = conv
            mix_send[a, at, :] = (mix[0, a, at, :] * conv).astype(BF16)

        exchange(fam.mix, mix_send, mix_recv, g)

    loop(0, GROUPS, operator)
    mix_recv[seq] = mix_send[seq]

    down_all = v.down_all
    down_all[core, z] = downw_v[...].astype(BF16)

    def forward_up(k):
        zz, _ = of_line(k)
        wait_for(up_all.at[0, 0], r_of(fam.upz, zz))
        twin_push(fam.upt, zz, up_all.at[core, zz])

    loop(1, 4, forward_up)

    def forward_out(k):
        q, _, _ = of_plane(k)
        wait_for(out_all.at[0, 0], r_of(fam.outp, q))
        twin_push(fam.outt, q, out_all.at[core, q])

    loop(1, 4, forward_out)
    w_up, w_out = v.w_up, v.w_out
    loop(0, 4, lambda k: wait_for(out_all.at[0, 0], r_of(fam.outt, k)))

    def place_out(i):
        q, zz = lax.div(i, 8) * 2 + lax.rem(i, 2), lax.rem(lax.div(i, 2), 4)
        both = jnp.concatenate(
            [out_all[0, q, zz].astype(F32), out_all[1, q, zz].astype(F32)], axis=0
        )
        w_out[tile(i, 48), :] = both.astype(BF16)

    loop(0, 16, place_out)
    for g in range(GROUPS):
        exchanged(fam.mix, mix_recv, g)

    def push_down(k):
        zz, s = of_line(k)
        mine = down_all.at[core, z]
        start_push(mine, mine, s_of(fam.down, k), r_of(fam.down, z), dp, s)

    loop(1, 4, push_down)
    twin_push(fam.downt, z, down_all.at[core, z])

    own_onehot = (id_rows == tok_v[...]).astype(F32)
    resid, unit2, inv2, n2_all = v.resid, v.unit2, v.inv2, v.n2_all
    mixer_t = mix_recv[...].reshape(WIDTH, ROWS)
    residual = dot32(own_onehot, embed, 0, 0) + dot16(mixer_t, w_out[...], 0, 0) + par_v[19:20, :]
    resid[...] = residual
    center = residual - jnp.mean(residual, axis=-1, keepdims=True)
    inv = lax.rsqrt(jnp.mean(center * center, axis=-1, keepdims=True) + epsilon)
    inv2[...] = inv
    unit = center * inv
    unit2[...] = unit
    n2_all[chip] = (unit * par_v[20:21, :] + par_v[21:22, :]).astype(BF16)

    def push_n2(k):
        q, d, s = of_plane(k)
        mine = n2_all.at[chip]
        start_push(mine, mine, s_of(fam.n2, k), r_of(fam.n2, chip), d, s)

    loop(1, 4, push_n2)

    loop(0, 4, lambda k: wait_for(up_all.at[0, 0], r_of(fam.upt, k)))

    def place_up(i):
        q, zz = lax.div(i, 8) * 2 + lax.rem(i, 2), lax.rem(lax.div(i, 2), 4)
        both = jnp.concatenate(
            [up_all[0, zz, q].astype(F32), up_all[1, zz, q].astype(F32)], axis=0
        )
        w_up[tile(i, 48), :] = both.astype(BF16)

    loop(0, 16, place_up)

    def wait_seed(k):
        q, _, _ = of_plane(k)
        wait_for(seed_all.at[0], r_of(fam.seed, q))

    loop(1, 4, wait_seed)

    def forward_down(k):
        zz, _ = of_line(k)
        wait_for(down_all.at[0, 0], r_of(fam.down, zz))
        twin_push(fam.downt, zz, down_all.at[core, zz])

    loop(1, 4, forward_down)
    loop(0, 4, lambda k: wait_for(down_all.at[0, 0], r_of(fam.downt, k)))

    up_bias = jnp.zeros((1, SPLIT), F32)
    for q in range(4):
        cut = []
        for c in range(2):
            for zz in range(4):
                first = 96 * shard_of(q, c, zz)
                row, lane0 = first // WIDTH, first % WIDTH
                cut.append(par_v[23 + row : 24 + row, lane0 : lane0 + 96])
        up_bias = jnp.where(chip == q, jnp.concatenate(cut, axis=1), up_bias)
    act_all, gl_all, po_all, gn_all = v.act_all, v.gl_all, v.po_all, v.gn_all
    gn_recv, po_recv = v.gn_recv, v.po_recv

    def feed(k, bias_sum):
        q, d, s = of_plane(k)

        @pl.when(k != 0)
        def _():
            wait_for(n2_all.at[0], r_of(fam.n2, q))

        down_w = down_all[...].reshape(SPLIT, WIDTH)
        lifted = dot16(n2_all[q], w_up[...], 1, 0) + up_bias
        cdf = 0.5 * (1.0 + lax.erf(lifted * (1.0 / math.sqrt(2.0))))
        pdf = jnp.exp(-0.5 * lifted * lifted) * (1.0 / math.sqrt(2.0 * math.pi))
        grad_act = dot16(seed_all[q], down_w, 1, 1)
        grad_lifted = grad_act * (cdf + lifted * pdf)
        act_all[q] = (lifted * cdf).astype(BF16)
        gl_all[q] = grad_lifted.astype(BF16)
        gn_all[q] = dot16(gl_all[q], w_up[...], 1, 1).astype(BF16)

        @pl.when(k != 0)
        def _():
            start_push(gn_all.at[q], gn_recv.at[chip], s_of(fam.gn, k), r_of(fam.gn, chip), d, s)

        po_all[q] = dot16(act_all[q], down_w, 1, 0).astype(BF16)
        return bias_sum + jnp.sum(grad_lifted, axis=0, keepdims=True)

    grad_up_bias = lax.fori_loop(0, 4, feed, jnp.zeros((1, SPLIT), F32))
    gn_recv[chip] = gn_all[chip]
    po_recv[chip] = po_all[chip]

    sd_x, sd_y, sd_t, sd_z = v.sd_x, v.sd_y, v.sd_t, v.sd_z
    su_x, su_y, su_t, su_z, su_p, su_r = (v.su_x, v.su_y, v.su_t, v.su_z, v.su_p, v.su_r)
    so_x, so_y, so_t, so_p, so_u, so_z = (v.so_x, v.so_y, v.so_t, v.so_p, v.so_u, v.so_z)
    acts = act_all[...].reshape(4 * ROWS, SPLIT)
    seeds = seed_all[...].reshape(4 * ROWS, WIDTH)
    for c in range(2):
        half = acts[:, c * 384 : (c + 1) * 384]
        sd_x[c] = dot16(half, seeds, 0, 0).astype(BF16).reshape(4, 96, WIDTH)
    twin_push(fam.sdt, 0, sd_x.at[other_core], sd_y)
    units = n2_all[...].reshape(4 * ROWS, WIDTH)
    lows = gl_all[...].reshape(4 * ROWS, SPLIT)
    for x in range(2):
        part = dot16(units[:, x * 384 : (x + 1) * 384], lows, 0, 0)
        for i in range(16):
            su_x[i % 2, i // 4, x * 2 + (i // 2) % 2] = part[24 * i : 24 * (i + 1)].astype(BF16)
    twin_push(fam.sut, 0, su_x.at[other_core], su_y)
    wait_for(sd_y, r_of(fam.sdt, 0))

    def add_sd(i):
        sd_t[i] = (sd_x[core, i].astype(F32) + sd_y[i].astype(F32)).astype(BF16)

    loop(0, 4, add_sd)
    sd_z[z] = sd_t[z]

    def push_sd(k):
        zz, s = of_line(k)
        start_push(sd_t.at[zz], sd_z.at[z], s_of(fam.sd, k), r_of(fam.sd, z), dp, s)

    loop(1, 4, push_sd)
    wait_for(su_y, r_of(fam.sut, 0))

    def add_su(i):
        for q in range(4):
            su_t[i, q] = (su_x[core, i, q].astype(F32) + su_y[i, q].astype(F32)).astype(BF16)

    loop(0, 4, add_su)
    su_z[z] = su_t[z]

    def wait_gn(k):
        q, _, _ = of_plane(k)
        wait_for(gn_recv.at[0], r_of(fam.gn, q))

    loop(1, 4, wait_gn)
    grad_n2 = gn_recv[0].astype(F32)
    for q in range(1, 4):
        grad_n2 = grad_n2 + gn_recv[q].astype(F32)
    unit, inv = unit2[...], inv2[...]
    seed = seed_all[chip].astype(F32)
    scaled = grad_n2 * par_v[20:21, :]
    grad_res = seed + inv * (
        scaled
        - jnp.mean(scaled, axis=-1, keepdims=True)
        - unit * jnp.mean(scaled * unit, axis=-1, keepdims=True)
    )
    gres = v.gres
    gres[...] = grad_res.astype(BF16)
    gm_send[...] = dot16(w_out[...], gres[...], 1, 1).astype(BF16).reshape(PARTS, LOCAL, ROWS)
    loop(0, GROUPS, lambda g: exchange(fam.gm, gm_send, gm_recv, g))
    gm_recv[seq] = gm_send[seq]

    b_x, b_y, b_p, b_t, b_z, b_f = (v.b_x, v.b_y, v.b_p, v.b_t, v.b_z, v.b_f)
    b_x[0:12, :] = dot32(own_onehot, grad_res, 1, 0)[0:12]
    b_x[12:13, :] = jnp.sum(grad_res, axis=0, keepdims=True)
    b_x[13:14, :] = jnp.sum(grad_n2 * unit, axis=0, keepdims=True)
    b_x[14:15, :] = jnp.sum(grad_n2, axis=0, keepdims=True)
    b_x[15:16, :] = jnp.sum(seed, axis=0, keepdims=True)
    for q in range(4):
        b_x[16 + q : 17 + q, :] = jnp.where(chip == q, grad_up_bias, 0.0)
    b_x[20:24, :] = jnp.zeros((4, WIDTH), F32)
    twin_push(fam.bt, 0, b_x, b_y)

    def push_po(k):
        q, d, s = of_plane(k)
        start_push(po_all.at[q], po_recv.at[chip], s_of(fam.po, k), r_of(fam.po, chip), d, s)

    loop(1, 4, push_po)
    for x in range(2):
        part = dot16(mixer_t[x * 384 : (x + 1) * 384], gres[...], 1, 0)
        for i in range(16):
            so_x[i % 2, x * 2 + (i // 2) % 2, i // 4] = part[24 * i : 24 * (i + 1)].astype(BF16)
    twin_push(fam.sot, 0, so_x.at[other_core], so_y)

    wait_for(b_y, r_of(fam.bt, 0))
    for c in range(2):

        @pl.when(core == c)
        def _():
            at = slice(c * 384, (c + 1) * 384)
            b_p[chip] = b_x[:, at] + b_y[:, at]

    def push_b(k):
        q, d, s = of_plane(k)
        mine = b_p.at[chip]
        start_push(mine, mine, s_of(fam.b, k), r_of(fam.b, chip), d, s)

    loop(1, 4, push_b)

    wait_for(so_y, r_of(fam.sot, 0))

    def add_so(i):
        for q in range(4):
            so_t[q, i] = (so_x[core, q, i].astype(F32) + so_y[q, i].astype(F32)).astype(BF16)

    loop(0, 4, add_so)
    so_p[chip] = so_t[chip]

    def push_so(k):
        q, d, s = of_plane(k)
        start_push(so_t.at[q], so_p.at[chip], s_of(fam.so, k), r_of(fam.so, chip), d, s)

    loop(1, 4, push_so)

    grad_mix, raw, q_s = v.grad_mix, v.raw, v.q_s

    def operator_back(g):
        at = tile(g, LANE_CH)
        skips = par_t[pl.ds(pl.multiple_of(seq * LOCAL + g * LANE_CH, LANE_CH), LANE_CH), :]
        skip0, skip1 = skips[:, 17:18], skips[:, 18:19]
        decay = decay_of(g)

        def rows_at(first, count=LANE_CH):
            return pl.ds(pl.multiple_of(first + g * LANE_CH, LANE_CH), count)

        seconds, total = [], jnp.zeros((LANE_CH, ROWS), F32)
        for a in range(PARTS):
            upstream = gm_recv[a, at, :].astype(F32)
            lanes = slice(a * ROWS, (a + 1) * ROWS)
            grad_mix[rows_at(0), lanes] = upstream * second_s[a, at, :]
            grad_second = upstream * mix[0, a, at, :]
            total = total + grad_second * gated_s[a, at, :]
            seconds.append(grad_second)
        q_s[rows_at(0), 49:50] = jnp.sum(total, axis=1, keepdims=True)
        forth(0, seconds)
        spec = dft(SPEC, 0)
        put_product(0, spec, spec_k2[g], True)
        put_product(SPEC, spec, spec_g[g], True)
        turned = dft(2 * SPEC, 2)
        signal = back(turned, 0)
        cross = back(turned, SPEC)
        firsts, total = [], jnp.zeros((LANE_CH, ROWS), F32)
        for a in range(PARTS):
            lanes = slice(a * ROWS, (a + 1) * ROWS)
            raw[rows_at(LOCAL), lanes] = cross[a] * decay(a)
            grad_second = gm_recv[a, at, :].astype(F32) * mix[0, a, at, :]
            grad_gated = skip1 * grad_second + signal[a]
            grad_mix[rows_at(LOCAL), lanes] = grad_gated * first_s[a, at, :]
            grad_first = grad_gated * mix[1, a, at, :]
            total = total + grad_first * mix[2, a, at, :]
            grad_mix[rows_at(2 * LOCAL), lanes] = skip0 * grad_first
            firsts.append(grad_first)
        q_s[rows_at(0), 48:49] = jnp.sum(total, axis=1, keepdims=True)
        forth(0, firsts)
        spec = dft(SPEC, 0)
        put_product(0, spec, spec_k1[g], True)
        put_product(SPEC, spec, spec_v[g], True)
        turned = dft(2 * SPEC, 2)
        signal = back(turned, 0)
        cross = back(turned, SPEC)
        for a in range(PARTS):
            lanes = slice(a * ROWS, (a + 1) * ROWS)
            raw[rows_at(0), lanes] = cross[a] * decay(a)
            grad_mix[rows_at(2 * LOCAL), lanes] = grad_mix[rows_at(2 * LOCAL), lanes] + signal[a]

    def push_su(k):
        zz, s = of_line(k)
        start_push(su_t.at[zz], su_z.at[z], s_of(fam.su, k), r_of(fam.su, z), dp, s)

    def group_back(g):
        exchanged(fam.gm, gm_recv, g)

        @pl.when(g == GROUPS - 1)
        def _():
            loop(1, 4, push_su)

        operator_back(g)

    loop(0, GROUPS, group_back)

    zx_send, zx_recv, z_send, z_recv = v.zx_send, v.zx_recv, v.z_send, v.z_recv
    by_id = dot32(grad_mix[...], onehot[...], 1, 1)
    sums = sum(taps_of(t) * by_id[:, t * IDS : (t + 1) * IDS] for t in range(3))
    taps_grad = [
        jnp.sum(table_t[...] * by_id[:, t * IDS : (t + 1) * IDS], axis=1, keepdims=True)
        for t in range(3)
    ]
    bias_grad = jnp.sum(by_id[:, 2 * IDS : 3 * IDS], axis=1, keepdims=True)
    columns = jnp.concatenate([sums[:, 0:12]] + taps_grad + [bias_grad], axis=1)
    skip_cols = jnp.concatenate(
        [q_s[:, 48:50], jnp.zeros((LOCAL, 14), F32)], axis=1
    )
    zx_send[...] = jnp.concatenate(
        [columns, skip_cols, jnp.zeros((64, IDS), F32)], axis=0
    ).T
    start_push(zx_send, zx_recv, s_of(fam.zx, 0), r_of(fam.zx, 0), other_dp, seq)

    f_send, f_recv, m_send, m_recv, m2_send, m2_recv = (v.f_send, v.f_recv, v.m_send, v.m_recv, v.m2_send, v.m2_recv)
    grad_filter = dot32(raw[...], act2[...], 1, 1)
    f_send[...] = grad_filter
    there = f_send.at[tile(other_dp, LOCAL), :]
    start_push(there, f_recv, s_of(fam.f, 0), r_of(fam.f, 0), other_dp, seq)
    grad_second_pre = dot32(filt, raw[...], 0, 0) * cos2[...]
    grad_inner = dot32(act1[...], grad_second_pre, 1, 1)
    grad_first_pre = dot32(inner, grad_second_pre, 1, 0) * cos1[...]
    grad_freq = dot32(feats_v[...], grad_first_pre, 1, 1)
    m_send[...] = jnp.concatenate(
        [
            jnp.concatenate([grad_freq, jnp.zeros((40, 64), F32)], axis=0),
            jnp.concatenate([grad_inner, jnp.zeros((8, 64), F32)], axis=0),
        ],
        axis=1,
    ).astype(BF16)
    j_me = dp * 4 + yc
    m_recv[j_me] = m_send[...]

    def push_m(k):
        j, d, s = of_eight(k)
        start_push(m_send, m_recv.at[j_me], s_of(fam.m, k), r_of(fam.m, j_me), d, s)

    loop(1, 8, push_m)

    wait_for(zx_recv, r_of(fam.zx, 0))
    z_send[...] = (zx_send[...] + zx_recv[...]).astype(BF16)
    z_recv[seq] = z_send[...]

    def push_z(k):
        s = of_seq(k)
        start_push(z_send, z_recv.at[seq], s_of(fam.z, k), r_of(fam.z, seq), dp, s)

    loop(1, PARTS, push_z)

    def wait_b(k):
        q, _, _ = of_plane(k)
        wait_for(b_p.at[0], r_of(fam.b, q))

    loop(1, 4, wait_b)
    b_t[...] = (b_p[0] + b_p[1]) + (b_p[2] + b_p[3])
    b_z[z] = b_t[...]

    def push_b2(k):
        zz, s = of_line(k)
        start_push(b_t, b_z.at[z], s_of(fam.b2, k), r_of(fam.b2, z), dp, s)

    loop(1, 4, push_b2)

    def wait_so(k):
        q, _, _ = of_plane(k)
        wait_for(so_p.at[0], r_of(fam.so, q))

    loop(1, 4, wait_so)
    for zz in range(4):
        part = so_p[0, zz].astype(F32)
        for q in range(1, 4):
            part = part + so_p[q, zz].astype(F32)
        so_u[zz] = part.astype(BF16)
    so_z[z] = so_u[z]

    def push_so2(k):
        zz, s = of_line(k)
        start_push(so_u.at[zz], so_z.at[z], s_of(fam.so2, k), r_of(fam.so2, z), dp, s)

    loop(1, 4, push_so2)

    def wait_m(k):
        j, _, _ = of_eight(k)
        wait_for(m_send, r_of(fam.m, j))

    loop(1, 8, wait_m)
    totals = m_recv[0].astype(F32)
    for j in range(1, 8):
        totals = totals + m_recv[j].astype(F32)
    m2_send[...] = totals.astype(BF16)
    m2_recv[z] = m2_send[...]

    def push_m2(k):
        zz, s = of_line(k)
        start_push(m2_send, m2_recv.at[z], s_of(fam.m2, k), r_of(fam.m2, z), dp, s)

    loop(1, 4, push_m2)

    def wait_su(k):
        zz, _ = of_line(k)
        wait_for(su_z.at[0], r_of(fam.su, zz))

    loop(1, 4, wait_su)
    for q in range(4):
        part = su_z[0, q].astype(F32)
        for zz in range(1, 4):
            part = part + su_z[zz, q].astype(F32)
        su_p[q] = part.astype(BF16)
    su_r[chip] = su_p[chip]

    def push_su2(k):
        q, d, s = of_plane(k)
        start_push(su_p.at[q], su_r.at[chip], s_of(fam.su2, k), r_of(fam.su2, chip), d, s)

    loop(1, 4, push_su2)

    wide, gt_all = v.wide, v.gt_all

    def wait_z(k):
        s = of_seq(k)
        wait_for(z_send, r_of(fam.z, s))

    loop(1, PARTS, wait_z)
    for p in range(4):
        for i in range(PARTS):
            wide[:, p * WIDTH + i * LOCAL : p * WIDTH + (i + 1) * LOCAL] = z_recv[i][
                :, p * LOCAL : (p + 1) * LOCAL
            ].astype(F32)
    by_ids = jnp.where(
        lax.broadcasted_iota(jnp.int32, (IDS, 3 * WIDTH), 0) < 12, wide[:, 0 : 3 * WIDTH], 0.0
    )
    gt_all[me] = dot32(in_low, by_ids, 1, 1)

    def push_gt(k):
        _, d, s = everyone(k)
        mine = gt_all.at[me]
        start_push(mine, mine, s_of(fam.gt, k), r_of(fam.gt, me), d, s)

    loop(1, 2 * PARTS, push_gt)

    stores = []

    def store(source, target):
        copy = pltpu.make_async_copy(source, target, sem_o.at[len(stores)])
        copy.start()
        stores.append(copy)

    o_in, o_wide, o_rows = v.o_in, v.o_wide, v.o_rows
    o_in[...] = dot32(normed_t[tile(me, 24), :], by_ids, 1, 0)
    o_wide[...] = jnp.sum(by_ids, axis=0, keepdims=True)
    o_rows[2:4, :] = wide[0:2, 3 * WIDTH :]
    store(o_in, out.in_weight)
    store(o_wide.at[0], out.in_bias)
    store(wide.at[12:15, 0 : 3 * WIDTH], out.short_taps)
    store(wide.at[15, pl.ds(0, 3 * WIDTH)], out.short_bias)
    store(o_rows.at[2:4, :], out.skip_scale)

    def wait_po(k):
        q, _, _ = of_plane(k)
        wait_for(po_recv.at[0], r_of(fam.po, q))

    loop(1, 4, wait_po)
    block = resid[...] + par_v[22:23, :]
    for q in range(4):
        block = block + po_recv[q].astype(F32)
    resid[...] = block
    store(resid, out.block)

    def wait_sd(k):
        zz, _ = of_line(k)
        wait_for(sd_z.at[0], r_of(fam.sd, zz))

    loop(1, 4, wait_sd)
    part = sd_z[0].astype(F32)
    for zz in range(1, 4):
        part = part + sd_z[zz].astype(F32)
    downw_v[...] = part
    store(downw_v, out.down_weight)
    wait_for(f_recv, r_of(fam.f, 0))
    f_recv[...] = f_send[tile(dp, LOCAL), :] + f_recv[...]
    store(f_recv, out.filter_weight)

    def wait_su2(k):
        q, _, _ = of_plane(k)
        wait_for(su_r.at[0], r_of(fam.su2, q))

    loop(1, 4, wait_su2)
    for q in range(4):
        part = su_r[q].astype(F32)
        for c in range(2):
            for zz in range(4):
                first, place = 96 * shard_of(q, c, zz), 384 * c + 96 * zz
                upw_v[:, first : first + 96] = part[:, place : place + 96]
    store(upw_v, out.up_weight)

    def wait_so2(k):
        zz, _ = of_line(k)
        wait_for(so_z.at[0], r_of(fam.so2, zz))
        wait_for(b_t, r_of(fam.b2, zz))
        wait_for(m2_send, r_of(fam.m2, zz))

    loop(1, 4, wait_so2)
    b_f[core] = (b_z[0] + b_z[1]) + (b_z[2] + b_z[3])
    mine = b_f.at[core]
    start_push(mine, mine, s_of(fam.bf, 0), r_of(fam.bf, 0), dp, twin)
    part = so_z[0].astype(F32)
    for zz in range(1, 4):
        part = part + so_z[zz].astype(F32)
    outw_v[...] = part
    store(outw_v, out.out_weight)
    totals = m2_recv[0].astype(F32)
    for zz in range(1, 4):
        totals = totals + m2_recv[zz].astype(F32)
    mlp_v[0:40, :] = totals[0:40, 0:64]
    mlp_v[40:112, :] = totals[0:72, 64:128]
    store(mlp_v.at[0:33, :], out.freq_weight)
    store(mlp_v.at[33], out.freq_bias)
    store(mlp_v.at[40:104, :], out.inner_weight)
    store(mlp_v.at[104], out.inner_bias)
    wait_for(b_f.at[0], r_of(fam.bf, 0))
    totals = jnp.concatenate([b_f[0], b_f[1]], axis=1)
    o_rows[4:8, :] = totals[12:16]
    o_up = v.o_up
    for q in range(4):
        for c in range(2):
            for zz in range(4):
                first, place = 96 * shard_of(q, c, zz), 384 * c + 96 * zz
                o_up[:, first : first + 96] = totals[16 + q : 17 + q, place : place + 96]
    store(o_rows.at[4], out.out_bias)
    store(o_rows.at[5], out.gain_two)
    store(o_rows.at[6], out.bias_two)
    store(o_rows.at[7], out.down_bias)
    store(o_up.at[0], out.up_bias)

    def wait_gt(k):
        d, _, _ = everyone(k)
        wait_for(gt_all.at[0], r_of(fam.gt, d))

    loop(1, 2 * PARTS, wait_gt)
    grad_normed = gt_all[...].reshape(WIDTH, IDS).T
    o_rows[0:1, :] = jnp.sum(grad_normed * unit_one, axis=0, keepdims=True)
    o_rows[1:2, :] = jnp.sum(grad_normed, axis=0, keepdims=True)
    scaled = grad_normed * par_v[0:1, :]
    grad_embed = inverse_one * (
        scaled
        - jnp.mean(scaled, axis=-1, keepdims=True)
        - unit_one * jnp.mean(scaled * unit_one, axis=-1, keepdims=True)
    )
    emb_v[...] = totals[0:12] + grad_embed[0:12]
    store(o_rows.at[0], out.gain_one)
    store(o_rows.at[1], out.bias_one)
    store(emb_v, out.embed_table)

    def sent(name, ref, low, high):
        loop(low, high, lambda k: wait_for(ref, s_of(name, k)))

    sent(fam.p, p_send.at[0], 1, PARTS)
    sent(fam.tok, tok_v, 1, PARTS)
    sent(fam.filt, filt_all.at[0], 0, 1)
    sent(fam.px, px_send, 0, 1)
    sent(fam.outz, out_all.at[0, 0, 0], 1, 4)
    sent(fam.outp, out_all.at[0, 0], 1, 4)
    sent(fam.outt, out_all.at[0, 0], 0, 4)
    sent(fam.up, up_send.at[0], 1, 4)
    sent(fam.upz, up_all.at[0, 0], 1, 4)
    sent(fam.upt, up_all.at[0, 0], 0, 4)
    sent(fam.seed, seed_all.at[0], 1, 4)
    sent(fam.down, down_all.at[0, 0], 1, 4)
    sent(fam.downt, down_all.at[0, 0], 0, 4)
    for g in range(GROUPS):
        sent(fam.mix, mix_send.at[0, 0:LANE_CH, :], g * PARTS + 1, (g + 1) * PARTS)
        sent(fam.gm, gm_send.at[0, 0:LANE_CH, :], g * PARTS + 1, (g + 1) * PARTS)
    sent(fam.n2, n2_all.at[0], 1, 4)
    sent(fam.gn, gn_all.at[0], 1, 4)
    sent(fam.po, po_all.at[0], 1, 4)
    sent(fam.sdt, sd_y, 0, 1)
    sent(fam.sut, su_y, 0, 1)
    sent(fam.sot, so_y, 0, 1)
    sent(fam.sd, sd_t.at[0], 1, 4)
    sent(fam.su, su_t.at[0], 1, 4)
    sent(fam.su2, su_p.at[0], 1, 4)
    sent(fam.so, so_t.at[0], 1, 4)
    sent(fam.so2, so_u.at[0], 1, 4)
    sent(fam.bt, b_x, 0, 1)
    sent(fam.b, b_p.at[0], 1, 4)
    sent(fam.b2, b_t, 1, 4)
    sent(fam.bf, b_f.at[0], 0, 1)
    sent(fam.m, m_send, 1, 8)
    sent(fam.m2, m2_send, 1, 4)
    sent(fam.z, z_send, 1, PARTS)
    sent(fam.zx, zx_send, 0, 1)
    sent(fam.f, f_recv, 0, 1)
    sent(fam.gt, gt_all.at[0], 1, 2 * PARTS)
    for copy in stores:
        copy.wait()


def copy_kernel(*refs):
    count = len(OUTPUTS)
    for source, target in zip(refs[:count], refs[count:]):
        target[...] = source[...]


FAMILIES = dict(
    p=16, tok=16, filt=1, px=1, outz=4, outp=4, outt=4, up=4,
    upz=4, upt=4, down=4, downt=4, seed=4, mix=48, gm=48, n2=4,
    gn=4, po=4, sdt=1, sd=4, sut=1, su=4, su2=4, sot=1, so=4,
    so2=4, bt=1, b=4, b2=4, bf=1, m=8, m2=4, z=16, zx=1,
    f=1, gt=32,
)
INPUTS = dict(
    token_ids=0, embed_table=0, gain_one=0, bias_one=0, in_weight=0, in_bias=0, short_taps=0, short_bias=0,
    freq_weight=0, freq_bias=0, inner_weight=0, inner_bias=0, filter_weight=0, skip_scale=0, out_weight=0,
    out_bias=0, gain_two=0, bias_two=0, up_weight=0, up_bias=0, down_weight=0, down_bias=0, cotangent=0,
    mats=0, twist=0, feats=0,
)
OUTPUTS = dict(
    block=(ROWS, WIDTH), embed_table=(12, WIDTH), gain_one=(WIDTH,),
    bias_one=(WIDTH,), in_weight=(24, 3 * WIDTH), in_bias=(3 * WIDTH,),
    short_taps=(3, 3 * WIDTH), short_bias=(3 * WIDTH,), freq_weight=(33, 64),
    freq_bias=(64,), inner_weight=(64, 64), inner_bias=(64,),
    filter_weight=(LOCAL, 64), skip_scale=(2, WIDTH), out_weight=(24, WIDTH),
    out_bias=(WIDTH,), gain_two=(WIDTH,), bias_two=(WIDTH,),
    up_weight=(24, HIDDEN), up_bias=(HIDDEN,), down_weight=(96, WIDTH),
    down_bias=(WIDTH,),
)
SPECTRUM = (GROUPS, SPEC, 2 * ROWS)
SCRATCH = dict(
    tok=((1, ROWS), jnp.int32), emb=((12, WIDTH), F32), par=((32, WIDTH), F32),
    inw=((24, 3 * WIDTH), F32), mlp=((112, 64), F32), filt=((LOCAL, 64), F32),
    outw=((24, WIDTH), F32), upw=((24, HIDDEN), F32), downw=((96, WIDTH), F32),
    mats=((4, 256, 256), BF16), twist=((72, ROWS), F32), feats=((40, LENGTH), F32),
    normed_t=((WIDTH, IDS), F32), p_send=((PARTS, IDS, 3 * LOCAL), BF16),
    p_recv=((PARTS, IDS, 3 * LOCAL), BF16), px_send=((IDS, 256), F32), px_recv=((IDS, 256), F32),
    filt_all=((2, LOCAL, 64), BF16), tok_all=((PARTS, 1, ROWS), jnp.int32),
    up_send=((4, 24, SPLIT), BF16), up_all=((2, 4, 4, 24, SPLIT), BF16),
    out_all=((2, 4, 4, 24, WIDTH), BF16), seed_all=((4, ROWS, WIDTH), BF16),
    down_all=((2, 4, 96, WIDTH), BF16), w_up=((WIDTH, SPLIT), BF16), w_out=((WIDTH, WIDTH), BF16),
    act1=((72, LENGTH), F32), cos1=((64, LENGTH), F32), act2=((64, LENGTH), F32),
    cos2=((64, LENGTH), F32), kern=((2, PARTS, LOCAL, ROWS), F32), par_t=((WIDTH, 32), F32),
    table_t=((3 * LOCAL, IDS), F32), onehot=((3 * IDS, LENGTH), F32),
    mix=((3, PARTS, LOCAL, ROWS), F32),
    hi=((2 * SPEC, 2 * ROWS), BF16), lo=((2 * SPEC, 2 * ROWS), BF16),
    spec_k1=(SPECTRUM, F32), spec_k2=(SPECTRUM, F32), spec_v=(SPECTRUM, F32),
    spec_g=(SPECTRUM, F32),
    first=((PARTS, LOCAL, ROWS), F32), gated=((PARTS, LOCAL, ROWS), F32),
    second=((PARTS, LOCAL, ROWS), F32),
    mix_send=((PARTS, LOCAL, ROWS), BF16), mix_recv=((PARTS, LOCAL, ROWS), BF16),
    gm_send=((PARTS, LOCAL, ROWS), BF16), gm_recv=((PARTS, LOCAL, ROWS), BF16),
    resid=((ROWS, WIDTH), F32), unit2=((ROWS, WIDTH), F32), inv2=((ROWS, 1), F32),
    n2_all=((4, ROWS, WIDTH), BF16), act_all=((4, ROWS, SPLIT), BF16),
    gl_all=((4, ROWS, SPLIT), BF16), po_all=((4, ROWS, WIDTH), BF16),
    po_recv=((4, ROWS, WIDTH), BF16), gn_all=((4, ROWS, WIDTH), BF16),
    gn_recv=((4, ROWS, WIDTH), BF16), gres=((ROWS, WIDTH), BF16),
    sd_x=((2, 4, 96, WIDTH), BF16), sd_y=((4, 96, WIDTH), BF16), sd_t=((4, 96, WIDTH), BF16),
    sd_z=((4, 96, WIDTH), BF16),
    su_x=((2, 4, 4, 24, SPLIT), BF16), su_y=((4, 4, 24, SPLIT), BF16),
    su_t=((4, 4, 24, SPLIT), BF16), su_z=((4, 4, 24, SPLIT), BF16), su_p=((4, 24, SPLIT), BF16),
    su_r=((4, 24, SPLIT), BF16),
    so_x=((2, 4, 4, 24, WIDTH), BF16), so_y=((4, 4, 24, WIDTH), BF16),
    so_t=((4, 4, 24, WIDTH), BF16), so_p=((4, 4, 24, WIDTH), BF16), so_u=((4, 24, WIDTH), BF16),
    so_z=((4, 24, WIDTH), BF16),
    b_x=((24, WIDTH), F32), b_y=((24, WIDTH), F32), b_p=((4, 24, 384), F32),
    b_t=((24, 384), F32), b_z=((4, 24, 384), F32), b_f=((2, 24, 384), F32),
    grad_mix=((3 * LOCAL, LENGTH), F32), raw=((2 * LOCAL, LENGTH), F32), q_s=((LOCAL, 128), F32),
    z_send=((IDS, 256), BF16), z_recv=((PARTS, IDS, 256), BF16), zx_send=((IDS, 256), F32),
    zx_recv=((IDS, 256), F32), wide=((IDS, 4 * WIDTH), F32), gt_all=((32, 24, IDS), F32),
    m_send=((80, 128), BF16), m_recv=((8, 80, 128), BF16), m2_send=((80, 128), BF16),
    m2_recv=((4, 80, 128), BF16), f_send=((2 * LOCAL, 64), F32), f_recv=((LOCAL, 64), F32),
    o_in=((24, 3 * WIDTH), F32), o_wide=((1, 3 * WIDTH), F32), o_rows=((8, WIDTH), F32),
    o_up=((1, HIDDEN), F32),
)


def fits(mesh_shape, args):
    return (
        mesh_shape["dp"] == 2
        and mesh_shape["seq"] == PARTS
        and args[0].shape == (1, ROWS)
        and args[1].shape == (12, WIDTH)
        and args[4].shape == (24, 3 * WIDTH)
        and args[8].shape == (33, 64)
        and args[18].shape == (24, HIDDEN)
    )


def fast_device(*args):
    given = SimpleNamespace(**dict(zip(INPUTS, args)))
    tables = tables_of(given.freq_weight.shape[0])
    given.mats, given.twist, given.feats = (jnp.asarray(table) for table in tables)
    given.cotangent = given.cotangent[0]
    anywhere, near = (pl.BlockSpec(memory_space=space) for space in (pl.ANY, pltpu.VMEM))
    shapes = [jax.ShapeDtypeStruct(shape, F32) for shape in OUTPUTS.values()]
    sem_count = sum(FAMILIES.values())
    made = pl.pallas_call(
        step_kernel,
        out_shape=shapes,
        in_specs=[anywhere] * len(INPUTS),
        out_specs=[anywhere] * len(shapes),
        scratch_shapes=[pltpu.VMEM(shape, kind) for shape, kind in SCRATCH.values()]
        + [pltpu.SemaphoreType.DMA((count,)) for count in (sem_count, sem_count, 48, len(shapes))],
        compiler_params=pltpu.CompilerParams(
            collective_id=0, has_side_effects=True, vmem_limit_bytes=60 * 1024 * 1024
        ),
    )(*(getattr(given, name) for name in INPUTS))
    made = pl.pallas_call(
        copy_kernel,
        out_shape=shapes,
        in_specs=[near] * len(shapes),
        out_specs=[near] * len(shapes),
    )(*made)
    return (made[0][None], *made[1:])


def solution(mesh):
    in_specs = (
        P("dp", "seq"),
        P(),
        P(),
        P(),
        P(("dp", "seq"), None),
        P(),
        P(),
        P(),
        P(),
        P(),
        P(),
        P(),
        P(("dp", "seq"), None),
        P(),
        P(("dp", "seq"), None),
        P(),
        P(),
        P(),
        P(("dp", "seq"), None),
        P(),
        P(("dp", "seq"), None),
        P(),
        P("dp", "seq", None),
    )
    out_specs = (
        P("dp", "seq", None),
        P(),
        P(),
        P(),
        P(("dp", "seq"), None),
        P(),
        P(),
        P(),
        P(),
        P(),
        P(),
        P(),
        P(("dp", "seq"), None),
        P(),
        P(("dp", "seq"), None),
        P(),
        P(),
        P(),
        P(("dp", "seq"), None),
        P(),
        P(("dp", "seq"), None),
        P(),
    )

    def either(*args):
        return (fast_device if fits(mesh.shape, args) else per_device)(*args)

    return jax.shard_map(
        either, mesh=mesh, in_specs=in_specs, out_specs=out_specs, check_vma=False
    )
```

```python
import math
from types import SimpleNamespace

import jax
import jax.numpy as jnp
import ml_dtypes
import numpy as np
from jax import lax
from jax.experimental import pallas as pl
from jax.experimental.pallas import tpu as pltpu
from jax.sharding import PartitionSpec as P

epsilon = 1e-05
slow_rate = -math.log(0.01) / 1.5
fast_rate = -math.log(0.01) / 0.3
decay_shift = 0.05
highest = lax.Precision.HIGHEST


def exact_dot(left_side, right_side):
    return jnp.dot(left_side, right_side, precision=highest, preferred_element_type=jnp.float32)


def narrow_dot(left_side, right_side):
    return jnp.dot(left_side, right_side, preferred_element_type=jnp.float32)


def rows_inner(left_side, right_side, accuracy=None):
    return lax.dot_general(
        left_side,
        right_side,
        (((0,), (0,)), ((), ())),
        precision=accuracy,
        preferred_element_type=jnp.float32,
    )


def against_rows(left_side, right_side, accuracy=None):
    return lax.dot_general(
        left_side,
        right_side,
        (((1,), (1,)), ((), ())),
        precision=accuracy,
        preferred_element_type=jnp.float32,
    )


def normalize(values):
    center = values - jnp.mean(values, axis=-1, keepdims=True)
    inverse = lax.rsqrt(jnp.mean(center * center, axis=-1, keepdims=True) + epsilon)
    return (center * inverse, inverse)


def norm_back(upstream, unit_vals, inverse):
    return inverse * (
        upstream
        - jnp.mean(upstream, axis=-1, keepdims=True)
        - unit_vals * jnp.mean(upstream * unit_vals, axis=-1, keepdims=True)
    )


def angle_table(row_count, column_count, modulus):
    product = (
        jnp.arange(row_count, dtype=jnp.int32)[:, None]
        * jnp.arange(column_count, dtype=jnp.int32)[None, :]
        % modulus
    )
    angles = 2.0 * math.pi / modulus * product.astype(jnp.float32)
    return (jnp.cos(angles), jnp.sin(angles))


def forward_transform(signal, tables):
    cos_section, sin_section, cos_twist, sin_twist, cos_last, sin_last = tables
    real_first = jnp.einsum("kn,...nm->...km", cos_section, signal, precision=highest)
    imag_first = -jnp.einsum("kn,...nm->...km", sin_section, signal, precision=highest)
    real_turn = real_first * cos_twist + imag_first * sin_twist
    imag_turn = imag_first * cos_twist - real_first * sin_twist
    real_out = exact_dot(real_turn, cos_last) + exact_dot(imag_turn, sin_last)
    imag_out = exact_dot(imag_turn, cos_last) - exact_dot(real_turn, sin_last)
    return (real_out, imag_out)


def inverse_transform(real_spec, imag_spec, tables):
    cos_section, sin_section, cos_twist, sin_twist, cos_last, sin_last = tables
    real_turn = exact_dot(real_spec, cos_last) - exact_dot(imag_spec, sin_last)
    imag_turn = exact_dot(imag_spec, cos_last) + exact_dot(real_spec, sin_last)
    real_first = real_turn * cos_twist - imag_turn * sin_twist
    imag_first = imag_turn * cos_twist + real_turn * sin_twist
    signal = jnp.einsum("kn,...km->...nm", cos_section, real_first, precision=highest) - jnp.einsum(
        "kn,...km->...nm", sin_section, imag_first, precision=highest
    )
    return signal / (cos_twist.shape[0] * cos_twist.shape[1])


def multiply(real_one, imag_one, real_two, imag_two):
    return (real_one * real_two - imag_one * imag_two, real_one * imag_two + imag_one * real_two)


def multiply_conj(real_one, imag_one, real_two, imag_two):
    return (real_one * real_two + imag_one * imag_two, imag_one * real_two - real_one * imag_two)


def to_channels(rows_in):
    return lax.all_to_all(rows_in.T, "seq", split_axis=0, concat_axis=1, tiled=True)


def to_rows(columns):
    return lax.all_to_all(columns, "seq", split_axis=1, concat_axis=0, tiled=True).T


def gather_all(pieces):
    shapes = [piece.shape for piece in pieces]
    flat = jnp.concatenate([piece.astype(jnp.bfloat16).reshape(-1) for piece in pieces])
    whole = lax.all_gather(flat, ("dp", "seq"), axis=0, tiled=False)
    result, start = [], 0
    for shape in shapes:
        size = math.prod(shape)
        result.append(whole[:, start : start + size].reshape((-1,) + shape[1:]))
        start += size
    return result


def per_device(
    token_ids,
    embed_table,
    gain_one,
    bias_one,
    in_weight,
    in_bias,
    short_taps,
    short_bias,
    freq_weight,
    freq_bias,
    inner_weight,
    inner_bias,
    filter_weight,
    skip_scale,
    out_weight,
    out_bias,
    gain_two,
    bias_two,
    up_weight,
    up_bias,
    down_weight,
    down_bias,
    cotangent,
):
    tokens = token_ids[0]
    row_count = tokens.shape[0]
    vocab, model_width = embed_table.shape
    seq_parts = lax.axis_size("seq")
    seq_index = lax.axis_index("seq")
    dp_index = lax.axis_index("dp")
    local_width = model_width // seq_parts
    length = row_count * seq_parts
    freq_rows = 2 * seq_parts
    low_rows = seq_index * local_width

    def own_channels(table):
        parts = table.reshape(table.shape[0], -1, model_width)
        return lax.dynamic_slice_in_dim(parts, low_rows, local_width, 2)

    in_full, out_full, up_full, down_full, filter_full, tokens_full = gather_all(
        (in_weight, out_weight, up_weight, down_weight, filter_weight, token_ids)
    )
    sequence = lax.dynamic_slice_in_dim(
        tokens_full.reshape(-1, length), dp_index, 1, 0
    )[0].astype(jnp.int32)
    cos_section, sin_section = angle_table(freq_rows, seq_parts, freq_rows)
    cos_twist, sin_twist = angle_table(freq_rows, row_count, freq_rows * row_count)
    cos_last, sin_last = angle_table(row_count, row_count, row_count)
    tables = (cos_section, sin_section, cos_twist, sin_twist, cos_last, sin_last)

    unit_one, inverse_one = normalize(embed_table)
    normed = (unit_one * gain_one + bias_one).astype(jnp.bfloat16)
    table = narrow_dot(normed, in_full) + in_bias
    local_table = own_channels(table)
    local_taps = own_channels(short_taps)
    local_bias = own_channels(short_bias[None])[0]
    local_skip = own_channels(skip_scale)[:, 0, :, None]
    ids = jnp.arange(vocab, dtype=jnp.int32)[:, None]
    padded = jnp.concatenate([jnp.full((2,), -1, jnp.int32), sequence])
    shifted = jnp.concatenate(
        [(padded[None, j : j + length] == ids).astype(jnp.float32) for j in range(3)], axis=0
    )
    weights = (local_taps[:, None] * local_table[None]).reshape(3 * vocab, 3 * local_width)
    mixed = rows_inner(weights, shifted, highest) + local_bias.reshape(-1, 1)
    gate_outer = mixed[:local_width]
    gate_inner = mixed[local_width : 2 * local_width]
    value_part = mixed[2 * local_width :]

    count = (freq_weight.shape[0] - 1) // 2
    position_phase = jnp.arange(length, dtype=jnp.float32) / length
    levels = 0.0001 + jnp.arange(count, dtype=jnp.float32) * ((count - 1 - 0.0001) / (count - 1))
    angles = 2.0 * math.pi * position_phase[None, :] * levels[:, None]
    features = jnp.concatenate([position_phase[None, :], jnp.cos(angles), -jnp.sin(angles)], axis=0)
    first_pre = rows_inner(freq_weight, features, highest) + freq_bias[:, None]
    first_act = jnp.sin(first_pre)
    second_pre = rows_inner(inner_weight, first_act, highest) + inner_bias[:, None]
    second_act = jnp.sin(second_pre)
    channel = (low_rows + jnp.arange(local_width, dtype=jnp.int32)).astype(jnp.float32) / (
        model_width - 1
    )
    decay_rate = slow_rate + (fast_rate - slow_rate) * channel
    decay = jnp.exp(-position_phase[None, :] * decay_rate[:, None]) + decay_shift
    local_filter = lax.dynamic_slice_in_dim(
        filter_full.reshape(2, model_width, -1), low_rows, local_width, 1
    ).astype(jnp.float32).reshape(2 * local_width, -1)
    kernels = exact_dot(local_filter, second_act).reshape(2, local_width, length) * decay

    def forth(signal):
        shape = signal.shape[:-1] + (seq_parts, row_count)
        return forward_transform(signal.reshape(shape), tables)

    def back(real_spec, imag_spec):
        result = inverse_transform(real_spec, imag_spec, tables)
        return result.reshape(result.shape[:-2] + (length,))

    kernel_real, kernel_imag = forth(kernels)
    value_real, value_imag = forth(value_part)
    first_conv = (
        back(*multiply(value_real, value_imag, kernel_real[0], kernel_imag[0]))
        + local_skip[0] * value_part
    )
    gated = gate_inner * first_conv
    gated_real, gated_imag = forth(gated)
    second_conv = (
        back(*multiply(gated_real, gated_imag, kernel_real[1], kernel_imag[1]))
        + local_skip[1] * gated
    )
    mixer = to_rows((gate_outer * second_conv).astype(jnp.bfloat16))

    onehot = (tokens[:, None] == ids[:, 0][None, :]).astype(jnp.float32)
    hidden = exact_dot(onehot, embed_table)
    residual = hidden + narrow_dot(mixer, out_full) + out_bias
    unit_two, inverse_two = normalize(residual)
    normed_two = (unit_two * gain_two + bias_two).astype(jnp.bfloat16)
    lifted = narrow_dot(normed_two, up_full) + up_bias
    normal_cdf = 0.5 * (1.0 + lax.erf(lifted * (1.0 / math.sqrt(2.0))))
    activated = (lifted * normal_cdf).astype(jnp.bfloat16)
    block_out = residual + narrow_dot(activated, down_full) + down_bias
    seed_low = cotangent[0]
    seed = seed_low.astype(jnp.float32)
    grad_down_bias = jnp.sum(seed, axis=0)
    grad_down = rows_inner(activated, seed_low)
    grad_activated = against_rows(seed_low, down_full)
    normal_pdf = jnp.exp(-0.5 * lifted * lifted) * (1.0 / math.sqrt(2.0 * math.pi))
    grad_lifted = grad_activated * (normal_cdf + lifted * normal_pdf)
    grad_up_bias = jnp.sum(grad_lifted, axis=0)
    lifted_low = grad_lifted.astype(jnp.bfloat16)
    grad_up = rows_inner(normed_two, lifted_low)
    grad_normed_two = against_rows(lifted_low, up_full)
    grad_gain_two = jnp.sum(grad_normed_two * unit_two, axis=0)
    grad_bias_two = jnp.sum(grad_normed_two, axis=0)
    grad_residual = seed + norm_back(grad_normed_two * gain_two, unit_two, inverse_two)
    grad_out_bias = jnp.sum(grad_residual, axis=0)
    residual_low = grad_residual.astype(jnp.bfloat16)
    grad_out = rows_inner(mixer, residual_low)
    grad_mixer = to_channels(against_rows(residual_low, out_full).astype(jnp.bfloat16)).astype(
        jnp.float32
    )
    embed_sum = rows_inner(onehot, grad_residual, highest)

    grad_outer = grad_mixer * second_conv
    grad_second = grad_mixer * gate_outer
    skip_second = jnp.sum(grad_second * gated, axis=1)
    back_real, back_imag = forth(grad_second)
    grad_gated = grad_second * local_skip[1] + back(
        *multiply_conj(back_real, back_imag, kernel_real[1], kernel_imag[1])
    )
    kernel_grad_two = back(*multiply_conj(back_real, back_imag, gated_real, gated_imag))
    grad_inner_gate = grad_gated * first_conv
    grad_first = grad_gated * gate_inner
    skip_first = jnp.sum(grad_first * value_part, axis=1)
    early_real, early_imag = forth(grad_first)
    grad_value = grad_first * local_skip[0] + back(
        *multiply_conj(early_real, early_imag, kernel_real[0], kernel_imag[0])
    )
    kernel_grad_one = back(*multiply_conj(early_real, early_imag, value_real, value_imag))
    grad_mixed = jnp.concatenate([grad_outer, grad_inner_gate, grad_value], axis=0)
    id_sums = against_rows(shifted, grad_mixed, highest).reshape(3, vocab, 3, local_width)
    local_sums = jnp.sum(id_sums * local_taps[:, None], axis=0)
    local_taps_grad = jnp.sum(id_sums * local_table[None], axis=1)
    local_short_bias = jnp.sum(id_sums[2], axis=0, keepdims=True)
    local_small = jnp.concatenate(
        [
            local_sums,
            local_taps_grad,
            local_short_bias,
            jnp.pad(jnp.stack([skip_first, skip_second])[:, None], ((0, 0), (0, 2), (0, 0))),
        ],
        axis=0,
    )
    wide_small = lax.dynamic_update_slice_in_dim(
        jnp.zeros((local_small.shape[0], 3, model_width), jnp.float32), local_small, low_rows, 2
    )

    raw_grads = (jnp.stack([kernel_grad_one, kernel_grad_two]) * decay).reshape(
        2 * local_width, length
    )
    grad_local_filter = against_rows(raw_grads, second_act, highest).reshape(2, local_width, -1)
    grad_second_act = rows_inner(local_filter, raw_grads, highest)
    grad_second_pre = grad_second_act * jnp.cos(second_pre)
    grad_inner_weight = against_rows(first_act, grad_second_pre, highest)
    grad_inner_bias = jnp.sum(grad_second_pre, axis=1)
    grad_first_pre = exact_dot(inner_weight, grad_second_pre) * jnp.cos(first_pre)
    grad_freq_weight = against_rows(features, grad_first_pre, highest)
    grad_freq_bias = jnp.sum(grad_first_pre, axis=1)
    sum_filter = lax.psum_scatter(grad_local_filter, "dp", scatter_dimension=0, tiled=False)

    devices = lax.axis_size("dp") * seq_parts
    up_rows = model_width // devices
    pieces = jnp.concatenate(
        [
            grad_up.reshape(devices, -1, model_width),
            grad_down.reshape(devices, -1, model_width),
            grad_out.reshape(devices, -1, model_width),
        ],
        axis=1,
    )
    summed = lax.psum_scatter(pieces, ("dp", "seq"), scatter_dimension=0, tiled=False)
    up_size = up_rows * up_weight.shape[1] // model_width
    sum_up = summed[:up_size].reshape(up_weight.shape)
    sum_down = summed[up_size : up_size + down_weight.shape[0]]
    sum_out = summed[up_size + down_weight.shape[0] :]

    (
        wide_small,
        embed_sum,
        sum_freq_weight,
        sum_freq_bias,
        sum_inner_weight,
        sum_inner_bias,
        sum_out_bias,
        sum_gain_two,
        sum_bias_two,
        sum_up_bias,
        sum_down_bias,
    ) = lax.psum(
        (
            wide_small,
            embed_sum,
            grad_freq_weight,
            grad_freq_bias,
            grad_inner_weight,
            grad_inner_bias,
            grad_out_bias,
            grad_gain_two,
            grad_bias_two,
            grad_up_bias,
            grad_down_bias,
        ),
        ("dp", "seq"),
    )
    total_ids = wide_small[:vocab].reshape(vocab, 3 * model_width)
    sum_taps = wide_small[vocab : vocab + 3].reshape(3, 3 * model_width)
    sum_short_bias = wide_small[vocab + 3].reshape(3 * model_width)
    sum_skip = wide_small[vocab + 4 :, 0]
    sum_in_bias = jnp.sum(total_ids, axis=0)
    own_row = (dp_index * seq_parts + seq_index) * up_rows
    own_normed = lax.dynamic_slice_in_dim(normed, own_row, up_rows, 1).astype(jnp.float32)
    sum_in = rows_inner(own_normed, total_ids, highest)
    grad_normed = against_rows(total_ids, in_full.astype(jnp.float32), highest)
    sum_gain_one = jnp.sum(grad_normed * unit_one, axis=0)
    sum_bias_one = jnp.sum(grad_normed, axis=0)
    sum_embed = embed_sum + norm_back(grad_normed * gain_one, unit_one, inverse_one)
    return (
        block_out[None],
        sum_embed,
        sum_gain_one,
        sum_bias_one,
        sum_in,
        sum_in_bias,
        sum_taps,
        sum_short_bias,
        sum_freq_weight,
        sum_freq_bias,
        sum_inner_weight,
        sum_inner_bias,
        sum_filter,
        sum_skip,
        sum_out,
        sum_out_bias,
        sum_gain_two,
        sum_bias_two,
        sum_up,
        sum_up_bias,
        sum_down,
        sum_down_bias,
    )


F32, BF16 = jnp.float32, jnp.bfloat16
ROWS, PARTS, LOCAL, WIDTH, HIDDEN, SPLIT, IDS = 128, 16, 48, 768, 3072, 768, 16
GROUPS, LANE_CH = 3, 16
BINS = PARTS + 1
SPEC = BINS * LANE_CH
LENGTH = ROWS * PARTS


def tables_of(feature_count):
    b = np.arange(ROWS)
    grid = 2 * np.pi * ((b[:, None] * b[None, :]) % ROWS) / ROWS
    cos, sin = np.cos(grid), np.sin(grid)
    forth = np.block([[cos, -sin], [sin, cos]])
    high = forth.astype(ml_dtypes.bfloat16)
    low = (forth - high.astype(np.float64)).astype(ml_dtypes.bfloat16)
    mats = np.stack([high, low, high.T, low.T])
    k = np.arange(BINS)
    turn = 2 * np.pi * k[:, None] * b[None, :] / (2 * LENGTH)
    scale = np.where((k == 0) | (k == PARTS), 1.0, 2.0)[:, None] / (2 * LENGTH)
    twist = np.zeros((72, ROWS))
    twist[0:17], twist[17:34] = np.cos(turn), np.sin(turn)
    twist[34:51], twist[51:68] = np.cos(turn) * scale, np.sin(turn) * scale
    count = (feature_count - 1) // 2
    phase = np.arange(LENGTH, dtype=np.float32) / np.float32(LENGTH)
    levels = np.float32(0.0001) + np.arange(count, dtype=np.float32) * np.float32(
        (count - 1 - 0.0001) / (count - 1)
    )
    angle = np.float32(2.0 * math.pi) * phase[None, :] * levels[:, None]
    feats = np.zeros((40, LENGTH), np.float32)
    feats[0] = phase
    feats[1 : 1 + count] = np.cos(angle.astype(np.float64))
    feats[1 + count : 1 + 2 * count] = -np.sin(angle.astype(np.float64))
    feats[1 + 2 * count] = 1.0
    return mats, twist.astype(np.float32), feats


def times_turn(value, quarter_count, k, m):
    re, im = value
    c, s = math.cos(math.pi * k / m), math.sin(math.pi * k / m)
    if im is None:
        return (re * c, re * (-s))
    return (re * c + im * s, im * c - re * s)


def real_spectrum(xs):
    m = len(xs)
    if m == 1:
        return [(xs[0], None), (xs[0], None)]
    even, odd = real_spectrum(xs[0::2]), real_spectrum(xs[1::2])
    bins = [None] * (m + 1)
    bins[0] = (even[0][0] + odd[0][0], None)
    bins[m] = (even[0][0] - odd[0][0], None)
    half = m // 2
    bins[half] = (even[half][0], -odd[half][0])
    for k in range(1, half):
        er, ei = even[k]
        tr, ti = times_turn(odd[k], None, k, m)
        bins[k] = (er + tr, ei + ti)
        bins[m - k] = (er - tr, ti - ei)
    return bins


def real_signal(bins):
    m = len(bins) - 1
    if m == 1:
        return [bins[0][0] + bins[1][0]]
    half = m // 2
    even, odd = [None] * (half + 1), [None] * (half + 1)
    even[0] = (bins[0][0] + bins[m][0], None)
    odd[0] = (bins[0][0] - bins[m][0], None)
    even[half] = (bins[half][0], None)
    odd[half] = (-bins[half][1], None)
    for k in range(1, half):
        (ar, ai), (br, bi) = bins[k], bins[m - k]
        even[k] = (ar + br, ai - bi)
        dr, di = ar - br, ai + bi
        c, s = math.cos(math.pi * k / m), math.sin(math.pi * k / m)
        odd[k] = (dr * c - di * s, di * c + dr * s)
    first, second = real_signal(even), real_signal(odd)
    out = [None] * m
    out[0::2], out[1::2] = first, second
    return out


def sin_cos(x):
    n = jnp.floor(x * (1.0 / math.pi) + 0.5)
    r = x - n * 3.140625
    r = r - n * 9.67025756835937500000e-4
    r = r - n * 6.2771141529083251953e-7
    r = r - n * 1.2154201256553420762e-10
    flip = 1.0 - 2.0 * (n - 2.0 * jnp.floor(n * 0.5))
    q = r * r
    s = -2.50507477628578072866e-8
    s = s * q + 2.75573136213857245213e-6
    s = s * q - 1.98412698295895385996e-4
    s = s * q + 8.33333333332211858878e-3
    s = s * q - 1.66666666666666307295e-1
    s = (s * q) * r + r
    c = 2.08757008419747316778e-9
    c = c * q - 2.75573141792967388112e-7
    c = c * q + 2.48015872888517045348e-5
    c = c * q - 1.38888888888730564116e-3
    c = c * q + 4.16666666666665929218e-2
    c = c * q - 0.5
    c = c * q + 1.0
    return s * flip, c * flip


def dot32(a, b, ca, cb, precision=lax.Precision.HIGH):
    return lax.dot_general(
        a, b, (((ca,), (cb,)), ((), ())), precision=precision, preferred_element_type=F32
    )


def dot16(a, b, ca, cb):
    return lax.dot_general(a, b, (((ca,), (cb,)), ((), ())), preferred_element_type=F32)


def start_push(src, dst, send, recv, dp, seq):
    pltpu.make_async_remote_copy(
        src_ref=src,
        dst_ref=dst,
        send_sem=send,
        recv_sem=recv,
        device_id=(dp, seq),
        device_id_type=pl.DeviceIdType.MESH,
    ).start()


def wait_for(ref, sem):
    pltpu.make_async_copy(ref, ref, sem).wait()


def step_kernel(*refs):
    it = iter(refs)

    def take(count):
        return [next(it) for _ in range(count)]

    sources = take(len(INPUTS))
    sinks = take(len(OUTPUTS))
    v = SimpleNamespace(**dict(zip(SCRATCH, take(len(SCRATCH)))))
    sem_s, sem_r, sem_l, sem_o = take(4)
    src = SimpleNamespace(**dict(zip(INPUTS, sources)))
    out = SimpleNamespace(**dict(zip(OUTPUTS, sinks)))
    tok_v, emb_v, par_v, inw_v, mlp_v, filt_v = v.tok, v.emb, v.par, v.inw, v.mlp, v.filt
    outw_v, upw_v, downw_v, mats_v, twist_v, feats_v = v.outw, v.upw, v.downw, v.mats, v.twist, v.feats
    dp, seq = lax.axis_index("dp"), lax.axis_index("seq")
    me = dp * PARTS + seq
    z, yc = lax.div(seq, 4), lax.rem(seq, 4)
    y, core = lax.div(yc, 2), lax.rem(yc, 2)
    chip = dp * 2 + y
    twin = seq + 1 - 2 * core
    other_core = 1 - core
    other_dp = 1 - dp

    def tile(index, size):
        return pl.ds(pl.multiple_of(index * size, size), size)

    def everyone(k):
        d = lax.rem(me + k, 2 * PARTS)
        return d, lax.div(d, PARTS), lax.rem(d, PARTS)

    def of_seq(k):
        return lax.rem(seq + k, PARTS)

    def of_plane(k):
        xx, yy = lax.rem(dp + lax.div(k, 2), 2), lax.rem(y + lax.rem(k, 2), 2)
        return xx * 2 + yy, xx, z * 4 + yy * 2 + core

    def of_line(k):
        zz = lax.rem(z + k, 4)
        return zz, zz * 4 + yc

    def of_eight(k):
        j = lax.rem(dp * 4 + yc + k, 8)
        return j, lax.div(j, 4), z * 4 + lax.rem(j, 4)

    def loop(low, high, body):
        def step(k, carry):
            body(k)
            return carry

        lax.fori_loop(low, high, step, 0)

    firsts = np.cumsum([0] + list(FAMILIES.values())).tolist()
    fam = SimpleNamespace(**dict(zip(FAMILIES, zip(range(len(FAMILIES)), firsts))))

    def s_of(family):
        return sem_s.at[family[0]]

    def r_of(family, index=0):
        return sem_r.at[family[1] + index]

    def push(family, source, target, dp_to, seq_to, index=0):
        start_push(source, target, s_of(family), r_of(family, index), dp_to, seq_to)

    def arrived(family, ref, index=0):
        wait_for(ref, r_of(family, index))

    barrier = pltpu.get_barrier_semaphore()

    def greet(k):
        _, d, s = everyone(k)
        pl.semaphore_signal(barrier, inc=1, device_id=(d, s), device_id_type=pl.DeviceIdType.MESH)

    loop(1, 2 * PARTS, greet)
    loads = []

    def load(source, target):
        copy = pltpu.make_async_copy(source, target, sem_l.at[len(loads)])
        copy.start()
        loads.append(copy)

    def load_row(source, row):
        target = par_v.at[row] if len(source.shape) == 1 else par_v.at[row : row + 1, :]
        pltpu.make_async_copy(source, target, sem_l.at[LOADS]).start()

    def wait_load(*which):
        for i in which:
            loads[i].wait()

    load(src.embed_table, emb_v)
    load(src.gain_one, par_v.at[0])
    load(src.bias_one, par_v.at[1])
    load(src.in_weight, inw_v)
    load(src.token_ids, tok_v)
    load(src.filter_weight, filt_v)
    LOAD_WEIGHTS = len(loads)
    load(src.up_weight, upw_v)
    load(src.out_weight, outw_v)
    load(src.cotangent, v.seed_all.at[chip])
    load(src.down_weight, downw_v)
    LOAD_NET = len(loads)
    load(src.freq_weight, mlp_v.at[0:33, :])
    load(src.freq_bias, mlp_v.at[33])
    load(src.inner_weight, mlp_v.at[40:104, :])
    load(src.inner_bias, mlp_v.at[104])
    load(src.feats, feats_v)
    LOAD_TAIL = len(loads)
    load(src.mats, mats_v)
    load(src.twist, twist_v)
    for p in range(3):
        at = pl.ds(p * WIDTH, WIDTH)
        load_row(src.in_bias.at[at], 2 + p)
        load_row(src.short_bias.at[at], 14 + p)
        for t in range(3):
            load_row(src.short_taps.at[t : t + 1, at], 5 + 3 * t + p)
    for t in range(2):
        load_row(src.skip_scale.at[t : t + 1, :], 17 + t)
    load(src.out_bias, par_v.at[19])
    load_row(src.gain_two, 20)
    load_row(src.bias_two, 21)
    load_row(src.down_bias, 22)
    for r in range(4):
        load_row(src.up_bias.at[pl.ds(r * WIDTH, WIDTH)], 23 + r)
    LOAD_END = len(loads)

    wait_load(*range(LOAD_WEIGHTS))
    lanes16 = lax.broadcasted_iota(jnp.int32, (IDS, WIDTH), 0)
    embed = jnp.concatenate([emb_v[...], jnp.zeros((4, WIDTH), F32)], axis=0)
    center = embed - jnp.mean(embed, axis=-1, keepdims=True)
    inverse_one = lax.rsqrt(jnp.mean(center * center, axis=-1, keepdims=True) + epsilon)
    unit_one = center * inverse_one
    normed = (unit_one * par_v[0:1, :] + par_v[1:2, :]).astype(BF16).astype(F32)
    normed = jnp.where(lanes16 < 12, normed, 0.0)
    normed_t = v.normed_t
    normed_t[...] = normed.T
    in_low = inw_v[...].astype(BF16).astype(F32)
    partial = dot32(normed_t[tile(me, 24), :], in_low, 0, 0, None)
    p_send, p_recv = v.p_send, v.p_recv
    for i in range(PARTS):
        block = [partial[:, p * WIDTH + i * LOCAL : p * WIDTH + (i + 1) * LOCAL] for p in range(3)]
        p_send[i] = jnp.concatenate(block + [jnp.zeros((IDS, 256 - 3 * LOCAL), F32)], axis=1).astype(BF16)
    filt_all, tok_all = v.filt_all, v.tok_all
    filt_all[dp] = filt_v[...].astype(BF16)
    tok_all[seq] = tok_v[...]
    p_recv[seq] = p_send[seq]
    mlp_v[34:40, :] = jnp.zeros((6, 64), F32)
    mlp_v[105:112, :] = jnp.zeros((7, 64), F32)

    pl.semaphore_wait(barrier, 2 * PARTS - 1)

    def push_p(k):
        s = of_seq(k)
        push(fam.p, p_send.at[s], p_recv.at[seq], dp, s)

    loop(1, PARTS, push_p)
    wait_load(*range(LOAD_WEIGHTS, LOAD_NET))
    up_send, up_all, out_all, seed_all = v.up_send, v.up_all, v.out_all, v.seed_all
    out_all[core, chip, z] = outw_v[...].astype(BF16)

    def push_out(k):
        zz, s = of_line(k)
        mine = out_all.at[core, chip, z]
        push(fam.outz, mine, mine, dp, s)

    loop(1, 4, push_out)

    def push_tok(k):
        s = of_seq(k)
        push(fam.tok, tok_v, tok_all.at[seq], dp, s)

    loop(1, PARTS, push_tok)
    push(fam.filt, filt_all.at[dp], filt_all.at[dp], other_dp, seq)


    def shard_of(q, c, zz):
        return (q // 2) * PARTS + zz * 4 + (q % 2) * 2 + c

    for q in range(4):
        cut = [
            upw_v[:, 96 * shard_of(q, c, zz) : 96 * (shard_of(q, c, zz) + 1)]
            for c in range(2)
            for zz in range(4)
        ]
        up_send[q] = jnp.concatenate(cut, axis=1).astype(BF16)

    def push_up(k):
        q, d, s = of_plane(k)
        push(fam.up, up_send.at[q], up_all.at[core, z, chip], d, s)

    across = lax.rem(z + 2, 4)
    beside = z + 1 - 2 * lax.rem(z, 2)
    beside_across = lax.rem(beside + 2, 4)

    def to_twin(family, source, target=None):
        push(family, source, source if target is None else target, dp, twin)

    def to_line(family, source, target, zz, index):
        push(family, source, target, dp, zz * 4 + yc, index)

    loop(1, 4, push_up)
    up_all[core, z, chip] = up_send[chip]
    act1, cos1, act2, cos2 = v.act1, v.cos1, v.act2, v.cos2
    wait_load(*range(LOAD_NET, LOAD_TAIL))
    mlp = mlp_v[...]
    freq_t = mlp[0:40].T
    inner_bias = mlp[104:112].T[:, 0:1]
    inner = mlp[40:104]

    def network(i):
        at = tile(i, 512)
        s1, c1 = sin_cos(dot32(freq_t, feats_v[:, at], 1, 0))
        act1[0:64, at] = s1
        cos1[:, at] = c1
        act1[64:72, at] = jnp.where(
            lax.broadcasted_iota(jnp.int32, (8, 512), 0) == 0, 1.0, 0.0
        ).astype(F32)
        s2, c2 = sin_cos(dot32(inner, s1, 0, 0) + inner_bias)
        act2[:, at] = s2
        cos2[:, at] = c2

    loop(0, 4, network)
    arrived(fam.p, p_recv.at[0 : PARTS - 1])
    table = p_recv[0].astype(F32)
    for s in range(1, PARTS):
        table = table + p_recv[s].astype(F32)
    px_send, px_recv = v.px_send, v.px_recv
    px_send[...] = table
    push(fam.px, px_send, px_recv, other_dp, seq)
    arrived(fam.up, up_send.at[0:3])
    to_line(fam.upz, up_all.at[core, z], up_all.at[core, z], across, 0)
    to_twin(fam.upt, up_all.at[core, z])
    down_all = v.down_all
    down_all[core, z] = downw_v[...].astype(BF16)
    own_down = down_all.at[core, z]
    to_line(fam.down, own_down, own_down, beside, 1)
    to_twin(fam.downt, own_down)
    arrived(fam.outz, out_all.at[0, 0, 0:3])

    def gather_first(family, ref, k):
        _, d, s = of_plane(k)
        push(family, ref.at[chip], ref.at[chip], d, s, 0)

    def gather_second(family, ref, k):
        arrived(family, ref.at[0], 0)
        q, _, _ = of_plane(k)
        _, d, s = of_plane(3 - k)
        push(family, ref.at[chip], ref.at[chip], d, s, 1)
        push(family, ref.at[q], ref.at[q], d, s, 1)

    gather_first(fam.outp, out_all.at[core], 1)
    to_twin(fam.outt, out_all.at[core, chip])

    wait_load(*range(LOAD_TAIL, LOAD_END))
    wait_for(par_v.at[0:24], sem_l.at[LOADS])
    par_t = v.par_t
    for i in range(WIDTH // 128):
        par_t[128 * i : 128 * (i + 1), :] = par_v[:, 128 * i : 128 * (i + 1)].T
    own_par = par_t[tile(seq, LOCAL), :]

    kern, hi_ref, lo_ref = v.kern, v.hi, v.lo
    spec_k1, spec_k2, spec_v, spec_g = v.spec_k1, v.spec_k2, v.spec_v, v.spec_g
    arrived(fam.filt, filt_all.at[0])
    filt = jnp.concatenate([filt_all[0], filt_all[1]], axis=0).astype(F32)
    for i in range(LENGTH // 256):
        both = dot32(filt, act2[:, 256 * i : 256 * (i + 1)], 1, 0)
        for h in range(2):
            for f in range(2):
                kern[f, 2 * i + h] = both[f * LOCAL : (f + 1) * LOCAL, 128 * h : 128 * (h + 1)]
    lane = lax.broadcasted_iota(jnp.int32, (LANE_CH, ROWS), 1).astype(F32)

    def decay_of(g):
        row = lax.broadcasted_iota(jnp.int32, (LANE_CH, ROWS), 0) + (seq * LOCAL + g * LANE_CH)
        rate = slow_rate + (fast_rate - slow_rate) * (row.astype(F32) * (1.0 / (WIDTH - 1)))
        return lambda a: jnp.exp((lane + float(a * ROWS)) * (rate * (-1.0 / LENGTH))) + decay_shift

    def put(row0, k, re, im):
        rows = pl.ds(row0 + k * LANE_CH, LANE_CH)
        for part, value in ((0, re), (1, im)):
            at = pl.ds(part * ROWS, ROWS)
            high = value.astype(BF16)
            hi_ref[rows, at] = high
            lo_ref[rows, at] = (value - high.astype(F32)).astype(BF16)

    def forth(row0, values):
        for k, (re, im) in enumerate(real_spectrum(values)):
            c, s = twist_v[k : k + 1, :], twist_v[17 + k : 18 + k, :]
            if im is None:
                put(row0, k, re * c, re * (-s))
            else:
                put(row0, k, re * c + im * s, im * c - re * s)

    def dft(rows, which):
        high, low = hi_ref[0:rows, :], lo_ref[0:rows, :]
        m_high, m_low = mats_v[which], mats_v[which + 1]
        return dot16(high, m_high, 1, 0) + dot16(low, m_high, 1, 0) + dot16(high, m_low, 1, 0)

    def put_product(row0, spec, other, conj):
        a_re, a_im = spec[:, 0:ROWS], spec[:, ROWS:]
        b_re, b_im = other[:, 0:ROWS], other[:, ROWS:]
        if conj:
            re, im = a_re * b_re + a_im * b_im, a_im * b_re - a_re * b_im
        else:
            re, im = a_re * b_re - a_im * b_im, a_re * b_im + a_im * b_re
        rows = pl.ds(row0, SPEC)
        for part, value in ((0, re), (1, im)):
            at = pl.ds(part * ROWS, ROWS)
            high = value.astype(BF16)
            hi_ref[rows, at] = high
            lo_ref[rows, at] = (value - high.astype(F32)).astype(BF16)

    def back(turned, row0):
        bins = []
        for k in range(BINS):
            part = turned[row0 + k * LANE_CH : row0 + (k + 1) * LANE_CH]
            re, im = part[:, 0:ROWS], part[:, ROWS:]
            c, s = twist_v[34 + k : 35 + k, :], twist_v[51 + k : 52 + k, :]
            if k in (0, PARTS):
                bins.append((re * c - im * s, None))
            else:
                bins.append((re * c - im * s, im * c + re * s))
        return real_signal(bins)

    def kernel_spectra(g):
        at = tile(g, LANE_CH)
        decay = decay_of(g)
        damp = [decay(a) for a in range(PARTS)]
        forth(0, [kern[0, a, at, :] * damp[a] for a in range(PARTS)])
        forth(SPEC, [kern[1, a, at, :] * damp[a] for a in range(PARTS)])
        spec = dft(2 * SPEC, 0)
        spec_k1[g] = spec[0:SPEC]
        spec_k2[g] = spec[SPEC:]

    loop(0, GROUPS, kernel_spectra)


    table_t, onehot, mix = v.table_t, v.onehot, v.mix
    arrived(fam.px, px_recv)
    wide_t = (px_send[...] + px_recv[...]).T
    table_t[...] = jnp.concatenate(
        [wide_t[p * LOCAL : (p + 1) * LOCAL] + own_par[:, 2 + p : 3 + p] for p in range(3)], axis=0
    )

    arrived(fam.tok, tok_all.at[0 : PARTS - 1])
    id_rows = lax.broadcasted_iota(jnp.int32, (IDS, ROWS), 0)
    for a in range(PARTS):
        now = tok_all[a]
        if a == 0:
            long = jnp.concatenate([jnp.full((1, ROWS), -1, jnp.int32), now], axis=1)
        else:
            long = jnp.concatenate([tok_all[a - 1], now], axis=1)
        for t in range(3):
            moved = long[:, ROWS - 2 + t : 2 * ROWS - 2 + t]
            onehot[t * IDS : (t + 1) * IDS, a * ROWS : (a + 1) * ROWS] = (
                id_rows == moved
            ).astype(F32)

    def taps_of(t):
        return jnp.concatenate(
            [own_par[:, 5 + 3 * t + p : 6 + 3 * t + p] for p in range(3)], axis=0
        )

    short = jnp.concatenate([taps_of(t) * table_t[...] for t in range(3)], axis=1)
    short_bias = jnp.concatenate([own_par[:, 14 + p : 15 + p] for p in range(3)], axis=0)
    for i in range(LENGTH // 256):
        both = dot32(short, onehot[:, 256 * i : 256 * (i + 1)], 1, 0) + short_bias
        for h in range(2):
            for p in range(3):
                mix[p, 2 * i + h] = both[p * LOCAL : (p + 1) * LOCAL, 128 * h : 128 * (h + 1)]

    first_s, gated_s, second_s = v.first, v.gated, v.second
    mix_send, mix_recv = v.mix_send, v.mix_recv
    gm_send, gm_recv = v.gm_send, v.gm_recv

    def exchange(family, send, recv, g):
        at = tile(g, LANE_CH)

        def one(k):
            s = of_seq(k)
            push(family, send.at[s, at, :], recv.at[seq, at, :], dp, s, g)

        loop(1, PARTS, one)

    def exchanged(family, recv, g):
        arrived(family, recv.at[0 : PARTS - 1, 0:LANE_CH, :], g)

    def operator(g):
        at = tile(g, LANE_CH)
        skips = par_t[pl.ds(pl.multiple_of(seq * LOCAL + g * LANE_CH, LANE_CH), LANE_CH), :]
        skip0, skip1 = skips[:, 17:18], skips[:, 18:19]
        forth(0, [mix[2, a, at, :] for a in range(PARTS)])
        spec = dft(SPEC, 0)
        spec_v[g] = spec
        put_product(0, spec, spec_k1[g], False)
        signal = back(dft(SPEC, 2), 0)
        gated = []
        for a in range(PARTS):
            conv = signal[a] + skip0 * mix[2, a, at, :]
            first_s[a, at, :] = conv
            gate = mix[1, a, at, :] * conv
            gated_s[a, at, :] = gate
            gated.append(gate)
        forth(0, gated)
        spec = dft(SPEC, 0)
        spec_g[g] = spec
        put_product(0, spec, spec_k2[g], False)
        signal = back(dft(SPEC, 2), 0)
        for a in range(PARTS):
            conv = signal[a] + skip1 * gated_s[a, at, :]
            second_s[a, at, :] = conv
            mix_send[a, at, :] = (mix[0, a, at, :] * conv).astype(BF16)

        exchange(fam.mix, mix_send, mix_recv, g)

        @pl.when(g == 0)
        def _():
            gather_second(fam.outp, out_all.at[core], 1)

        @pl.when(g == 1)
        def _():
            gather_second(fam.seed, seed_all, 2 - core)

    gather_first(fam.seed, seed_all, 2 - core)
    loop(0, GROUPS, operator)
    arrived(fam.upz, up_all.at[0, 0], 0)
    to_line(fam.upz, up_all.at[core, z], up_all.at[core, z], beside, 1)
    to_line(fam.upz, up_all.at[core, across], up_all.at[core, across], beside, 1)
    to_twin(fam.upt, up_all.at[core, across])
    to_line(fam.down, own_down, own_down, across, 0)
    mix_recv[seq] = mix_send[seq]

    own_onehot = (id_rows == tok_v[...]).astype(F32)
    resid, unit2, inv2, n2_all = v.resid, v.unit2, v.inv2, v.n2_all
    resid[...] = dot32(own_onehot, embed, 0, 0) + par_v[19:20, :]
    arrived(fam.outp, out_all.at[0, 0:2], 1)

    def forward_out(k):
        q, _, _ = of_plane(k)
        to_twin(fam.outt, out_all.at[core, q])

    loop(1, 4, forward_out)
    w_up, w_out = v.w_up, v.w_out
    arrived(fam.outt, out_all.at[0])

    def place_out(i):
        q, zz = lax.div(i, 8) * 2 + lax.rem(i, 2), lax.rem(lax.div(i, 2), 4)
        both = jnp.concatenate(
            [out_all[0, q, zz].astype(F32), out_all[1, q, zz].astype(F32)], axis=0
        )
        w_out[tile(i, 48), :] = both.astype(BF16)

    loop(0, 16, place_out)
    for g in range(GROUPS):
        exchanged(fam.mix, mix_recv, g)


    to_line(fam.down, own_down, own_down, beside_across, 2)

    mixer_t = mix_recv[...].reshape(WIDTH, ROWS)
    residual = resid[...] + dot16(mixer_t, w_out[...], 0, 0)
    resid[...] = residual
    center = residual - jnp.mean(residual, axis=-1, keepdims=True)
    inv = lax.rsqrt(jnp.mean(center * center, axis=-1, keepdims=True) + epsilon)
    inv2[...] = inv
    unit = center * inv
    unit2[...] = unit
    n2_all[chip] = (unit * par_v[20:21, :] + par_v[21:22, :]).astype(BF16)

    def push_n2(k):
        q, d, s = of_plane(k)
        mine = n2_all.at[chip]
        push(fam.n2, mine, mine, d, s, chip)

    loop(1, 3, push_n2)

    arrived(fam.upz, up_all.at[0, 0:2], 1)
    to_twin(fam.upt, up_all.at[core, beside])
    to_twin(fam.upt, up_all.at[core, beside_across])
    arrived(fam.upt, up_all.at[0])

    def place_up(i):
        q, zz = lax.div(i, 8) * 2 + lax.rem(i, 2), lax.rem(lax.div(i, 2), 4)
        both = jnp.concatenate(
            [up_all[0, zz, q].astype(F32), up_all[1, zz, q].astype(F32)], axis=0
        )
        w_up[tile(i, 48), :] = both.astype(BF16)

    loop(0, 16, place_up)
    push_n2(3)
    for index, place in ((0, across), (1, beside), (2, beside_across)):
        arrived(fam.down, down_all.at[0, 0], index)
        to_twin(fam.downt, down_all.at[core, place])
    up_bias = jnp.zeros((1, SPLIT), F32)
    for q in range(4):
        cut = []
        for c in range(2):
            for zz in range(4):
                first = 96 * shard_of(q, c, zz)
                row, lane0 = first // WIDTH, first % WIDTH
                cut.append(par_v[23 + row : 24 + row, lane0 : lane0 + 96])
        up_bias = jnp.where(chip == q, jnp.concatenate(cut, axis=1), up_bias)

    act_all, gl_all, po_all, gn_all, slope = v.act_all, v.gl_all, v.po_all, v.gn_all, v.slope
    gn_recv, po_recv = v.gn_recv, v.po_recv

    def feed(k):
        q, _, _ = of_plane(k)

        @pl.when(k != 0)
        def _():
            arrived(fam.n2, n2_all.at[0], q)

        lifted = dot16(n2_all[q], w_up[...], 1, 0) + up_bias
        cdf = 0.5 * (1.0 + lax.erf(lifted * (1.0 / math.sqrt(2.0))))
        pdf = jnp.exp(-0.5 * lifted * lifted) * (1.0 / math.sqrt(2.0 * math.pi))
        act_all[q] = (lifted * cdf).astype(BF16)
        slope[q] = cdf + lifted * pdf

    loop(0, 4, feed)
    arrived(fam.seed, seed_all.at[0:2], 1)
    arrived(fam.downt, down_all.at[0])

    def feed_back(k, bias_sum):
        q, d, s = of_plane(lax.rem(k, 4))
        grad_act = dot16(seed_all[q], down_all[...].reshape(SPLIT, WIDTH), 1, 1)
        grad_lifted = grad_act * slope[q]
        gl_all[q] = grad_lifted.astype(BF16)
        gn_all[q] = dot16(gl_all[q], w_up[...], 1, 1).astype(BF16)

        @pl.when(k != 4)
        def _():
            push(fam.gn, gn_all.at[q], gn_recv.at[chip], d, s)

        return bias_sum + jnp.sum(grad_lifted, axis=0, keepdims=True)

    grad_up_bias = lax.fori_loop(1, 5, feed_back, jnp.zeros((1, SPLIT), F32))
    gn_recv[chip] = gn_all[chip]

    sd_x, sd_y, sd_t, sd_z = v.sd_x, v.sd_y, v.sd_t, v.sd_z
    su_x, su_y, su_t, su_z, su_p, su_r = v.su_x, v.su_y, v.su_t, v.su_z, v.su_p, v.su_r
    so_x, so_y, so_t, so_p, so_u, so_z = v.so_x, v.so_y, v.so_t, v.so_p, v.so_u, v.so_z
    acts = act_all[...].reshape(4 * ROWS, SPLIT)
    seeds = seed_all[...].reshape(4 * ROWS, WIDTH)
    for c in range(2):
        half = acts[:, c * 384 : (c + 1) * 384]
        sd_x[c] = dot16(half, seeds, 0, 0).astype(BF16).reshape(4, 96, WIDTH)
    to_twin(fam.sdt, sd_x.at[other_core], sd_y)
    units = n2_all[...].reshape(4 * ROWS, WIDTH)
    lows = gl_all[...].reshape(4 * ROWS, SPLIT)
    for x in range(2):
        part = dot16(units[:, x * 384 : (x + 1) * 384], lows, 0, 0)
        for i in range(16):
            su_x[i % 2, i // 4, x * 2 + (i // 2) % 2] = part[24 * i : 24 * (i + 1)].astype(BF16)
    to_twin(fam.sut, su_x.at[other_core], su_y)

    def add_sd(zz):
        sd_t[zz] = (sd_x[core, zz].astype(F32) + sd_y[zz].astype(F32)).astype(BF16)

    def add_su(zz):
        for q in range(4):
            su_t[zz, q] = (su_x[core, zz, q].astype(F32) + su_y[zz, q].astype(F32)).astype(BF16)

    def pair_first(family, sums, landing):
        to_line(family, sums.at[beside_across], landing.at[1], beside, 0)

    def pair_own(family, sums, landing):
        to_line(family, sums.at[beside], landing.at[0], beside, 2)

    def pair_second(family, sums, landing):
        arrived(family, landing.at[0], 0)
        sums[across] = (sums[across].astype(F32) + landing[1].astype(F32)).astype(BF16)
        to_line(family, sums.at[across], landing.at[2], across, 1)

    arrived(fam.sdt, sd_y)
    loop(0, 4, add_sd)
    pair_first(fam.sd, sd_t, sd_z)
    pair_own(fam.sd, sd_t, sd_z)
    arrived(fam.sut, su_y)
    loop(0, 4, add_su)
    pair_first(fam.su, su_t, su_z)


    def outputs_part(k):
        q, _, _ = of_plane(k)
        po_all[q] = dot16(act_all[q], down_all[...].reshape(SPLIT, WIDTH), 1, 0).astype(BF16)

    loop(0, 4, outputs_part)

    arrived(fam.gn, gn_all.at[0:3])
    grad_n2 = gn_recv[0].astype(F32)
    for q in range(1, 4):
        grad_n2 = grad_n2 + gn_recv[q].astype(F32)
    unit, inv = unit2[...], inv2[...]
    seed = seed_all[chip].astype(F32)
    scaled = grad_n2 * par_v[20:21, :]
    grad_res = seed + inv * (
        scaled
        - jnp.mean(scaled, axis=-1, keepdims=True)
        - unit * jnp.mean(scaled * unit, axis=-1, keepdims=True)
    )
    gres = v.gres
    gres[...] = grad_res.astype(BF16)
    gm_send[...] = dot16(w_out[...], gres[...], 1, 1).astype(BF16).reshape(PARTS, LOCAL, ROWS)
    loop(0, GROUPS, lambda g: exchange(fam.gm, gm_send, gm_recv, g))
    gm_recv[seq] = gm_send[seq]

    def sum_first(family, sums, landing, k):
        q, d, s = of_plane(k)
        push(family, sums.at[q], landing.at[0], d, s, 0)
        q, _, _ = of_plane(3)
        push(family, sums.at[q], landing.at[1], d, s, 0)

    def sum_second(family, sums, landing, k):
        arrived(family, landing.at[0:2], 0)
        q, d, s = of_plane(3 - k)
        sums[q] = (sums[q].astype(F32) + landing[1].astype(F32)).astype(BF16)
        push(family, sums.at[q], landing.at[2], d, s, 1)

    sum_first(fam.po, po_all, po_recv, 2 - core)
    b_x, b_y, b_p, b_t, b_z, b_f = v.b_x, v.b_y, v.b_p, v.b_t, v.b_z, v.b_f
    b_x[0:12, :] = dot32(own_onehot, grad_res, 1, 0)[0:12]
    b_x[12:13, :] = jnp.sum(grad_res, axis=0, keepdims=True)
    b_x[13:14, :] = jnp.sum(grad_n2 * unit, axis=0, keepdims=True)
    b_x[14:15, :] = jnp.sum(grad_n2, axis=0, keepdims=True)
    b_x[15:16, :] = jnp.sum(seed, axis=0, keepdims=True)
    for q in range(4):
        b_x[16 + q : 17 + q, :] = jnp.where(chip == q, grad_up_bias, 0.0)
    b_x[20:24, :] = jnp.zeros((4, WIDTH), F32)
    to_twin(fam.bt, b_x, b_y)
    for x in range(2):
        part = dot16(mixer_t[x * 384 : (x + 1) * 384], gres[...], 1, 0)
        for i in range(16):
            so_x[i % 2, x * 2 + (i // 2) % 2, i // 4] = part[24 * i : 24 * (i + 1)].astype(BF16)
    to_twin(fam.sot, so_x.at[other_core], so_y)

    def push_b(k):
        q, d, s = of_plane(k)
        mine = b_p.at[chip]
        push(fam.b, mine, mine, d, s)

    def add_so(zz):
        for q in range(4):
            so_t[q, zz] = (so_x[core, q, zz].astype(F32) + so_y[q, zz].astype(F32)).astype(BF16)

    grad_mix, raw, q_s = v.grad_mix, v.raw, v.q_s

    def operator_back(g):
        at = tile(g, LANE_CH)
        skips = par_t[pl.ds(pl.multiple_of(seq * LOCAL + g * LANE_CH, LANE_CH), LANE_CH), :]
        skip0, skip1 = skips[:, 17:18], skips[:, 18:19]
        decay = decay_of(g)

        def rows_at(first, count=LANE_CH):
            return pl.ds(pl.multiple_of(first + g * LANE_CH, LANE_CH), count)

        seconds, total = [], jnp.zeros((LANE_CH, ROWS), F32)
        for a in range(PARTS):
            upstream = gm_recv[a, at, :].astype(F32)
            lanes = slice(a * ROWS, (a + 1) * ROWS)
            grad_mix[rows_at(0), lanes] = upstream * second_s[a, at, :]
            grad_second = upstream * mix[0, a, at, :]
            total = total + grad_second * gated_s[a, at, :]
            seconds.append(grad_second)
        q_s[rows_at(0), 49:50] = jnp.sum(total, axis=1, keepdims=True)
        forth(0, seconds)
        spec = dft(SPEC, 0)
        put_product(0, spec, spec_k2[g], True)
        put_product(SPEC, spec, spec_g[g], True)
        turned = dft(2 * SPEC, 2)
        signal = back(turned, 0)
        cross = back(turned, SPEC)
        firsts, total = [], jnp.zeros((LANE_CH, ROWS), F32)
        for a in range(PARTS):
            lanes = slice(a * ROWS, (a + 1) * ROWS)
            raw[rows_at(LOCAL), lanes] = cross[a] * decay(a)
            grad_second = gm_recv[a, at, :].astype(F32) * mix[0, a, at, :]
            grad_gated = skip1 * grad_second + signal[a]
            grad_mix[rows_at(LOCAL), lanes] = grad_gated * first_s[a, at, :]
            grad_first = grad_gated * mix[1, a, at, :]
            total = total + grad_first * mix[2, a, at, :]
            grad_mix[rows_at(2 * LOCAL), lanes] = skip0 * grad_first
            firsts.append(grad_first)
        q_s[rows_at(0), 48:49] = jnp.sum(total, axis=1, keepdims=True)
        forth(0, firsts)
        spec = dft(SPEC, 0)
        put_product(0, spec, spec_k1[g], True)
        put_product(SPEC, spec, spec_v[g], True)
        turned = dft(2 * SPEC, 2)
        signal = back(turned, 0)
        cross = back(turned, SPEC)
        for a in range(PARTS):
            lanes = slice(a * ROWS, (a + 1) * ROWS)
            raw[rows_at(0), lanes] = cross[a] * decay(a)
            grad_mix[rows_at(2 * LOCAL), lanes] = grad_mix[rows_at(2 * LOCAL), lanes] + signal[a]

    def sums_of_rows():
        arrived(fam.bt, b_y)
        for c in range(2):

            @pl.when(core == c)
            def _():
                at = slice(c * 384, (c + 1) * 384)
                b_p[chip] = b_x[:, at] + b_y[:, at]

        loop(1, 4, push_b)

    def group_back(g):
        exchanged(fam.gm, gm_recv, g)

        @pl.when(g == 0)
        def _():
            pair_second(fam.su, su_t, su_z)
            arrived(fam.sot, so_y)
            loop(0, 4, add_so)
            sum_first(fam.so, so_t, so_p, 2)

        operator_back(g)

        @pl.when(g == 0)
        def _():
            sums_of_rows()
            pair_second(fam.sd, sd_t, sd_z)
            pair_own(fam.su, su_t, su_z)

    loop(0, GROUPS, group_back)
    sum_second(fam.po, po_all, po_recv, 2 - core)

    zx_send, zx_recv, z_send, z_recv = v.zx_send, v.zx_recv, v.z_send, v.z_recv
    by_id = dot32(grad_mix[...], onehot[...], 1, 1)
    sums = sum(taps_of(t) * by_id[:, t * IDS : (t + 1) * IDS] for t in range(3))
    taps_grad = [
        jnp.sum(table_t[...] * by_id[:, t * IDS : (t + 1) * IDS], axis=1, keepdims=True)
        for t in range(3)
    ]
    bias_grad = jnp.sum(by_id[:, 2 * IDS : 3 * IDS], axis=1, keepdims=True)
    columns = jnp.concatenate([sums[:, 0:12]] + taps_grad + [bias_grad], axis=1)
    skip_cols = jnp.concatenate(
        [q_s[:, 48:50], jnp.zeros((LOCAL, 14), F32)], axis=1
    )
    zx_send[...] = jnp.concatenate(
        [columns, skip_cols, jnp.zeros((64, IDS), F32)], axis=0
    ).T
    push(fam.zx, zx_send, zx_recv, other_dp, seq)
    sum_second(fam.so, so_t, so_p, 2)

    f_send, f_recv, m_send, m_recv, m2_send, m2_recv = (v.f_send, v.f_recv, v.m_send, v.m_recv, v.m2_send, v.m2_recv)
    grad_filter = dot32(raw[...], act2[...], 1, 1)
    f_send[...] = grad_filter
    there = f_send.at[tile(other_dp, LOCAL), :]
    push(fam.f, there, f_recv, other_dp, seq)
    grad_second_pre = dot32(filt, raw[...], 0, 0) * cos2[...]
    grad_inner = dot32(act1[...], grad_second_pre, 1, 1)
    grad_first_pre = dot32(inner, grad_second_pre, 1, 0) * cos1[...]
    grad_freq = dot32(feats_v[...], grad_first_pre, 1, 1)
    m_send[...] = jnp.concatenate(
        [
            jnp.concatenate([grad_freq, jnp.zeros((40, 64), F32)], axis=0),
            jnp.concatenate([grad_inner, jnp.zeros((8, 64), F32)], axis=0),
        ],
        axis=1,
    ).astype(BF16)
    j_me = dp * 4 + yc
    m_recv[j_me] = m_send[...]

    def push_m(k):
        j, d, s = of_eight(k)
        push(fam.m, m_send, m_recv.at[j_me], d, s)

    loop(1, 8, push_m)

    arrived(fam.zx, zx_recv)
    z_send[...] = (zx_send[...] + zx_recv[...]).astype(BF16)
    z_recv[seq] = z_send[...]

    def push_z(k):
        s = of_seq(k)
        push(fam.z, z_send, z_recv.at[seq], dp, s)

    loop(1, PARTS, push_z)
    arrived(fam.su, su_z.at[2], 1)
    arrived(fam.su, su_z.at[0], 2)
    for q in range(4):
        part = su_t[z, q].astype(F32) + su_z[0, q].astype(F32) + su_z[2, q].astype(F32)
        su_p[q] = part.astype(BF16)
    su_r[chip] = su_p[chip]

    def push_su2(k):
        q, d, s = of_plane(k)
        push(fam.su2, su_p.at[q], su_r.at[chip], d, s)

    loop(1, 4, push_su2)
    arrived(fam.m, m_recv.at[0:7])
    totals = m_recv[0].astype(F32)
    for j in range(1, 8):
        totals = totals + m_recv[j].astype(F32)
    m2_send[...] = totals.astype(BF16)
    m2_recv[z] = m2_send[...]

    def push_m2(k):
        zz, s = of_line(k)
        push(fam.m2, m2_send, m2_recv.at[z], dp, s)

    loop(1, 4, push_m2)


    arrived(fam.b, b_p.at[0:3])
    b_t[...] = (b_p[0] + b_p[1]) + (b_p[2] + b_p[3])
    b_z[z] = b_t[...]

    def push_b2(k):
        zz, s = of_line(k)
        push(fam.b2, b_t, b_z.at[z], dp, s)

    loop(1, 4, push_b2)
    arrived(fam.so, so_p.at[0], 1)
    for zz in range(4):
        part = so_t[chip, zz].astype(F32) + so_p[0, zz].astype(F32) + so_p[2, zz].astype(F32)
        so_u[zz] = part.astype(BF16)
    so_z[z] = so_u[z]

    def push_so2(k):
        zz, s = of_line(k)
        push(fam.so2, so_u.at[zz], so_z.at[z], dp, s)

    loop(1, 4, push_so2)

    wide, gt_all = v.wide, v.gt_all
    arrived(fam.z, z_recv.at[0 : PARTS - 1])
    for p in range(4):
        for i in range(PARTS):
            wide[:, p * WIDTH + i * LOCAL : p * WIDTH + (i + 1) * LOCAL] = z_recv[i][
                :, p * LOCAL : (p + 1) * LOCAL
            ].astype(F32)
    by_ids = jnp.where(
        lax.broadcasted_iota(jnp.int32, (IDS, 3 * WIDTH), 0) < 12, wide[:, 0 : 3 * WIDTH], 0.0
    )
    own_gt = dot32(in_low, by_ids, 1, 1)
    gt_all[me] = jnp.concatenate(
        [own_gt[8 * t : 8 * (t + 1)] for t in range(3)] + [jnp.zeros((8, 80), F32)], axis=1
    )

    def push_gt(k):
        _, d, s = everyone(k)
        mine = gt_all.at[me]
        push(fam.gt, mine, mine, d, s)

    loop(1, 2 * PARTS, push_gt)

    stores = []

    def store(source, target):
        copy = pltpu.make_async_copy(source, target, sem_o.at[len(stores)])
        copy.start()
        stores.append(copy)

    o_in, o_wide, o_rows = v.o_in, v.o_wide, v.o_rows
    o_in[...] = dot32(normed_t[tile(me, 24), :], by_ids, 1, 0)
    o_wide[...] = jnp.sum(by_ids, axis=0, keepdims=True)
    o_rows[2:4, :] = wide[0:2, 3 * WIDTH :]
    store(o_in, out.in_weight)
    store(o_wide.at[0], out.in_bias)
    store(wide.at[12:15, 0 : 3 * WIDTH], out.short_taps)
    store(wide.at[15, pl.ds(0, 3 * WIDTH)], out.short_bias)
    store(o_rows.at[2:4, :], out.skip_scale)

    arrived(fam.po, po_recv.at[0], 1)
    block = resid[...] + par_v[22:23, :] + po_all[chip].astype(F32)
    block = block + po_recv[0].astype(F32) + po_recv[2].astype(F32)
    resid[...] = block
    store(resid, out.block)

    arrived(fam.sd, sd_z.at[2], 1)
    arrived(fam.sd, sd_z.at[0], 2)
    part = sd_t[z].astype(F32) + sd_z[0].astype(F32) + sd_z[2].astype(F32)
    downw_v[...] = part
    store(downw_v, out.down_weight)
    arrived(fam.f, f_recv)
    f_recv[...] = f_send[tile(dp, LOCAL), :] + f_recv[...]
    store(f_recv, out.filter_weight)

    arrived(fam.su2, su_r.at[0:3])
    for q in range(4):
        part = su_r[q].astype(F32)
        for c in range(2):
            for zz in range(4):
                first, place = 96 * shard_of(q, c, zz), 384 * c + 96 * zz
                upw_v[:, first : first + 96] = part[:, place : place + 96]
    store(upw_v, out.up_weight)

    arrived(fam.b2, b_z.at[0:3])
    b_f[core] = (b_z[0] + b_z[1]) + (b_z[2] + b_z[3])
    to_twin(fam.bf, b_f.at[core])
    arrived(fam.so2, so_z.at[0:3])
    part = so_z[0].astype(F32)
    for zz in range(1, 4):
        part = part + so_z[zz].astype(F32)
    outw_v[...] = part
    store(outw_v, out.out_weight)
    arrived(fam.m2, m2_recv.at[0:3])
    totals = m2_recv[0].astype(F32)
    for zz in range(1, 4):
        totals = totals + m2_recv[zz].astype(F32)
    mlp_v[0:40, :] = totals[0:40, 0:64]
    mlp_v[40:112, :] = totals[0:72, 64:128]
    store(mlp_v.at[0:33, :], out.freq_weight)
    store(mlp_v.at[33], out.freq_bias)
    store(mlp_v.at[40:104, :], out.inner_weight)
    store(mlp_v.at[104], out.inner_bias)
    arrived(fam.bf, b_f.at[0])
    totals = jnp.concatenate([b_f[0], b_f[1]], axis=1)
    o_rows[4:8, :] = totals[12:16]
    o_up = v.o_up
    for q in range(4):
        for c in range(2):
            for zz in range(4):
                first, place = 96 * shard_of(q, c, zz), 384 * c + 96 * zz
                o_up[:, first : first + 96] = totals[16 + q : 17 + q, place : place + 96]
    store(o_rows.at[4], out.out_bias)
    store(o_rows.at[5], out.gain_two)
    store(o_rows.at[6], out.bias_two)
    store(o_rows.at[7], out.down_bias)
    store(o_up.at[0], out.up_bias)

    arrived(fam.gt, gt_all.at[0 : 2 * PARTS - 1])
    gts = gt_all[...]
    grad_normed = jnp.concatenate([gts[:, :, IDS * t : IDS * (t + 1)] for t in range(3)], axis=1)
    grad_normed = grad_normed.reshape(WIDTH, IDS).T
    o_rows[0:1, :] = jnp.sum(grad_normed * unit_one, axis=0, keepdims=True)
    o_rows[1:2, :] = jnp.sum(grad_normed, axis=0, keepdims=True)
    scaled = grad_normed * par_v[0:1, :]
    grad_embed = inverse_one * (
        scaled
        - jnp.mean(scaled, axis=-1, keepdims=True)
        - unit_one * jnp.mean(scaled * unit_one, axis=-1, keepdims=True)
    )
    emb_v[...] = totals[0:12] + grad_embed[0:12]
    store(o_rows.at[0], out.gain_one)
    store(o_rows.at[1], out.bias_one)
    store(emb_v, out.embed_table)

    for family, ref in (
        (fam.p, p_send.at[0 : PARTS - 1]), (fam.tok, tok_all.at[0 : PARTS - 1]), (fam.filt, filt_all.at[0]),
        (fam.px, px_send), (fam.outz, out_all.at[0, 0, 0:3]), (fam.outp, out_all.at[0, 0:3]),
        (fam.outt, out_all.at[0]), (fam.up, up_send.at[0:3]), (fam.upz, up_all.at[0, 0:3]),
        (fam.upt, up_all.at[0]), (fam.seed, seed_all.at[0:3]), (fam.down, down_all.at[0, 0:3]),
        (fam.downt, down_all.at[0]), (fam.mix, mix_send.at[0 : PARTS - 1]),
        (fam.gm, gm_send.at[0 : PARTS - 1]), (fam.n2, n2_all.at[0:3]), (fam.gn, gn_all.at[0:3]),
        (fam.po, po_all.at[0:3]), (fam.sdt, sd_y), (fam.sut, su_y), (fam.sot, so_y), (fam.sd, sd_t.at[0:3]),
        (fam.su, su_t.at[0:3]), (fam.su2, su_p.at[0:3]), (fam.so, so_t.at[0:3]), (fam.so2, so_u.at[0:3]),
        (fam.bt, b_x), (fam.b, b_p.at[0:3]), (fam.b2, b_z.at[0:3]), (fam.bf, b_f.at[0]),
        (fam.m, m_recv.at[0:7]), (fam.m2, m2_recv.at[0:3]), (fam.z, z_recv.at[0 : PARTS - 1]),
        (fam.zx, zx_send), (fam.f, f_recv), (fam.gt, gt_all.at[0 : 2 * PARTS - 1]),
    ):
        wait_for(ref, s_of(family))
    for copy in stores:
        copy.wait()


def copy_kernel(*refs):
    count = len(OUTPUTS)
    for source, target in zip(refs[:count], refs[count:]):
        target[...] = source[...]


FAMILIES = dict(
    p=1, tok=1, filt=1, px=1, outz=1, outp=2, outt=1, up=1, upz=2, upt=1, down=3, downt=1, seed=2, mix=3,
    gm=3, n2=4, gn=1, po=2, sdt=1, sd=3, sut=1, su=3, su2=1, sot=1, so=2, so2=1, bt=1, b=1, b2=1, bf=1,
    m=1, m2=1, z=1, zx=1, f=1, gt=1,
)
LOADS = 18
INPUTS = dict(
    token_ids=0, embed_table=0, gain_one=0, bias_one=0, in_weight=0, in_bias=0, short_taps=0, short_bias=0,
    freq_weight=0, freq_bias=0, inner_weight=0, inner_bias=0, filter_weight=0, skip_scale=0, out_weight=0,
    out_bias=0, gain_two=0, bias_two=0, up_weight=0, up_bias=0, down_weight=0, down_bias=0, cotangent=0,
    mats=0, twist=0, feats=0,
)
OUTPUTS = dict(
    block=(ROWS, WIDTH), embed_table=(12, WIDTH), gain_one=(WIDTH,),
    bias_one=(WIDTH,), in_weight=(24, 3 * WIDTH), in_bias=(3 * WIDTH,),
    short_taps=(3, 3 * WIDTH), short_bias=(3 * WIDTH,), freq_weight=(33, 64),
    freq_bias=(64,), inner_weight=(64, 64), inner_bias=(64,),
    filter_weight=(LOCAL, 64), skip_scale=(2, WIDTH), out_weight=(24, WIDTH),
    out_bias=(WIDTH,), gain_two=(WIDTH,), bias_two=(WIDTH,),
    up_weight=(24, HIDDEN), up_bias=(HIDDEN,), down_weight=(96, WIDTH),
    down_bias=(WIDTH,),
)
SPECTRUM = (GROUPS, SPEC, 2 * ROWS)
SCRATCH = dict(
    tok=((1, ROWS), jnp.int32), emb=((12, WIDTH), F32), par=((32, WIDTH), F32),
    inw=((24, 3 * WIDTH), F32), mlp=((112, 64), F32), filt=((LOCAL, 64), F32),
    outw=((24, WIDTH), F32), upw=((24, HIDDEN), F32), downw=((96, WIDTH), F32),
    mats=((4, 256, 256), BF16), twist=((72, ROWS), F32), feats=((40, LENGTH), F32),
    normed_t=((WIDTH, IDS), F32), p_send=((PARTS, IDS, 256), BF16),
    p_recv=((PARTS, IDS, 256), BF16), px_send=((IDS, 256), F32), px_recv=((IDS, 256), F32),
    filt_all=((2, LOCAL, 64), BF16), tok_all=((PARTS, 1, ROWS), jnp.int32),
    up_send=((4, 24, SPLIT), BF16), up_all=((2, 4, 4, 24, SPLIT), BF16),
    out_all=((2, 4, 4, 24, WIDTH), BF16), seed_all=((4, ROWS, WIDTH), BF16),
    down_all=((2, 4, 96, WIDTH), BF16), w_up=((WIDTH, SPLIT), BF16), w_out=((WIDTH, WIDTH), BF16),
    act1=((72, LENGTH), F32), cos1=((64, LENGTH), F32), act2=((64, LENGTH), F32),
    cos2=((64, LENGTH), F32), kern=((2, PARTS, LOCAL, ROWS), F32), par_t=((WIDTH, 32), F32),
    table_t=((3 * LOCAL, IDS), F32), onehot=((3 * IDS, LENGTH), F32),
    mix=((3, PARTS, LOCAL, ROWS), F32),
    hi=((2 * SPEC, 2 * ROWS), BF16), lo=((2 * SPEC, 2 * ROWS), BF16),
    spec_k1=(SPECTRUM, F32), spec_k2=(SPECTRUM, F32), spec_v=(SPECTRUM, F32),
    spec_g=(SPECTRUM, F32),
    first=((PARTS, LOCAL, ROWS), F32), gated=((PARTS, LOCAL, ROWS), F32),
    second=((PARTS, LOCAL, ROWS), F32),
    mix_send=((PARTS, LOCAL, ROWS), BF16), mix_recv=((PARTS, LOCAL, ROWS), BF16),
    gm_send=((PARTS, LOCAL, ROWS), BF16), gm_recv=((PARTS, LOCAL, ROWS), BF16),
    resid=((ROWS, WIDTH), F32), unit2=((ROWS, WIDTH), F32), inv2=((ROWS, 1), F32),
    n2_all=((4, ROWS, WIDTH), BF16), act_all=((4, ROWS, SPLIT), BF16),
    gl_all=((4, ROWS, SPLIT), BF16), slope=((4, ROWS, SPLIT), F32), po_all=((4, ROWS, WIDTH), BF16),
    po_recv=((3, ROWS, WIDTH), BF16), gn_all=((4, ROWS, WIDTH), BF16),
    gn_recv=((4, ROWS, WIDTH), BF16), gres=((ROWS, WIDTH), BF16),
    sd_x=((2, 4, 96, WIDTH), BF16), sd_y=((4, 96, WIDTH), BF16), sd_t=((4, 96, WIDTH), BF16),
    sd_z=((3, 96, WIDTH), BF16),
    su_x=((2, 4, 4, 24, SPLIT), BF16), su_y=((4, 4, 24, SPLIT), BF16),
    su_t=((4, 4, 24, SPLIT), BF16), su_z=((3, 4, 24, SPLIT), BF16), su_p=((4, 24, SPLIT), BF16),
    su_r=((4, 24, SPLIT), BF16),
    so_x=((2, 4, 4, 24, WIDTH), BF16), so_y=((4, 4, 24, WIDTH), BF16),
    so_t=((4, 4, 24, WIDTH), BF16), so_p=((3, 4, 24, WIDTH), BF16), so_u=((4, 24, WIDTH), BF16),
    so_z=((4, 24, WIDTH), BF16),
    b_x=((24, WIDTH), F32), b_y=((24, WIDTH), F32), b_p=((4, 24, 384), F32),
    b_t=((24, 384), F32), b_z=((4, 24, 384), F32), b_f=((2, 24, 384), F32),
    grad_mix=((3 * LOCAL, LENGTH), F32), raw=((2 * LOCAL, LENGTH), F32), q_s=((LOCAL, 128), F32),
    z_send=((IDS, 256), BF16), z_recv=((PARTS, IDS, 256), BF16), zx_send=((IDS, 256), F32),
    zx_recv=((IDS, 256), F32), wide=((IDS, 4 * WIDTH), F32), gt_all=((32, 8, 128), F32),
    m_send=((80, 128), BF16), m_recv=((8, 80, 128), BF16), m2_send=((80, 128), BF16),
    m2_recv=((4, 80, 128), BF16), f_send=((2 * LOCAL, 64), F32), f_recv=((LOCAL, 64), F32),
    o_in=((24, 3 * WIDTH), F32), o_wide=((1, 3 * WIDTH), F32), o_rows=((8, WIDTH), F32),
    o_up=((1, HIDDEN), F32),
)


def fits(mesh_shape, args):
    return (
        mesh_shape["dp"] == 2
        and mesh_shape["seq"] == PARTS
        and args[0].shape == (1, ROWS)
        and args[1].shape == (12, WIDTH)
        and args[4].shape == (24, 3 * WIDTH)
        and args[8].shape == (33, 64)
        and args[18].shape == (24, HIDDEN)
    )


def fast_device(*args):
    given = SimpleNamespace(**dict(zip(INPUTS, args)))
    tables = tables_of(given.freq_weight.shape[0])
    given.mats, given.twist, given.feats = (jnp.asarray(table) for table in tables)
    given.cotangent = given.cotangent[0]
    anywhere, near = (pl.BlockSpec(memory_space=space) for space in (pl.ANY, pltpu.VMEM))
    shapes = [jax.ShapeDtypeStruct(shape, F32) for shape in OUTPUTS.values()]
    counts = (len(FAMILIES), sum(FAMILIES.values()), LOADS + 1, len(shapes))
    made = pl.pallas_call(
        step_kernel,
        out_shape=shapes,
        in_specs=[anywhere] * len(INPUTS),
        out_specs=[anywhere] * len(shapes),
        scratch_shapes=[pltpu.VMEM(shape, kind) for shape, kind in SCRATCH.values()]
        + [pltpu.SemaphoreType.DMA((count,)) for count in counts],
        compiler_params=pltpu.CompilerParams(
            collective_id=0, has_side_effects=True, vmem_limit_bytes=60 * 1024 * 1024
        ),
    )(*(getattr(given, name) for name in INPUTS))
    made = pl.pallas_call(
        copy_kernel,
        out_shape=shapes,
        in_specs=[near] * len(shapes),
        out_specs=[near] * len(shapes),
    )(*made)
    return (made[0][None], *made[1:])


def solution(mesh):
    in_specs = (
        P("dp", "seq"),
        P(),
        P(),
        P(),
        P(("dp", "seq"), None),
        P(),
        P(),
        P(),
        P(),
        P(),
        P(),
        P(),
        P(("dp", "seq"), None),
        P(),
        P(("dp", "seq"), None),
        P(),
        P(),
        P(),
        P(("dp", "seq"), None),
        P(),
        P(("dp", "seq"), None),
        P(),
        P("dp", "seq", None),
    )
    out_specs = (
        P("dp", "seq", None),
        P(),
        P(),
        P(),
        P(("dp", "seq"), None),
        P(),
        P(),
        P(),
        P(),
        P(),
        P(),
        P(),
        P(("dp", "seq"), None),
        P(),
        P(("dp", "seq"), None),
        P(),
        P(),
        P(),
        P(("dp", "seq"), None),
        P(),
        P(("dp", "seq"), None),
        P(),
    )

    def either(*args):
        return (fast_device if fits(mesh.shape, args) else per_device)(*args)

    return jax.shard_map(
        either, mesh=mesh, in_specs=in_specs, out_specs=out_specs, check_vma=False
    )
```

```python
import math
from types import SimpleNamespace

import jax
import jax.numpy as jnp
import ml_dtypes
import numpy as np
from jax import lax
from jax.experimental import pallas as pl
from jax.experimental.pallas import tpu as pltpu
from jax.sharding import PartitionSpec as P

epsilon = 1e-05
slow_rate = -math.log(0.01) / 1.5
fast_rate = -math.log(0.01) / 0.3
decay_shift = 0.05
highest = lax.Precision.HIGHEST


def exact_dot(left_side, right_side):
    return jnp.dot(left_side, right_side, precision=highest, preferred_element_type=jnp.float32)


def narrow_dot(left_side, right_side):
    return jnp.dot(left_side, right_side, preferred_element_type=jnp.float32)


def rows_inner(left_side, right_side, accuracy=None):
    return lax.dot_general(
        left_side,
        right_side,
        (((0,), (0,)), ((), ())),
        precision=accuracy,
        preferred_element_type=jnp.float32,
    )


def against_rows(left_side, right_side, accuracy=None):
    return lax.dot_general(
        left_side,
        right_side,
        (((1,), (1,)), ((), ())),
        precision=accuracy,
        preferred_element_type=jnp.float32,
    )


def normalize(values):
    center = values - jnp.mean(values, axis=-1, keepdims=True)
    inverse = lax.rsqrt(jnp.mean(center * center, axis=-1, keepdims=True) + epsilon)
    return (center * inverse, inverse)


def norm_back(upstream, unit_vals, inverse):
    return inverse * (
        upstream
        - jnp.mean(upstream, axis=-1, keepdims=True)
        - unit_vals * jnp.mean(upstream * unit_vals, axis=-1, keepdims=True)
    )


def angle_table(row_count, column_count, modulus):
    product = (
        jnp.arange(row_count, dtype=jnp.int32)[:, None]
        * jnp.arange(column_count, dtype=jnp.int32)[None, :]
        % modulus
    )
    angles = 2.0 * math.pi / modulus * product.astype(jnp.float32)
    return (jnp.cos(angles), jnp.sin(angles))


def forward_transform(signal, tables):
    cos_section, sin_section, cos_twist, sin_twist, cos_last, sin_last = tables
    real_first = jnp.einsum("kn,...nm->...km", cos_section, signal, precision=highest)
    imag_first = -jnp.einsum("kn,...nm->...km", sin_section, signal, precision=highest)
    real_turn = real_first * cos_twist + imag_first * sin_twist
    imag_turn = imag_first * cos_twist - real_first * sin_twist
    real_out = exact_dot(real_turn, cos_last) + exact_dot(imag_turn, sin_last)
    imag_out = exact_dot(imag_turn, cos_last) - exact_dot(real_turn, sin_last)
    return (real_out, imag_out)


def inverse_transform(real_spec, imag_spec, tables):
    cos_section, sin_section, cos_twist, sin_twist, cos_last, sin_last = tables
    real_turn = exact_dot(real_spec, cos_last) - exact_dot(imag_spec, sin_last)
    imag_turn = exact_dot(imag_spec, cos_last) + exact_dot(real_spec, sin_last)
    real_first = real_turn * cos_twist - imag_turn * sin_twist
    imag_first = imag_turn * cos_twist + real_turn * sin_twist
    signal = jnp.einsum("kn,...km->...nm", cos_section, real_first, precision=highest) - jnp.einsum(
        "kn,...km->...nm", sin_section, imag_first, precision=highest
    )
    return signal / (cos_twist.shape[0] * cos_twist.shape[1])


def multiply(real_one, imag_one, real_two, imag_two):
    return (real_one * real_two - imag_one * imag_two, real_one * imag_two + imag_one * real_two)


def multiply_conj(real_one, imag_one, real_two, imag_two):
    return (real_one * real_two + imag_one * imag_two, imag_one * real_two - real_one * imag_two)


def to_channels(rows_in):
    return lax.all_to_all(rows_in.T, "seq", split_axis=0, concat_axis=1, tiled=True)


def to_rows(columns):
    return lax.all_to_all(columns, "seq", split_axis=1, concat_axis=0, tiled=True).T


def gather_all(pieces):
    shapes = [piece.shape for piece in pieces]
    flat = jnp.concatenate([piece.astype(jnp.bfloat16).reshape(-1) for piece in pieces])
    whole = lax.all_gather(flat, ("dp", "seq"), axis=0, tiled=False)
    result, start = [], 0
    for shape in shapes:
        size = math.prod(shape)
        result.append(whole[:, start : start + size].reshape((-1,) + shape[1:]))
        start += size
    return result


def per_device(
    token_ids,
    embed_table,
    gain_one,
    bias_one,
    in_weight,
    in_bias,
    short_taps,
    short_bias,
    freq_weight,
    freq_bias,
    inner_weight,
    inner_bias,
    filter_weight,
    skip_scale,
    out_weight,
    out_bias,
    gain_two,
    bias_two,
    up_weight,
    up_bias,
    down_weight,
    down_bias,
    cotangent,
):
    tokens = token_ids[0]
    row_count = tokens.shape[0]
    vocab, model_width = embed_table.shape
    seq_parts = lax.axis_size("seq")
    seq_index = lax.axis_index("seq")
    dp_index = lax.axis_index("dp")
    local_width = model_width // seq_parts
    length = row_count * seq_parts
    freq_rows = 2 * seq_parts
    low_rows = seq_index * local_width

    def own_channels(table):
        parts = table.reshape(table.shape[0], -1, model_width)
        return lax.dynamic_slice_in_dim(parts, low_rows, local_width, 2)

    in_full, out_full, up_full, down_full, filter_full, tokens_full = gather_all(
        (in_weight, out_weight, up_weight, down_weight, filter_weight, token_ids)
    )
    sequence = lax.dynamic_slice_in_dim(
        tokens_full.reshape(-1, length), dp_index, 1, 0
    )[0].astype(jnp.int32)
    cos_section, sin_section = angle_table(freq_rows, seq_parts, freq_rows)
    cos_twist, sin_twist = angle_table(freq_rows, row_count, freq_rows * row_count)
    cos_last, sin_last = angle_table(row_count, row_count, row_count)
    tables = (cos_section, sin_section, cos_twist, sin_twist, cos_last, sin_last)

    unit_one, inverse_one = normalize(embed_table)
    normed = (unit_one * gain_one + bias_one).astype(jnp.bfloat16)
    table = narrow_dot(normed, in_full) + in_bias
    local_table = own_channels(table)
    local_taps = own_channels(short_taps)
    local_bias = own_channels(short_bias[None])[0]
    local_skip = own_channels(skip_scale)[:, 0, :, None]
    ids = jnp.arange(vocab, dtype=jnp.int32)[:, None]
    padded = jnp.concatenate([jnp.full((2,), -1, jnp.int32), sequence])
    shifted = jnp.concatenate(
        [(padded[None, j : j + length] == ids).astype(jnp.float32) for j in range(3)], axis=0
    )
    weights = (local_taps[:, None] * local_table[None]).reshape(3 * vocab, 3 * local_width)
    mixed = rows_inner(weights, shifted, highest) + local_bias.reshape(-1, 1)
    gate_outer = mixed[:local_width]
    gate_inner = mixed[local_width : 2 * local_width]
    value_part = mixed[2 * local_width :]

    count = (freq_weight.shape[0] - 1) // 2
    position_phase = jnp.arange(length, dtype=jnp.float32) / length
    levels = 0.0001 + jnp.arange(count, dtype=jnp.float32) * ((count - 1 - 0.0001) / (count - 1))
    angles = 2.0 * math.pi * position_phase[None, :] * levels[:, None]
    features = jnp.concatenate([position_phase[None, :], jnp.cos(angles), -jnp.sin(angles)], axis=0)
    first_pre = rows_inner(freq_weight, features, highest) + freq_bias[:, None]
    first_act = jnp.sin(first_pre)
    second_pre = rows_inner(inner_weight, first_act, highest) + inner_bias[:, None]
    second_act = jnp.sin(second_pre)
    channel = (low_rows + jnp.arange(local_width, dtype=jnp.int32)).astype(jnp.float32) / (
        model_width - 1
    )
    decay_rate = slow_rate + (fast_rate - slow_rate) * channel
    decay = jnp.exp(-position_phase[None, :] * decay_rate[:, None]) + decay_shift
    local_filter = lax.dynamic_slice_in_dim(
        filter_full.reshape(2, model_width, -1), low_rows, local_width, 1
    ).astype(jnp.float32).reshape(2 * local_width, -1)
    kernels = exact_dot(local_filter, second_act).reshape(2, local_width, length) * decay

    def forth(signal):
        shape = signal.shape[:-1] + (seq_parts, row_count)
        return forward_transform(signal.reshape(shape), tables)

    def back(real_spec, imag_spec):
        result = inverse_transform(real_spec, imag_spec, tables)
        return result.reshape(result.shape[:-2] + (length,))

    kernel_real, kernel_imag = forth(kernels)
    value_real, value_imag = forth(value_part)
    first_conv = (
        back(*multiply(value_real, value_imag, kernel_real[0], kernel_imag[0]))
        + local_skip[0] * value_part
    )
    gated = gate_inner * first_conv
    gated_real, gated_imag = forth(gated)
    second_conv = (
        back(*multiply(gated_real, gated_imag, kernel_real[1], kernel_imag[1]))
        + local_skip[1] * gated
    )
    mixer = to_rows((gate_outer * second_conv).astype(jnp.bfloat16))

    onehot = (tokens[:, None] == ids[:, 0][None, :]).astype(jnp.float32)
    hidden = exact_dot(onehot, embed_table)
    residual = hidden + narrow_dot(mixer, out_full) + out_bias
    unit_two, inverse_two = normalize(residual)
    normed_two = (unit_two * gain_two + bias_two).astype(jnp.bfloat16)
    lifted = narrow_dot(normed_two, up_full) + up_bias
    normal_cdf = 0.5 * (1.0 + lax.erf(lifted * (1.0 / math.sqrt(2.0))))
    activated = (lifted * normal_cdf).astype(jnp.bfloat16)
    block_out = residual + narrow_dot(activated, down_full) + down_bias
    seed_low = cotangent[0]
    seed = seed_low.astype(jnp.float32)
    grad_down_bias = jnp.sum(seed, axis=0)
    grad_down = rows_inner(activated, seed_low)
    grad_activated = against_rows(seed_low, down_full)
    normal_pdf = jnp.exp(-0.5 * lifted * lifted) * (1.0 / math.sqrt(2.0 * math.pi))
    grad_lifted = grad_activated * (normal_cdf + lifted * normal_pdf)
    grad_up_bias = jnp.sum(grad_lifted, axis=0)
    lifted_low = grad_lifted.astype(jnp.bfloat16)
    grad_up = rows_inner(normed_two, lifted_low)
    grad_normed_two = against_rows(lifted_low, up_full)
    grad_gain_two = jnp.sum(grad_normed_two * unit_two, axis=0)
    grad_bias_two = jnp.sum(grad_normed_two, axis=0)
    grad_residual = seed + norm_back(grad_normed_two * gain_two, unit_two, inverse_two)
    grad_out_bias = jnp.sum(grad_residual, axis=0)
    residual_low = grad_residual.astype(jnp.bfloat16)
    grad_out = rows_inner(mixer, residual_low)
    grad_mixer = to_channels(against_rows(residual_low, out_full).astype(jnp.bfloat16)).astype(
        jnp.float32
    )
    embed_sum = rows_inner(onehot, grad_residual, highest)

    grad_outer = grad_mixer * second_conv
    grad_second = grad_mixer * gate_outer
    skip_second = jnp.sum(grad_second * gated, axis=1)
    back_real, back_imag = forth(grad_second)
    grad_gated = grad_second * local_skip[1] + back(
        *multiply_conj(back_real, back_imag, kernel_real[1], kernel_imag[1])
    )
    kernel_grad_two = back(*multiply_conj(back_real, back_imag, gated_real, gated_imag))
    grad_inner_gate = grad_gated * first_conv
    grad_first = grad_gated * gate_inner
    skip_first = jnp.sum(grad_first * value_part, axis=1)
    early_real, early_imag = forth(grad_first)
    grad_value = grad_first * local_skip[0] + back(
        *multiply_conj(early_real, early_imag, kernel_real[0], kernel_imag[0])
    )
    kernel_grad_one = back(*multiply_conj(early_real, early_imag, value_real, value_imag))
    grad_mixed = jnp.concatenate([grad_outer, grad_inner_gate, grad_value], axis=0)
    id_sums = against_rows(shifted, grad_mixed, highest).reshape(3, vocab, 3, local_width)
    local_sums = jnp.sum(id_sums * local_taps[:, None], axis=0)
    local_taps_grad = jnp.sum(id_sums * local_table[None], axis=1)
    local_short_bias = jnp.sum(id_sums[2], axis=0, keepdims=True)
    local_small = jnp.concatenate(
        [
            local_sums,
            local_taps_grad,
            local_short_bias,
            jnp.pad(jnp.stack([skip_first, skip_second])[:, None], ((0, 0), (0, 2), (0, 0))),
        ],
        axis=0,
    )
    wide_small = lax.dynamic_update_slice_in_dim(
        jnp.zeros((local_small.shape[0], 3, model_width), jnp.float32), local_small, low_rows, 2
    )

    raw_grads = (jnp.stack([kernel_grad_one, kernel_grad_two]) * decay).reshape(
        2 * local_width, length
    )
    grad_local_filter = against_rows(raw_grads, second_act, highest).reshape(2, local_width, -1)
    grad_second_act = rows_inner(local_filter, raw_grads, highest)
    grad_second_pre = grad_second_act * jnp.cos(second_pre)
    grad_inner_weight = against_rows(first_act, grad_second_pre, highest)
    grad_inner_bias = jnp.sum(grad_second_pre, axis=1)
    grad_first_pre = exact_dot(inner_weight, grad_second_pre) * jnp.cos(first_pre)
    grad_freq_weight = against_rows(features, grad_first_pre, highest)
    grad_freq_bias = jnp.sum(grad_first_pre, axis=1)
    sum_filter = lax.psum_scatter(grad_local_filter, "dp", scatter_dimension=0, tiled=False)

    devices = lax.axis_size("dp") * seq_parts
    up_rows = model_width // devices
    pieces = jnp.concatenate(
        [
            grad_up.reshape(devices, -1, model_width),
            grad_down.reshape(devices, -1, model_width),
            grad_out.reshape(devices, -1, model_width),
        ],
        axis=1,
    )
    summed = lax.psum_scatter(pieces, ("dp", "seq"), scatter_dimension=0, tiled=False)
    up_size = up_rows * up_weight.shape[1] // model_width
    sum_up = summed[:up_size].reshape(up_weight.shape)
    sum_down = summed[up_size : up_size + down_weight.shape[0]]
    sum_out = summed[up_size + down_weight.shape[0] :]

    (
        wide_small,
        embed_sum,
        sum_freq_weight,
        sum_freq_bias,
        sum_inner_weight,
        sum_inner_bias,
        sum_out_bias,
        sum_gain_two,
        sum_bias_two,
        sum_up_bias,
        sum_down_bias,
    ) = lax.psum(
        (
            wide_small,
            embed_sum,
            grad_freq_weight,
            grad_freq_bias,
            grad_inner_weight,
            grad_inner_bias,
            grad_out_bias,
            grad_gain_two,
            grad_bias_two,
            grad_up_bias,
            grad_down_bias,
        ),
        ("dp", "seq"),
    )
    total_ids = wide_small[:vocab].reshape(vocab, 3 * model_width)
    sum_taps = wide_small[vocab : vocab + 3].reshape(3, 3 * model_width)
    sum_short_bias = wide_small[vocab + 3].reshape(3 * model_width)
    sum_skip = wide_small[vocab + 4 :, 0]
    sum_in_bias = jnp.sum(total_ids, axis=0)
    own_row = (dp_index * seq_parts + seq_index) * up_rows
    own_normed = lax.dynamic_slice_in_dim(normed, own_row, up_rows, 1).astype(jnp.float32)
    sum_in = rows_inner(own_normed, total_ids, highest)
    grad_normed = against_rows(total_ids, in_full.astype(jnp.float32), highest)
    sum_gain_one = jnp.sum(grad_normed * unit_one, axis=0)
    sum_bias_one = jnp.sum(grad_normed, axis=0)
    sum_embed = embed_sum + norm_back(grad_normed * gain_one, unit_one, inverse_one)
    return (
        block_out[None],
        sum_embed,
        sum_gain_one,
        sum_bias_one,
        sum_in,
        sum_in_bias,
        sum_taps,
        sum_short_bias,
        sum_freq_weight,
        sum_freq_bias,
        sum_inner_weight,
        sum_inner_bias,
        sum_filter,
        sum_skip,
        sum_out,
        sum_out_bias,
        sum_gain_two,
        sum_bias_two,
        sum_up,
        sum_up_bias,
        sum_down,
        sum_down_bias,
    )


F32, BF16 = jnp.float32, jnp.bfloat16
ROWS, PARTS, LOCAL, WIDTH, HIDDEN, SPLIT, IDS = 128, 16, 48, 768, 3072, 768, 16
GROUPS, LANE_CH = 3, 16
BINS = PARTS + 1
SPEC = BINS * LANE_CH
LENGTH = ROWS * PARTS


def tables_of(feature_count):
    b = np.arange(ROWS)
    grid = 2 * np.pi * ((b[:, None] * b[None, :]) % ROWS) / ROWS
    cos, sin = np.cos(grid), np.sin(grid)
    forth = np.block([[cos, -sin], [sin, cos]])
    high = forth.astype(ml_dtypes.bfloat16)
    low = (forth - high.astype(np.float64)).astype(ml_dtypes.bfloat16)
    mats = np.stack([high, low, high.T, low.T])
    k = np.arange(BINS)
    turn = 2 * np.pi * k[:, None] * b[None, :] / (2 * LENGTH)
    scale = np.where((k == 0) | (k == PARTS), 1.0, 2.0)[:, None] / (2 * LENGTH)
    twist = np.zeros((72, ROWS))
    twist[0:17], twist[17:34] = np.cos(turn), np.sin(turn)
    twist[34:51], twist[51:68] = np.cos(turn) * scale, np.sin(turn) * scale
    count = (feature_count - 1) // 2
    phase = np.arange(LENGTH, dtype=np.float32) / np.float32(LENGTH)
    levels = np.float32(0.0001) + np.arange(count, dtype=np.float32) * np.float32(
        (count - 1 - 0.0001) / (count - 1)
    )
    angle = np.float32(2.0 * math.pi) * phase[None, :] * levels[:, None]
    feats = np.zeros((40, LENGTH), np.float32)
    feats[0] = phase
    feats[1 : 1 + count] = np.cos(angle.astype(np.float64))
    feats[1 + count : 1 + 2 * count] = -np.sin(angle.astype(np.float64))
    feats[1 + 2 * count] = 1.0
    return mats, twist.astype(np.float32), feats


def times_turn(value, quarter_count, k, m):
    re, im = value
    c, s = math.cos(math.pi * k / m), math.sin(math.pi * k / m)
    if im is None:
        return (re * c, re * (-s))
    return (re * c + im * s, im * c - re * s)


def real_spectrum(xs):
    m = len(xs)
    if m == 1:
        return [(xs[0], None), (xs[0], None)]
    even, odd = real_spectrum(xs[0::2]), real_spectrum(xs[1::2])
    bins = [None] * (m + 1)
    bins[0] = (even[0][0] + odd[0][0], None)
    bins[m] = (even[0][0] - odd[0][0], None)
    half = m // 2
    bins[half] = (even[half][0], -odd[half][0])
    for k in range(1, half):
        er, ei = even[k]
        tr, ti = times_turn(odd[k], None, k, m)
        bins[k] = (er + tr, ei + ti)
        bins[m - k] = (er - tr, ti - ei)
    return bins


def real_signal(bins):
    m = len(bins) - 1
    if m == 1:
        return [bins[0][0] + bins[1][0]]
    half = m // 2
    even, odd = [None] * (half + 1), [None] * (half + 1)
    even[0] = (bins[0][0] + bins[m][0], None)
    odd[0] = (bins[0][0] - bins[m][0], None)
    even[half] = (bins[half][0], None)
    odd[half] = (-bins[half][1], None)
    for k in range(1, half):
        (ar, ai), (br, bi) = bins[k], bins[m - k]
        even[k] = (ar + br, ai - bi)
        dr, di = ar - br, ai + bi
        c, s = math.cos(math.pi * k / m), math.sin(math.pi * k / m)
        odd[k] = (dr * c - di * s, di * c + dr * s)
    first, second = real_signal(even), real_signal(odd)
    out = [None] * m
    out[0::2], out[1::2] = first, second
    return out


def sin_cos(x):
    n = jnp.floor(x * (1.0 / math.pi) + 0.5)
    r = x - n * 3.140625
    r = r - n * 9.67025756835937500000e-4
    r = r - n * 6.2771141529083251953e-7
    r = r - n * 1.2154201256553420762e-10
    flip = 1.0 - 2.0 * (n - 2.0 * jnp.floor(n * 0.5))
    q = r * r
    s = -2.50507477628578072866e-8
    s = s * q + 2.75573136213857245213e-6
    s = s * q - 1.98412698295895385996e-4
    s = s * q + 8.33333333332211858878e-3
    s = s * q - 1.66666666666666307295e-1
    s = (s * q) * r + r
    c = 2.08757008419747316778e-9
    c = c * q - 2.75573141792967388112e-7
    c = c * q + 2.48015872888517045348e-5
    c = c * q - 1.38888888888730564116e-3
    c = c * q + 4.16666666666665929218e-2
    c = c * q - 0.5
    c = c * q + 1.0
    return s * flip, c * flip


def dot32(a, b, ca, cb, precision=lax.Precision.HIGH):
    return lax.dot_general(
        a, b, (((ca,), (cb,)), ((), ())), precision=precision, preferred_element_type=F32
    )


def dot16(a, b, ca, cb):
    return lax.dot_general(a, b, (((ca,), (cb,)), ((), ())), preferred_element_type=F32)


def start_push(src, dst, send, recv, dp, seq):
    pltpu.make_async_remote_copy(
        src_ref=src,
        dst_ref=dst,
        send_sem=send,
        recv_sem=recv,
        device_id=(dp, seq),
        device_id_type=pl.DeviceIdType.MESH,
    ).start()


def wait_for(ref, sem):
    pltpu.make_async_copy(ref, ref, sem).wait()


def step_kernel(*refs):
    it = iter(refs)

    def take(count):
        return [next(it) for _ in range(count)]

    sources = take(len(INPUTS))
    sinks = take(len(OUTPUTS))
    v = SimpleNamespace(**dict(zip(SCRATCH, take(len(SCRATCH)))))
    sem_s, sem_r, sem_l, sem_o = take(4)
    src = SimpleNamespace(**dict(zip(INPUTS, sources)))
    out = SimpleNamespace(**dict(zip(OUTPUTS, sinks)))
    tok_v, emb_v, par_v, inw_v, mlp_v, filt_v = v.tok, v.emb, v.par, v.inw, v.mlp, v.filt
    outw_v, upw_v, downw_v, mats_v, twist_v, feats_v = v.outw, v.upw, v.downw, v.mats, v.twist, v.feats
    dp, seq = lax.axis_index("dp"), lax.axis_index("seq")
    me = dp * PARTS + seq
    z, yc = lax.div(seq, 4), lax.rem(seq, 4)
    y, core = lax.div(yc, 2), lax.rem(yc, 2)
    chip = dp * 2 + y
    twin = seq + 1 - 2 * core
    other_core = 1 - core
    other_dp = 1 - dp

    def tile(index, size):
        return pl.ds(index * size if isinstance(index, int) else pl.multiple_of(index * size, size), size)

    def everyone(k):
        d = lax.rem(me + k, 2 * PARTS)
        return d, lax.div(d, PARTS), lax.rem(d, PARTS)

    def of_seq(k):
        return lax.rem(seq + k, PARTS)

    def of_plane(k):
        xx, yy = lax.rem(dp + lax.div(k, 2), 2), lax.rem(y + lax.rem(k, 2), 2)
        return xx * 2 + yy, xx, z * 4 + yy * 2 + core

    def of_line(k):
        zz = lax.rem(z + k, 4)
        return zz, zz * 4 + yc

    def of_eight(k):
        j = lax.rem(dp * 4 + yc + k, 8)
        return j, lax.div(j, 4), z * 4 + lax.rem(j, 4)

    def loop(low, high, body):
        def step(k, carry):
            body(k)
            return carry

        lax.fori_loop(low, high, step, 0)

    firsts = np.cumsum([0] + list(FAMILIES.values())).tolist()
    fam = SimpleNamespace(**dict(zip(FAMILIES, zip(range(len(FAMILIES)), firsts))))

    def s_of(family):
        return sem_s.at[family[0]]

    def r_of(family, index=0):
        return sem_r.at[family[1] + index]

    def push(family, source, target, dp_to, seq_to, index=0):
        start_push(source, target, s_of(family), r_of(family, index), dp_to, seq_to)

    def arrived(family, ref, index=0):
        wait_for(ref, r_of(family, index))

    barrier = pltpu.get_barrier_semaphore()

    def greet(k):
        _, d, s = everyone(k)
        pl.semaphore_signal(barrier, inc=1, device_id=(d, s), device_id_type=pl.DeviceIdType.MESH)

    loop(1, 2 * PARTS, greet)
    loads = []

    def load(source, target):
        copy = pltpu.make_async_copy(source, target, sem_l.at[len(loads)])
        copy.start()
        loads.append(copy)

    def load_row(source, row):
        target = par_v.at[row] if len(source.shape) == 1 else par_v.at[row : row + 1, :]
        pltpu.make_async_copy(source, target, sem_l.at[LOADS]).start()

    def wait_load(*which):
        for i in which:
            loads[i].wait()

    load(src.embed_table, emb_v)
    load(src.gain_one, par_v.at[0])
    load(src.bias_one, par_v.at[1])
    load(src.in_weight, inw_v)
    load(src.token_ids, tok_v)
    load(src.filter_weight, filt_v)
    LOAD_WEIGHTS = len(loads)
    load(src.up_weight, upw_v)
    load(src.out_weight, outw_v)
    load(src.cotangent, v.seed_all.at[chip])
    load(src.down_weight, downw_v)
    LOAD_NET = len(loads)
    load(src.freq_weight, mlp_v.at[0:33, :])
    load(src.freq_bias, mlp_v.at[33])
    load(src.inner_weight, mlp_v.at[40:104, :])
    load(src.inner_bias, mlp_v.at[104])
    load(src.feats, feats_v)
    LOAD_TAIL = len(loads)
    load(src.mats, mats_v)
    load(src.twist, twist_v)
    for p in range(3):
        at = pl.ds(p * WIDTH, WIDTH)
        load_row(src.in_bias.at[at], 2 + p)
        load_row(src.short_bias.at[at], 14 + p)
        for t in range(3):
            load_row(src.short_taps.at[t : t + 1, at], 5 + 3 * t + p)
    for t in range(2):
        load_row(src.skip_scale.at[t : t + 1, :], 17 + t)
    load(src.out_bias, par_v.at[19])
    load_row(src.gain_two, 20)
    load_row(src.bias_two, 21)
    load_row(src.down_bias, 22)
    for r in range(4):
        load_row(src.up_bias.at[pl.ds(r * WIDTH, WIDTH)], 23 + r)
    LOAD_END = len(loads)

    wait_load(*range(LOAD_WEIGHTS))
    lanes16 = lax.broadcasted_iota(jnp.int32, (IDS, WIDTH), 0)
    embed = jnp.concatenate([emb_v[...], jnp.zeros((4, WIDTH), F32)], axis=0)
    center = embed - jnp.mean(embed, axis=-1, keepdims=True)
    inverse_one = lax.rsqrt(jnp.mean(center * center, axis=-1, keepdims=True) + epsilon)
    unit_one = center * inverse_one
    normed = (unit_one * par_v[0:1, :] + par_v[1:2, :]).astype(BF16).astype(F32)
    normed = jnp.where(lanes16 < 12, normed, 0.0)
    normed_t = v.normed_t
    normed_t[...] = normed.T
    in_low = inw_v[...].astype(BF16).astype(F32)
    partial = dot32(normed_t[tile(me, 24), :], in_low, 0, 0, None)
    p_send, p_recv = v.p_send, v.p_recv
    for i in range(PARTS):
        block = [partial[:, p * WIDTH + i * LOCAL : p * WIDTH + (i + 1) * LOCAL] for p in range(3)]
        p_send[i] = jnp.concatenate(block + [jnp.zeros((IDS, 256 - 3 * LOCAL), F32)], axis=1).astype(BF16)
    filt_all, tok_all = v.filt_all, v.tok_all
    filt_all[dp] = filt_v[...].astype(BF16)
    tok_all[seq] = tok_v[...]
    p_recv[seq] = p_send[seq]
    mlp_v[34:40, :] = jnp.zeros((6, 64), F32)
    mlp_v[105:112, :] = jnp.zeros((7, 64), F32)

    pl.semaphore_wait(barrier, 2 * PARTS - 1)

    def push_p(k):
        s = of_seq(k)
        push(fam.p, p_send.at[s], p_recv.at[seq], dp, s)

    loop(1, PARTS, push_p)
    wait_load(*range(LOAD_WEIGHTS, LOAD_NET))
    up_send, up_all, out_all, seed_all = v.up_send, v.up_all, v.out_all, v.seed_all
    out_all[core, chip, z] = outw_v[...].astype(BF16)

    def push_out(k):
        zz, s = of_line(k)
        mine = out_all.at[core, chip, z]
        push(fam.outz, mine, mine, dp, s)

    loop(1, 4, push_out)

    def push_tok(k):
        s = of_seq(k)
        push(fam.tok, tok_v, tok_all.at[seq], dp, s)

    loop(1, PARTS, push_tok)
    push(fam.filt, filt_all.at[dp], filt_all.at[dp], other_dp, seq)


    def shard_of(q, c, zz):
        return (q // 2) * PARTS + zz * 4 + (q % 2) * 2 + c

    for q in range(4):
        cut = [
            upw_v[:, 96 * shard_of(q, c, zz) : 96 * (shard_of(q, c, zz) + 1)]
            for c in range(2)
            for zz in range(4)
        ]
        up_send[q] = jnp.concatenate(cut, axis=1).astype(BF16)

    def push_up(k):
        q, d, s = of_plane(k)
        push(fam.up, up_send.at[q], up_all.at[core, z, chip], d, s)

    across = lax.rem(z + 2, 4)
    beside = z + 1 - 2 * lax.rem(z, 2)
    beside_across = lax.rem(beside + 2, 4)

    def to_twin(family, source, target=None):
        push(family, source, source if target is None else target, dp, twin)

    def relay(family, onward, ref, block, zz):
        start_push(ref.at[block], ref.at[block], s_of(onward), r_of(family, block), dp, zz * 4 + yc)

    def spread_start(family, ref):
        @pl.when(z > 0)
        def _():
            relay(family, family, ref, z, z - 1)

        @pl.when(z < 3)
        def _():
            relay(family, family, ref, z, z + 1)

    def spread_near(family, onward, twins, ref):
        @pl.when(z > 0)
        def _():
            arrived(family, ref.at[0], z - 1)

            @pl.when(z < 3)
            def _():
                relay(family, onward, ref, z - 1, z + 1)

            to_twin(twins, ref.at[z - 1])

        @pl.when(z < 3)
        def _():
            arrived(family, ref.at[0], z + 1)

            @pl.when(z > 0)
            def _():
                relay(family, onward, ref, z + 1, z - 1)

            to_twin(twins, ref.at[z + 1])

    def spread_far(family, onward, twins, ref):
        arrived(family, ref.at[0], across)

        @pl.when(z == 1)
        def _():
            relay(family, onward, ref, across, 0)

        @pl.when(z == 2)
        def _():
            relay(family, onward, ref, across, 3)

        to_twin(twins, ref.at[across])

    def spread_last(family, twins, ref):
        @pl.when(lax.rem(z, 3) == 0)
        def _():
            arrived(family, ref.at[0], 3 - z)
            to_twin(twins, ref.at[3 - z])

    def to_line(family, source, target, zz, index):
        push(family, source, target, dp, zz * 4 + yc, index)

    loop(1, 4, push_up)
    down_all = v.down_all
    down_all[core, z] = downw_v[...].astype(BF16)
    spread_start(fam.down, down_all.at[core])
    to_twin(fam.downt, down_all.at[core, z])
    up_all[core, z, chip] = up_send[chip]
    act1, cos1, act2, cos2 = v.act1, v.cos1, v.act2, v.cos2
    wait_load(*range(LOAD_NET, LOAD_TAIL))
    mlp = mlp_v[...]
    freq_t = mlp[0:40].T
    inner_bias = mlp[104:112].T[:, 0:1]
    inner = mlp[40:104]

    def network(i):
        at = tile(i, 512)
        s1, c1 = sin_cos(dot32(freq_t, feats_v[:, at], 1, 0))
        act1[0:64, at] = s1
        cos1[:, at] = c1
        act1[64:72, at] = jnp.where(
            lax.broadcasted_iota(jnp.int32, (8, 512), 0) == 0, 1.0, 0.0
        ).astype(F32)
        s2, c2 = sin_cos(dot32(inner, s1, 0, 0) + inner_bias)
        act2[:, at] = s2
        cos2[:, at] = c2

    loop(0, 4, network)
    def gather_first(family, ref, k):
        _, d, s = of_plane(k)
        push(family, ref.at[chip], ref.at[chip], d, s, 0)

    def gather_second(family, ref, k):
        arrived(family, ref.at[0], 0)
        q, _, _ = of_plane(k)
        _, d, s = of_plane(3 - k)
        push(family, ref.at[chip], ref.at[chip], d, s, 1)
        push(family, ref.at[q], ref.at[q], d, s, 1)


    wait_load(*range(LOAD_TAIL, LOAD_END))
    wait_for(par_v.at[0:24], sem_l.at[LOADS])
    par_t = v.par_t
    for i in range(WIDTH // 128):
        par_t[128 * i : 128 * (i + 1), :] = par_v[:, 128 * i : 128 * (i + 1)].T
    own_par = par_t[tile(seq, LOCAL), :]

    kern, hi_ref, lo_ref = v.kern, v.hi, v.lo
    spec_k1, spec_k2, spec_v, spec_g = v.spec_k1, v.spec_k2, v.spec_v, v.spec_g
    arrived(fam.filt, filt_all.at[0])
    filt = jnp.concatenate([filt_all[0], filt_all[1]], axis=0).astype(F32)
    for i in range(LENGTH // 256):
        both = dot32(filt, act2[:, 256 * i : 256 * (i + 1)], 1, 0)
        for h in range(2):
            for f in range(2):
                kern[f, 2 * i + h] = both[f * LOCAL : (f + 1) * LOCAL, 128 * h : 128 * (h + 1)]
    lane = lax.broadcasted_iota(jnp.int32, (LANE_CH, ROWS), 1).astype(F32)

    def decay_of(g):
        row = lax.broadcasted_iota(jnp.int32, (LANE_CH, ROWS), 0) + (seq * LOCAL + g * LANE_CH)
        rate = slow_rate + (fast_rate - slow_rate) * (row.astype(F32) * (1.0 / (WIDTH - 1)))
        return lambda a: jnp.exp((lane + float(a * ROWS)) * (rate * (-1.0 / LENGTH))) + decay_shift

    turn = [0]

    def put(row0, k, re, im):
        rows = pl.ds(row0 + k * LANE_CH, LANE_CH)
        for part, value in ((0, re), (1, im)):
            at = pl.ds(part * ROWS, ROWS)
            high = value.astype(BF16)
            hi_ref[turn[0], rows, at] = high
            lo_ref[turn[0], rows, at] = (value - high.astype(F32)).astype(BF16)

    def forth(row0, values):
        for k, (re, im) in enumerate(real_spectrum(values)):
            c, s = twist_v[k : k + 1, :], twist_v[17 + k : 18 + k, :]
            if im is None:
                put(row0, k, re * c, re * (-s))
            else:
                put(row0, k, re * c + im * s, im * c - re * s)

    def dft(rows, which):
        high, low = hi_ref[turn[0], 0:rows, :], lo_ref[turn[0], 0:rows, :]
        m_high, m_low = mats_v[which], mats_v[which + 1]
        return dot16(high, m_high, 1, 0) + dot16(low, m_high, 1, 0) + dot16(high, m_low, 1, 0)

    def put_product(row0, spec, other, conj):
        a_re, a_im = spec[:, 0:ROWS], spec[:, ROWS:]
        b_re, b_im = other[:, 0:ROWS], other[:, ROWS:]
        if conj:
            re, im = a_re * b_re + a_im * b_im, a_im * b_re - a_re * b_im
        else:
            re, im = a_re * b_re - a_im * b_im, a_re * b_im + a_im * b_re
        rows = pl.ds(row0, SPEC)
        for part, value in ((0, re), (1, im)):
            at = pl.ds(part * ROWS, ROWS)
            high = value.astype(BF16)
            hi_ref[turn[0], rows, at] = high
            lo_ref[turn[0], rows, at] = (value - high.astype(F32)).astype(BF16)

    def back(turned, row0):
        bins = []
        for k in range(BINS):
            part = turned[row0 + k * LANE_CH : row0 + (k + 1) * LANE_CH]
            re, im = part[:, 0:ROWS], part[:, ROWS:]
            c, s = twist_v[34 + k : 35 + k, :], twist_v[51 + k : 52 + k, :]
            if k in (0, PARTS):
                bins.append((re * c - im * s, None))
            else:
                bins.append((re * c - im * s, im * c + re * s))
        return real_signal(bins)

    def kernel_spectra(g):
        turn[0] = g
        at = tile(g, LANE_CH)
        decay = decay_of(g)
        damp = [decay(a) for a in range(PARTS)]
        forth(0, [kern[0, a, at, :] * damp[a] for a in range(PARTS)])
        forth(SPEC, [kern[1, a, at, :] * damp[a] for a in range(PARTS)])
        spec = dft(2 * SPEC, 0)
        spec_k1[g] = spec[0:SPEC]
        spec_k2[g] = spec[SPEC:]

    kernel_spectra(0)
    kernel_spectra(1)

    arrived(fam.p, p_recv.at[0 : PARTS - 1])
    table = p_recv[0].astype(F32)
    for s in range(1, PARTS):
        table = table + p_recv[s].astype(F32)
    px_send, px_recv = v.px_send, v.px_recv
    px_send[...] = table
    push(fam.px, px_send, px_recv, other_dp, seq)
    arrived(fam.up, up_send.at[0:3])
    spread_start(fam.upz, up_all.at[core])
    to_twin(fam.upt, up_all.at[core, z])
    arrived(fam.outz, out_all.at[0, 0, 0:3])
    gather_first(fam.outp, out_all.at[core], 2 - core)
    to_twin(fam.outt, out_all.at[core, chip])
    kernel_spectra(2)
    spread_near(fam.down, fam.downf, fam.downt, down_all.at[core])


    table_t, onehot, mix = v.table_t, v.onehot, v.mix
    arrived(fam.px, px_recv)
    wide_t = (px_send[...] + px_recv[...]).T
    table_t[...] = jnp.concatenate(
        [wide_t[p * LOCAL : (p + 1) * LOCAL] + own_par[:, 2 + p : 3 + p] for p in range(3)], axis=0
    )

    arrived(fam.tok, tok_all.at[0 : PARTS - 1])
    id_rows = lax.broadcasted_iota(jnp.int32, (IDS, ROWS), 0)
    for a in range(PARTS):
        now = tok_all[a]
        if a == 0:
            long = jnp.concatenate([jnp.full((1, ROWS), -1, jnp.int32), now], axis=1)
        else:
            long = jnp.concatenate([tok_all[a - 1], now], axis=1)
        for t in range(3):
            moved = long[:, ROWS - 2 + t : 2 * ROWS - 2 + t]
            onehot[t * IDS : (t + 1) * IDS, a * ROWS : (a + 1) * ROWS] = (
                id_rows == moved
            ).astype(F32)

    def taps_of(t):
        return jnp.concatenate(
            [own_par[:, 5 + 3 * t + p : 6 + 3 * t + p] for p in range(3)], axis=0
        )

    short = jnp.concatenate([taps_of(t) * table_t[...] for t in range(3)], axis=1)
    short_bias = jnp.concatenate([own_par[:, 14 + p : 15 + p] for p in range(3)], axis=0)
    for i in range(LENGTH // 256):
        both = dot32(short, onehot[:, 256 * i : 256 * (i + 1)], 1, 0) + short_bias
        for h in range(2):
            for p in range(3):
                mix[p, 2 * i + h] = both[p * LOCAL : (p + 1) * LOCAL, 128 * h : 128 * (h + 1)]

    first_s, gated_s, second_s = v.first, v.gated, v.second
    mix_send, mix_recv = v.mix_send, v.mix_recv
    gm_send, gm_recv = v.gm_send, v.gm_recv

    def exchange(family, send, recv):
        def one(k):
            s = of_seq(k)
            push(family, send.at[s], recv.at[seq], dp, s)

        loop(1, PARTS, one)

    def operator(g):
        turn[0] = g
        at = tile(g, LANE_CH)
        skips = par_t[pl.ds(pl.multiple_of(seq * LOCAL + g * LANE_CH, LANE_CH), LANE_CH), :]
        skip0, skip1 = skips[:, 17:18], skips[:, 18:19]
        forth(0, [mix[2, a, at, :] for a in range(PARTS)])
        spec = dft(SPEC, 0)
        spec_v[g] = spec
        put_product(0, spec, spec_k1[g], False)
        signal = back(dft(SPEC, 2), 0)
        gated = []
        for a in range(PARTS):
            conv = signal[a] + skip0 * mix[2, a, at, :]
            first_s[a, at, :] = conv
            gate = mix[1, a, at, :] * conv
            gated_s[a, at, :] = gate
            gated.append(gate)
        forth(0, gated)
        spec = dft(SPEC, 0)
        spec_g[g] = spec
        put_product(0, spec, spec_k2[g], False)
        signal = back(dft(SPEC, 2), 0)
        for a in range(PARTS):
            conv = signal[a] + skip1 * gated_s[a, at, :]
            second_s[a, at, :] = conv
            mix_send[a, at, :] = (mix[0, a, at, :] * conv).astype(BF16)


    gather_second(fam.outp, out_all.at[core], 2 - core)
    gather_first(fam.seed, seed_all, 2 - core)
    for g in range(GROUPS):
        operator(g)
    exchange(fam.mix, mix_send, mix_recv)
    spread_near(fam.upz, fam.upf, fam.upt, up_all.at[core])
    mix_recv[seq] = mix_send[seq]

    own_onehot = (id_rows == tok_v[...]).astype(F32)
    resid, unit2, inv2, n2_all = v.resid, v.unit2, v.inv2, v.n2_all
    resid[...] = dot32(own_onehot, embed, 0, 0) + par_v[19:20, :]
    arrived(fam.outp, out_all.at[0, 0:2], 1)

    def forward_out(k):
        q, _, _ = of_plane(k)
        to_twin(fam.outt, out_all.at[core, q])

    loop(1, 4, forward_out)
    w_up, w_out = v.w_up, v.w_out
    arrived(fam.outt, out_all.at[0])

    def place_out(i):
        q, zz = lax.div(i, 8) * 2 + lax.rem(i, 2), lax.rem(lax.div(i, 2), 4)
        both = jnp.concatenate(
            [out_all[0, q, zz].astype(F32), out_all[1, q, zz].astype(F32)], axis=0
        )
        w_out[tile(i, 48), :] = both.astype(BF16)

    loop(0, 16, place_out)
    arrived(fam.mix, mix_recv.at[0 : PARTS - 1])


    mixer_t = mix_recv[...].reshape(WIDTH, ROWS)
    residual = resid[...] + dot16(mixer_t, w_out[...], 0, 0)
    resid[...] = residual
    center = residual - jnp.mean(residual, axis=-1, keepdims=True)
    inv = lax.rsqrt(jnp.mean(center * center, axis=-1, keepdims=True) + epsilon)
    inv2[...] = inv
    unit = center * inv
    unit2[...] = unit
    n2_all[chip] = (unit * par_v[20:21, :] + par_v[21:22, :]).astype(BF16)

    def push_n2(k, q):
        _, d, s = of_plane(k)
        push(fam.n2, n2_all.at[q], n2_all.at[q], d, s, q)

    push_n2(1, chip)
    push_n2(2, chip)
    gather_second(fam.seed, seed_all, 2 - core)
    spread_far(fam.upz, fam.upf, fam.upt, up_all.at[core])
    spread_far(fam.down, fam.downf, fam.downt, down_all.at[core])

    up_bias = jnp.zeros((1, SPLIT), F32)
    for q in range(4):
        cut = []
        for c in range(2):
            for zz in range(4):
                first = 96 * shard_of(q, c, zz)
                row, lane0 = first // WIDTH, first % WIDTH
                cut.append(par_v[23 + row : 24 + row, lane0 : lane0 + 96])
        up_bias = jnp.where(chip == q, jnp.concatenate(cut, axis=1), up_bias)

    spread_last(fam.upz, fam.upt, up_all.at[core])
    arrived(fam.upt, up_all.at[0])

    def place_up(i):
        q, zz = lax.div(i, 8) * 2 + lax.rem(i, 2), lax.rem(lax.div(i, 2), 4)
        both = jnp.concatenate(
            [up_all[0, zz, q].astype(F32), up_all[1, zz, q].astype(F32)], axis=0
        )
        w_up[tile(i, 48), :] = both.astype(BF16)

    loop(0, 16, place_up)
    act_all, gl_all, po_all, gn_all, slope = v.act_all, v.gl_all, v.po_all, v.gn_all, v.slope
    gn_recv, po_recv = v.gn_recv, v.po_recv

    def feed(k):
        q, _, _ = of_plane(k)
        lifted = dot16(n2_all[q], w_up[...], 1, 0) + up_bias
        cdf = 0.5 * (1.0 + lax.erf(lifted * (1.0 / math.sqrt(2.0))))
        pdf = jnp.exp(-0.5 * lifted * lifted) * (1.0 / math.sqrt(2.0 * math.pi))
        act_all[q] = (lifted * cdf).astype(BF16)
        slope[q] = cdf + lifted * pdf

    feed(0)
    first_k = 2 - core
    first_q, _, _ = of_plane(first_k)
    arrived(fam.n2, n2_all.at[0], first_q)
    push_n2(3 - first_k, first_q)
    feed(first_k)
    second_q, _, _ = of_plane(3 - first_k)
    arrived(fam.n2, n2_all.at[0], second_q)
    feed(3 - first_k)
    last_q, _, _ = of_plane(3)
    arrived(fam.n2, n2_all.at[0], last_q)
    feed(3)
    arrived(fam.seed, seed_all.at[0:2], 1)

    sd_x, sd_y, sd_t, sd_z = v.sd_x, v.sd_y, v.sd_t, v.sd_z
    su_x, su_y, su_t, su_z, su_p, su_r = v.su_x, v.su_y, v.su_t, v.su_z, v.su_p, v.su_r
    so_x, so_y, so_t, so_p, so_u, so_z = v.so_x, v.so_y, v.so_t, v.so_p, v.so_u, v.so_z
    acts = act_all[...].reshape(4 * ROWS, SPLIT)
    seeds = seed_all[...].reshape(4 * ROWS, WIDTH)
    for c in range(2):
        half = acts[:, c * 384 : (c + 1) * 384]
        sd_x[c] = dot16(half, seeds, 0, 0).astype(BF16).reshape(4, 96, WIDTH)
    to_twin(fam.sdt, sd_x.at[other_core], sd_y)

    def add_sd(zz):
        sd_t[zz] = (sd_x[core, zz].astype(F32) + sd_y[zz].astype(F32)).astype(BF16)

    def add_su(zz):
        for q in range(4):
            su_t[zz, q] = (su_x[core, zz, q].astype(F32) + su_y[zz, q].astype(F32)).astype(BF16)

    def fold_send(family, sums, landing, block, zz, side):
        to_line(family, sums.at[block], landing.at[side, block], zz, side * 4 + block)

    def fold_add(family, sums, landing, block, side):
        arrived(family, landing.at[side, block], side * 4 + block)
        sums[block] = (sums[block].astype(F32) + landing[side, block].astype(F32)).astype(BF16)

    def fold_start(family, sums, landing, blocks):
        @pl.when(z == 0)
        def _():
            for far in blocks:
                fold_send(family, sums, landing, far, 1, 0)

        @pl.when(z == 3)
        def _():
            for far in blocks:
                fold_send(family, sums, landing, 3 - far, 2, 1)

    def fold_middle(family, sums, landing):
        @pl.when(z == 1)
        def _():
            for block in (3, 2):
                fold_add(family, sums, landing, block, 0)
                fold_send(family, sums, landing, block, 2, 0)

        @pl.when(z == 2)
        def _():
            for block in (0, 1):
                fold_add(family, sums, landing, block, 1)
                fold_send(family, sums, landing, block, 1, 1)

    def fold_end(family, sums, landing):
        @pl.when(z == 2)
        def _():
            fold_add(family, sums, landing, 3, 0)
            fold_send(family, sums, landing, 3, 3, 0)

        @pl.when(z == 1)
        def _():
            fold_add(family, sums, landing, 0, 1)
            fold_send(family, sums, landing, 0, 0, 1)

    def fold_total(family, sums, landing, total):
        total[...] = sums[z].astype(F32)

        @pl.when(z > 0)
        def _():
            arrived(family, landing.at[0, z], z)
            total[...] = total[...] + landing[0, z].astype(F32)

        @pl.when(z < 3)
        def _():
            arrived(family, landing.at[1, z], 4 + z)
            total[...] = total[...] + landing[1, z].astype(F32)

    spread_last(fam.down, fam.downt, down_all.at[core])
    arrived(fam.downt, down_all.at[0])

    def feed_back(k, bias_sum):
        q, d, s = of_plane(lax.rem(k, 4))
        grad_act = dot16(seed_all[q], down_all[...].reshape(SPLIT, WIDTH), 1, 1)
        grad_lifted = grad_act * slope[q]
        gl_all[q] = grad_lifted.astype(BF16)
        gn_all[q] = dot16(gl_all[q], w_up[...], 1, 1).astype(BF16)

        @pl.when(k != 4)
        def _():
            push(fam.gn, gn_all.at[q], gn_recv.at[chip], d, s)

        return bias_sum + jnp.sum(grad_lifted, axis=0, keepdims=True)

    grad_up_bias = lax.fori_loop(1, 3, feed_back, jnp.zeros((1, SPLIT), F32))
    arrived(fam.sdt, sd_y)
    loop(0, 4, add_sd)
    fold_start(fam.sd, sd_t, sd_z, (3, 2))
    grad_up_bias = lax.fori_loop(3, 5, feed_back, grad_up_bias)
    gn_recv[chip] = gn_all[chip]
    units = n2_all[...].reshape(4 * ROWS, WIDTH)
    lows = gl_all[...].reshape(4 * ROWS, SPLIT)
    for x in range(2):
        part = dot16(units[:, x * 384 : (x + 1) * 384], lows, 0, 0)
        for i in range(16):
            su_x[i % 2, i // 4, x * 2 + (i // 2) % 2] = part[24 * i : 24 * (i + 1)].astype(BF16)
    to_twin(fam.sut, su_x.at[other_core], su_y)
    arrived(fam.sut, su_y)
    loop(0, 4, add_su)
    fold_start(fam.su, su_t, su_z, (3, 2))


    def outputs_part(k):
        q, _, _ = of_plane(k)
        po_all[q] = dot16(act_all[q], down_all[...].reshape(SPLIT, WIDTH), 1, 0).astype(BF16)

    loop(0, 4, outputs_part)

    fold_middle(fam.sd, sd_t, sd_z)

    arrived(fam.gn, gn_all.at[0:3])
    grad_n2 = gn_recv[0].astype(F32)
    for q in range(1, 4):
        grad_n2 = grad_n2 + gn_recv[q].astype(F32)
    unit, inv = unit2[...], inv2[...]
    seed = seed_all[chip].astype(F32)
    scaled = grad_n2 * par_v[20:21, :]
    grad_res = seed + inv * (
        scaled
        - jnp.mean(scaled, axis=-1, keepdims=True)
        - unit * jnp.mean(scaled * unit, axis=-1, keepdims=True)
    )
    gres = v.gres
    gres[...] = grad_res.astype(BF16)
    gm_send[...] = dot16(w_out[...], gres[...], 1, 1).astype(BF16).reshape(PARTS, LOCAL, ROWS)
    exchange(fam.gm, gm_send, gm_recv)
    gm_recv[seq] = gm_send[seq]

    def sum_first(family, sums, landing, k):
        q, d, s = of_plane(k)
        push(family, sums.at[q], landing.at[0], d, s, 0)
        q, _, _ = of_plane(3)
        push(family, sums.at[q], landing.at[1], d, s, 0)

    def sum_second(family, sums, landing, k):
        arrived(family, landing.at[0:2], 0)
        q, d, s = of_plane(3 - k)
        sums[q] = (sums[q].astype(F32) + landing[1].astype(F32)).astype(BF16)
        push(family, sums.at[q], landing.at[2], d, s, 1)

    sum_first(fam.po, po_all, po_recv, 2 - core)
    b_x, b_y, b_p, b_t, b_z, b_f = v.b_x, v.b_y, v.b_p, v.b_t, v.b_z, v.b_f
    b_x[0:12, :] = dot32(own_onehot, grad_res, 1, 0)[0:12]
    b_x[12:13, :] = jnp.sum(grad_res, axis=0, keepdims=True)
    b_x[13:14, :] = jnp.sum(grad_n2 * unit, axis=0, keepdims=True)
    b_x[14:15, :] = jnp.sum(grad_n2, axis=0, keepdims=True)
    b_x[15:16, :] = jnp.sum(seed, axis=0, keepdims=True)
    for q in range(4):
        b_x[16 + q : 17 + q, :] = jnp.where(chip == q, grad_up_bias, 0.0)
    b_x[20:24, :] = jnp.zeros((4, WIDTH), F32)
    to_twin(fam.bt, b_x, b_y)
    for x in range(2):
        part = dot16(mixer_t[x * 384 : (x + 1) * 384], gres[...], 1, 0)
        for i in range(16):
            so_x[i % 2, x * 2 + (i // 2) % 2, i // 4] = part[24 * i : 24 * (i + 1)].astype(BF16)
    to_twin(fam.sot, so_x.at[other_core], so_y)

    def push_b(k):
        q, d, s = of_plane(k)
        mine = b_p.at[chip]
        push(fam.b, mine, mine, d, s)

    def add_so(zz):
        for q in range(4):
            so_t[q, zz] = (so_x[core, q, zz].astype(F32) + so_y[q, zz].astype(F32)).astype(BF16)

    grad_mix, raw, q_s = v.grad_mix, v.raw, v.q_s

    def operator_back(g):
        turn[0] = g
        at = tile(g, LANE_CH)
        skips = par_t[pl.ds(pl.multiple_of(seq * LOCAL + g * LANE_CH, LANE_CH), LANE_CH), :]
        skip0, skip1 = skips[:, 17:18], skips[:, 18:19]
        decay = decay_of(g)

        def rows_at(first, count=LANE_CH):
            return pl.ds(first + g * LANE_CH, count)

        seconds, total = [], jnp.zeros((LANE_CH, ROWS), F32)
        for a in range(PARTS):
            upstream = gm_recv[a, at, :].astype(F32)
            lanes = slice(a * ROWS, (a + 1) * ROWS)
            grad_mix[rows_at(0), lanes] = upstream * second_s[a, at, :]
            grad_second = upstream * mix[0, a, at, :]
            total = total + grad_second * gated_s[a, at, :]
            seconds.append(grad_second)
        q_s[rows_at(0), 49:50] = jnp.sum(total, axis=1, keepdims=True)
        forth(0, seconds)
        spec = dft(SPEC, 0)
        put_product(0, spec, spec_k2[g], True)
        put_product(SPEC, spec, spec_g[g], True)
        turned = dft(2 * SPEC, 2)
        signal = back(turned, 0)
        cross = back(turned, SPEC)
        firsts, total = [], jnp.zeros((LANE_CH, ROWS), F32)
        for a in range(PARTS):
            lanes = slice(a * ROWS, (a + 1) * ROWS)
            raw[rows_at(LOCAL), lanes] = cross[a] * decay(a)
            grad_second = gm_recv[a, at, :].astype(F32) * mix[0, a, at, :]
            grad_gated = skip1 * grad_second + signal[a]
            grad_mix[rows_at(LOCAL), lanes] = grad_gated * first_s[a, at, :]
            grad_first = grad_gated * mix[1, a, at, :]
            total = total + grad_first * mix[2, a, at, :]
            grad_mix[rows_at(2 * LOCAL), lanes] = skip0 * grad_first
            firsts.append(grad_first)
        q_s[rows_at(0), 48:49] = jnp.sum(total, axis=1, keepdims=True)
        forth(0, firsts)
        spec = dft(SPEC, 0)
        put_product(0, spec, spec_k1[g], True)
        put_product(SPEC, spec, spec_v[g], True)
        turned = dft(2 * SPEC, 2)
        signal = back(turned, 0)
        cross = back(turned, SPEC)
        for a in range(PARTS):
            lanes = slice(a * ROWS, (a + 1) * ROWS)
            raw[rows_at(0), lanes] = cross[a] * decay(a)
            grad_mix[rows_at(2 * LOCAL), lanes] = grad_mix[rows_at(2 * LOCAL), lanes] + signal[a]

    def sums_of_rows():
        arrived(fam.bt, b_y)
        for c in range(2):

            @pl.when(core == c)
            def _():
                at = slice(c * 384, (c + 1) * 384)
                b_p[chip] = (b_x[:, at] + b_y[:, at]).astype(BF16)

        loop(1, 4, push_b)

    arrived(fam.gm, gm_recv.at[0 : PARTS - 1])
    fold_end(fam.sd, sd_t, sd_z)
    fold_middle(fam.su, su_t, su_z)
    arrived(fam.sot, so_y)
    loop(0, 4, add_so)
    sum_first(fam.so, so_t, so_p, 2 - core)
    sums_of_rows()
    fold_start(fam.su, su_t, su_z, (1,))
    fold_start(fam.sd, sd_t, sd_z, (1,))
    for g in range(GROUPS):
        operator_back(g)
    fold_end(fam.su, su_t, su_z)
    sum_second(fam.so, so_t, so_p, 2 - core)
    sum_second(fam.po, po_all, po_recv, 2 - core)
    arrived(fam.b, b_p.at[0:3])
    b_t[...] = (
        (b_p[0].astype(F32) + b_p[1].astype(F32)) + (b_p[2].astype(F32) + b_p[3].astype(F32))
    ).astype(BF16)
    b_z[z] = b_t[...]

    def push_b2(k):
        zz, s = of_line(k)
        push(fam.b2, b_t, b_z.at[z], dp, s)

    loop(1, 4, push_b2)

    zx_send, zx_recv, z_send, z_recv = v.zx_send, v.zx_recv, v.z_send, v.z_recv
    by_id = dot32(grad_mix[...], onehot[...], 1, 1)
    sums = sum(taps_of(t) * by_id[:, t * IDS : (t + 1) * IDS] for t in range(3))
    taps_grad = [
        jnp.sum(table_t[...] * by_id[:, t * IDS : (t + 1) * IDS], axis=1, keepdims=True)
        for t in range(3)
    ]
    bias_grad = jnp.sum(by_id[:, 2 * IDS : 3 * IDS], axis=1, keepdims=True)
    columns = jnp.concatenate([sums[:, 0:12]] + taps_grad + [bias_grad], axis=1)
    skip_cols = jnp.concatenate(
        [q_s[:, 48:50], jnp.zeros((LOCAL, 14), F32)], axis=1
    )
    zx_send[...] = jnp.concatenate(
        [columns, skip_cols, jnp.zeros((64, IDS), F32)], axis=0
    ).T
    push(fam.zx, zx_send, zx_recv, other_dp, seq)

    f_send, f_recv, m_send, m_recv, m2_send, m2_recv = (v.f_send, v.f_recv, v.m_send, v.m_recv, v.m2_send, v.m2_recv)
    grad_filter = dot32(raw[...], act2[...], 1, 1)
    f_send[...] = grad_filter
    there = f_send.at[tile(other_dp, LOCAL), :]
    push(fam.f, there, f_recv, other_dp, seq)
    grad_second_pre = dot32(filt, raw[...], 0, 0) * cos2[...]
    grad_inner = dot32(act1[...], grad_second_pre, 1, 1)
    grad_first_pre = dot32(inner, grad_second_pre, 1, 0) * cos1[...]
    grad_freq = dot32(feats_v[...], grad_first_pre, 1, 1)
    m_send[...] = jnp.concatenate(
        [
            jnp.concatenate([grad_freq, jnp.zeros((40, 64), F32)], axis=0),
            jnp.concatenate([grad_inner, jnp.zeros((8, 64), F32)], axis=0),
        ],
        axis=1,
    ).astype(BF16)
    j_me = dp * 4 + yc
    m_recv[j_me] = m_send[...]

    def push_m(k):
        j, d, s = of_eight(k)
        push(fam.m, m_send, m_recv.at[j_me], d, s)

    loop(1, 8, push_m)

    arrived(fam.zx, zx_recv)
    z_send[...] = (zx_send[...] + zx_recv[...]).astype(BF16)
    z_recv[seq] = z_send[...]

    def push_z(k):
        s = of_seq(k)
        push(fam.z, z_send, z_recv.at[seq], dp, s)

    loop(1, PARTS, push_z)
    arrived(fam.so, so_p.at[0], 1)
    for zz in range(4):
        part = so_t[chip, zz].astype(F32) + so_p[0, zz].astype(F32) + so_p[2, zz].astype(F32)
        so_u[zz] = part.astype(BF16)
    so_z[z] = so_u[z]

    def push_so2(k):
        zz, s = of_line(k)
        push(fam.so2, so_u.at[zz], so_z.at[z], dp, s)

    loop(1, 4, push_so2)
    fold_total(fam.su, su_t, su_z, v.su_f)
    su_p[...] = v.su_f[...].astype(BF16)
    su_r[chip] = su_p[chip]

    def push_su2(k):
        q, d, s = of_plane(k)
        push(fam.su2, su_p.at[q], su_r.at[chip], d, s)

    loop(1, 4, push_su2)


    arrived(fam.m, m_recv.at[0:7])
    totals = m_recv[0].astype(F32)
    for j in range(1, 8):
        totals = totals + m_recv[j].astype(F32)
    m2_send[...] = totals.astype(BF16)
    m2_recv[z] = m2_send[...]

    def push_m2(k):
        zz, s = of_line(k)
        push(fam.m2, m2_send, m2_recv.at[z], dp, s)

    loop(1, 4, push_m2)

    wide, gt_all = v.wide, v.gt_all
    arrived(fam.z, z_recv.at[0 : PARTS - 1])
    for p in range(4):
        for i in range(PARTS):
            wide[:, p * WIDTH + i * LOCAL : p * WIDTH + (i + 1) * LOCAL] = z_recv[i][
                :, p * LOCAL : (p + 1) * LOCAL
            ].astype(F32)
    by_ids = jnp.where(
        lax.broadcasted_iota(jnp.int32, (IDS, 3 * WIDTH), 0) < 12, wide[:, 0 : 3 * WIDTH], 0.0
    )
    own_gt = dot32(in_low, by_ids, 1, 1)
    gt_all[me] = jnp.concatenate(
        [own_gt[8 * t : 8 * (t + 1)] for t in range(3)] + [jnp.zeros((8, 80), F32)], axis=1
    )

    def push_gt(k):
        _, d, s = everyone(k)
        mine = gt_all.at[me]
        push(fam.gt, mine, mine, d, s)

    loop(1, 2 * PARTS, push_gt)

    stores = []

    def store(source, target):
        copy = pltpu.make_async_copy(source, target, sem_o.at[len(stores)])
        copy.start()
        stores.append(copy)

    o_in, o_wide, o_rows = v.o_in, v.o_wide, v.o_rows
    o_in[...] = dot32(normed_t[tile(me, 24), :], by_ids, 1, 0)
    o_wide[...] = jnp.sum(by_ids, axis=0, keepdims=True)
    o_rows[2:4, :] = wide[0:2, 3 * WIDTH :]
    store(o_in, out.in_weight)
    store(o_wide.at[0], out.in_bias)
    store(wide.at[12:15, 0 : 3 * WIDTH], out.short_taps)
    store(wide.at[15, pl.ds(0, 3 * WIDTH)], out.short_bias)
    store(o_rows.at[2:4, :], out.skip_scale)

    arrived(fam.po, po_recv.at[0], 1)
    block = resid[...] + par_v[22:23, :] + po_all[chip].astype(F32)
    block = block + po_recv[0].astype(F32) + po_recv[2].astype(F32)
    resid[...] = block
    store(resid, out.block)

    fold_total(fam.sd, sd_t, sd_z, downw_v)
    store(downw_v, out.down_weight)
    arrived(fam.f, f_recv)
    f_recv[...] = f_send[tile(dp, LOCAL), :] + f_recv[...]
    store(f_recv, out.filter_weight)

    arrived(fam.su2, su_r.at[0:3])
    for q in range(4):
        part = su_r[q].astype(F32)
        for c in range(2):
            for zz in range(4):
                first, place = 96 * shard_of(q, c, zz), 384 * c + 96 * zz
                upw_v[:, first : first + 96] = part[:, place : place + 96]
    store(upw_v, out.up_weight)

    arrived(fam.b2, b_z.at[0:3])
    b_f[core] = (b_z[0].astype(F32) + b_z[1].astype(F32)) + (b_z[2].astype(F32) + b_z[3].astype(F32))
    to_twin(fam.bf, b_f.at[core])
    arrived(fam.so2, so_z.at[0:3])
    part = so_z[0].astype(F32)
    for zz in range(1, 4):
        part = part + so_z[zz].astype(F32)
    outw_v[...] = part
    store(outw_v, out.out_weight)
    arrived(fam.m2, m2_recv.at[0:3])
    totals = m2_recv[0].astype(F32)
    for zz in range(1, 4):
        totals = totals + m2_recv[zz].astype(F32)
    mlp_v[0:40, :] = totals[0:40, 0:64]
    mlp_v[40:112, :] = totals[0:72, 64:128]
    store(mlp_v.at[0:33, :], out.freq_weight)
    store(mlp_v.at[33], out.freq_bias)
    store(mlp_v.at[40:104, :], out.inner_weight)
    store(mlp_v.at[104], out.inner_bias)
    arrived(fam.bf, b_f.at[0])
    totals = jnp.concatenate([b_f[0], b_f[1]], axis=1)
    o_rows[4:8, :] = totals[12:16]
    o_up = v.o_up
    for q in range(4):
        for c in range(2):
            for zz in range(4):
                first, place = 96 * shard_of(q, c, zz), 384 * c + 96 * zz
                o_up[:, first : first + 96] = totals[16 + q : 17 + q, place : place + 96]
    store(o_rows.at[4], out.out_bias)
    store(o_rows.at[5], out.gain_two)
    store(o_rows.at[6], out.bias_two)
    store(o_rows.at[7], out.down_bias)
    store(o_up.at[0], out.up_bias)

    arrived(fam.gt, gt_all.at[0 : 2 * PARTS - 1])
    gts = gt_all[...]
    grad_normed = jnp.concatenate([gts[:, :, IDS * t : IDS * (t + 1)] for t in range(3)], axis=1)
    grad_normed = grad_normed.reshape(WIDTH, IDS).T
    o_rows[0:1, :] = jnp.sum(grad_normed * unit_one, axis=0, keepdims=True)
    o_rows[1:2, :] = jnp.sum(grad_normed, axis=0, keepdims=True)
    scaled = grad_normed * par_v[0:1, :]
    grad_embed = inverse_one * (
        scaled
        - jnp.mean(scaled, axis=-1, keepdims=True)
        - unit_one * jnp.mean(scaled * unit_one, axis=-1, keepdims=True)
    )
    emb_v[...] = totals[0:12] + grad_embed[0:12]
    store(o_rows.at[0], out.gain_one)
    store(o_rows.at[1], out.bias_one)
    store(emb_v, out.embed_table)

    for family, ref in (
        (fam.p, p_send.at[0 : PARTS - 1]), (fam.tok, tok_all.at[0 : PARTS - 1]), (fam.filt, filt_all.at[0]),
        (fam.px, px_send), (fam.outz, out_all.at[0, 0, 0:3]), (fam.outp, out_all.at[0, 0:3]),
        (fam.outt, out_all.at[0]), (fam.up, up_send.at[0:3]),
        (fam.upt, up_all.at[0]), (fam.seed, seed_all.at[0:3]),
        (fam.downt, down_all.at[0]), (fam.mix, mix_send.at[0 : PARTS - 1]),
        (fam.gm, gm_send.at[0 : PARTS - 1]), (fam.n2, n2_all.at[0:3]), (fam.gn, gn_all.at[0:3]),
        (fam.po, po_all.at[0:3]), (fam.sdt, sd_y), (fam.sut, su_y), (fam.sot, so_y), (fam.sd, sd_t.at[0:3]),
        (fam.su, su_t.at[0:3]), (fam.su2, su_p.at[0:3]), (fam.so, so_t.at[0:3]), (fam.so2, so_u.at[0:3]),
        (fam.bt, b_x), (fam.b, b_p.at[0:3]), (fam.b2, b_z.at[0:3]), (fam.bf, b_f.at[0]),
        (fam.m, m_recv.at[0:7]), (fam.m2, m2_recv.at[0:3]), (fam.z, z_recv.at[0 : PARTS - 1]),
        (fam.zx, zx_send), (fam.f, f_recv), (fam.gt, gt_all.at[0 : 2 * PARTS - 1]),
    ):
        wait_for(ref, s_of(family))
    for family, onward, ref in (
        (fam.upz, fam.upf, up_all.at[0]),
        (fam.down, fam.downf, down_all.at[0]),
    ):

        @pl.when(lax.rem(z, 3) == 0)
        def _():
            wait_for(ref.at[0], s_of(family))

        @pl.when(lax.rem(z, 3) != 0)
        def _():
            wait_for(ref.at[0:2], s_of(family))
            wait_for(ref.at[0:3], s_of(onward))

    for copy in stores:
        copy.wait()


def copy_kernel(*refs):
    count = len(OUTPUTS)
    for source, target in zip(refs[:count], refs[count:]):
        target[...] = source[...]


FAMILIES = dict(
    p=1, tok=1, filt=1, px=1, outz=1, outp=2, outt=1, up=1, upz=4, upf=0, upt=1, down=4, downf=0, downt=1, seed=2, mix=1,
    gm=1, n2=4, gn=1, po=2, sdt=1, sd=8, sut=1, su=8, su2=1, sot=1, so=2, so2=1, bt=1, b=1, b2=1, bf=1,
    m=1, m2=1, z=1, zx=1, f=1, gt=1,
)
LOADS = 18
INPUTS = dict(
    token_ids=0, embed_table=0, gain_one=0, bias_one=0, in_weight=0, in_bias=0, short_taps=0, short_bias=0,
    freq_weight=0, freq_bias=0, inner_weight=0, inner_bias=0, filter_weight=0, skip_scale=0, out_weight=0,
    out_bias=0, gain_two=0, bias_two=0, up_weight=0, up_bias=0, down_weight=0, down_bias=0, cotangent=0,
    mats=0, twist=0, feats=0,
)
OUTPUTS = dict(
    block=(ROWS, WIDTH), embed_table=(12, WIDTH), gain_one=(WIDTH,),
    bias_one=(WIDTH,), in_weight=(24, 3 * WIDTH), in_bias=(3 * WIDTH,),
    short_taps=(3, 3 * WIDTH), short_bias=(3 * WIDTH,), freq_weight=(33, 64),
    freq_bias=(64,), inner_weight=(64, 64), inner_bias=(64,),
    filter_weight=(LOCAL, 64), skip_scale=(2, WIDTH), out_weight=(24, WIDTH),
    out_bias=(WIDTH,), gain_two=(WIDTH,), bias_two=(WIDTH,),
    up_weight=(24, HIDDEN), up_bias=(HIDDEN,), down_weight=(96, WIDTH),
    down_bias=(WIDTH,),
)
SPECTRUM = (GROUPS, SPEC, 2 * ROWS)
SCRATCH = dict(
    tok=((1, ROWS), jnp.int32), emb=((12, WIDTH), F32), par=((32, WIDTH), F32),
    inw=((24, 3 * WIDTH), F32), mlp=((112, 64), F32), filt=((LOCAL, 64), F32),
    outw=((24, WIDTH), F32), upw=((24, HIDDEN), F32), downw=((96, WIDTH), F32),
    mats=((4, 256, 256), BF16), twist=((72, ROWS), F32), feats=((40, LENGTH), F32),
    normed_t=((WIDTH, IDS), F32), p_send=((PARTS, IDS, 256), BF16),
    p_recv=((PARTS, IDS, 256), BF16), px_send=((IDS, 256), F32), px_recv=((IDS, 256), F32),
    filt_all=((2, LOCAL, 64), BF16), tok_all=((PARTS, 1, ROWS), jnp.int32),
    up_send=((4, 24, SPLIT), BF16), up_all=((2, 4, 4, 24, SPLIT), BF16),
    out_all=((2, 4, 4, 24, WIDTH), BF16), seed_all=((4, ROWS, WIDTH), BF16),
    down_all=((2, 4, 96, WIDTH), BF16), w_up=((WIDTH, SPLIT), BF16), w_out=((WIDTH, WIDTH), BF16),
    act1=((72, LENGTH), F32), cos1=((64, LENGTH), F32), act2=((64, LENGTH), F32),
    cos2=((64, LENGTH), F32), kern=((2, PARTS, LOCAL, ROWS), F32), par_t=((WIDTH, 32), F32),
    table_t=((3 * LOCAL, IDS), F32), onehot=((3 * IDS, LENGTH), F32),
    mix=((3, PARTS, LOCAL, ROWS), F32),
    hi=((GROUPS, 2 * SPEC, 2 * ROWS), BF16), lo=((GROUPS, 2 * SPEC, 2 * ROWS), BF16),
    spec_k1=(SPECTRUM, F32), spec_k2=(SPECTRUM, F32), spec_v=(SPECTRUM, F32),
    spec_g=(SPECTRUM, F32),
    first=((PARTS, LOCAL, ROWS), F32), gated=((PARTS, LOCAL, ROWS), F32),
    second=((PARTS, LOCAL, ROWS), F32),
    mix_send=((PARTS, LOCAL, ROWS), BF16), mix_recv=((PARTS, LOCAL, ROWS), BF16),
    gm_send=((PARTS, LOCAL, ROWS), BF16), gm_recv=((PARTS, LOCAL, ROWS), BF16),
    resid=((ROWS, WIDTH), F32), unit2=((ROWS, WIDTH), F32), inv2=((ROWS, 1), F32),
    n2_all=((4, ROWS, WIDTH), BF16), act_all=((4, ROWS, SPLIT), BF16),
    gl_all=((4, ROWS, SPLIT), BF16), slope=((4, ROWS, SPLIT), F32), po_all=((4, ROWS, WIDTH), BF16),
    po_recv=((3, ROWS, WIDTH), BF16), gn_all=((4, ROWS, WIDTH), BF16),
    gn_recv=((4, ROWS, WIDTH), BF16), gres=((ROWS, WIDTH), BF16),
    sd_x=((2, 4, 96, WIDTH), BF16), sd_y=((4, 96, WIDTH), BF16), sd_t=((4, 96, WIDTH), BF16),
    sd_z=((2, 4, 96, WIDTH), BF16),
    su_x=((2, 4, 4, 24, SPLIT), BF16), su_y=((4, 4, 24, SPLIT), BF16),
    su_t=((4, 4, 24, SPLIT), BF16), su_z=((2, 4, 4, 24, SPLIT), BF16), su_f=((4, 24, SPLIT), F32), su_p=((4, 24, SPLIT), BF16),
    su_r=((4, 24, SPLIT), BF16),
    so_x=((2, 4, 4, 24, WIDTH), BF16), so_y=((4, 4, 24, WIDTH), BF16),
    so_t=((4, 4, 24, WIDTH), BF16), so_p=((3, 4, 24, WIDTH), BF16), so_u=((4, 24, WIDTH), BF16),
    so_z=((4, 24, WIDTH), BF16),
    b_x=((24, WIDTH), F32), b_y=((24, WIDTH), F32), b_p=((4, 24, 384), BF16),
    b_t=((24, 384), BF16), b_z=((4, 24, 384), BF16), b_f=((2, 24, 384), F32),
    grad_mix=((3 * LOCAL, LENGTH), F32), raw=((2 * LOCAL, LENGTH), F32), q_s=((LOCAL, 128), F32),
    z_send=((IDS, 256), BF16), z_recv=((PARTS, IDS, 256), BF16), zx_send=((IDS, 256), F32),
    zx_recv=((IDS, 256), F32), wide=((IDS, 4 * WIDTH), F32), gt_all=((32, 8, 128), F32),
    m_send=((80, 128), BF16), m_recv=((8, 80, 128), BF16), m2_send=((80, 128), BF16),
    m2_recv=((4, 80, 128), BF16), f_send=((2 * LOCAL, 64), F32), f_recv=((LOCAL, 64), F32),
    o_in=((24, 3 * WIDTH), F32), o_wide=((1, 3 * WIDTH), F32), o_rows=((8, WIDTH), F32),
    o_up=((1, HIDDEN), F32),
)


def fits(mesh_shape, args):
    return (
        mesh_shape["dp"] == 2
        and mesh_shape["seq"] == PARTS
        and args[0].shape == (1, ROWS)
        and args[1].shape == (12, WIDTH)
        and args[4].shape == (24, 3 * WIDTH)
        and args[8].shape == (33, 64)
        and args[18].shape == (24, HIDDEN)
    )


def fast_device(*args):
    given = SimpleNamespace(**dict(zip(INPUTS, args)))
    tables = tables_of(given.freq_weight.shape[0])
    given.mats, given.twist, given.feats = (jnp.asarray(table) for table in tables)
    given.cotangent = given.cotangent[0]
    anywhere, near = (pl.BlockSpec(memory_space=space) for space in (pl.ANY, pltpu.VMEM))
    shapes = [jax.ShapeDtypeStruct(shape, F32) for shape in OUTPUTS.values()]
    counts = (len(FAMILIES), sum(FAMILIES.values()), LOADS + 1, len(shapes))
    made = pl.pallas_call(
        step_kernel,
        out_shape=shapes,
        in_specs=[anywhere] * len(INPUTS),
        out_specs=[anywhere] * len(shapes),
        scratch_shapes=[pltpu.VMEM(shape, kind) for shape, kind in SCRATCH.values()]
        + [pltpu.SemaphoreType.DMA((count,)) for count in counts],
        compiler_params=pltpu.CompilerParams(
            collective_id=0, has_side_effects=True, vmem_limit_bytes=60 * 1024 * 1024
        ),
    )(*(getattr(given, name) for name in INPUTS))
    made = pl.pallas_call(
        copy_kernel,
        out_shape=shapes,
        in_specs=[near] * len(shapes),
        out_specs=[near] * len(shapes),
    )(*made)
    return (made[0][None], *made[1:])


def solution(mesh):
    in_specs = (
        P("dp", "seq"),
        P(),
        P(),
        P(),
        P(("dp", "seq"), None),
        P(),
        P(),
        P(),
        P(),
        P(),
        P(),
        P(),
        P(("dp", "seq"), None),
        P(),
        P(("dp", "seq"), None),
        P(),
        P(),
        P(),
        P(("dp", "seq"), None),
        P(),
        P(("dp", "seq"), None),
        P(),
        P("dp", "seq", None),
    )
    out_specs = (
        P("dp", "seq", None),
        P(),
        P(),
        P(),
        P(("dp", "seq"), None),
        P(),
        P(),
        P(),
        P(),
        P(),
        P(),
        P(),
        P(("dp", "seq"), None),
        P(),
        P(("dp", "seq"), None),
        P(),
        P(),
        P(),
        P(("dp", "seq"), None),
        P(),
        P(("dp", "seq"), None),
        P(),
    )

    def either(*args):
        return (fast_device if fits(mesh.shape, args) else per_device)(*args)

    return jax.shard_map(
        either, mesh=mesh, in_specs=in_specs, out_specs=out_specs, check_vma=False
    )
```

```python
import math
from types import SimpleNamespace

import jax
import jax.numpy as jnp
import ml_dtypes
import numpy as np
from jax import lax
from jax.experimental import pallas as pl
from jax.experimental.pallas import tpu as pltpu
from jax.sharding import PartitionSpec as P

epsilon = 1e-05
slow_rate = -math.log(0.01) / 1.5
fast_rate = -math.log(0.01) / 0.3
decay_shift = 0.05
highest = lax.Precision.HIGHEST


def exact_dot(left_side, right_side):
    return jnp.dot(left_side, right_side, precision=highest, preferred_element_type=jnp.float32)


def narrow_dot(left_side, right_side):
    return jnp.dot(left_side, right_side, preferred_element_type=jnp.float32)


def rows_inner(left_side, right_side, accuracy=None):
    return lax.dot_general(
        left_side,
        right_side,
        (((0,), (0,)), ((), ())),
        precision=accuracy,
        preferred_element_type=jnp.float32,
    )


def against_rows(left_side, right_side, accuracy=None):
    return lax.dot_general(
        left_side,
        right_side,
        (((1,), (1,)), ((), ())),
        precision=accuracy,
        preferred_element_type=jnp.float32,
    )


def normalize(values):
    center = values - jnp.mean(values, axis=-1, keepdims=True)
    inverse = lax.rsqrt(jnp.mean(center * center, axis=-1, keepdims=True) + epsilon)
    return (center * inverse, inverse)


def norm_back(upstream, unit_vals, inverse):
    return inverse * (
        upstream
        - jnp.mean(upstream, axis=-1, keepdims=True)
        - unit_vals * jnp.mean(upstream * unit_vals, axis=-1, keepdims=True)
    )


def angle_table(row_count, column_count, modulus):
    product = (
        jnp.arange(row_count, dtype=jnp.int32)[:, None]
        * jnp.arange(column_count, dtype=jnp.int32)[None, :]
        % modulus
    )
    angles = 2.0 * math.pi / modulus * product.astype(jnp.float32)
    return (jnp.cos(angles), jnp.sin(angles))


def forward_transform(signal, tables):
    cos_section, sin_section, cos_twist, sin_twist, cos_last, sin_last = tables
    real_first = jnp.einsum("kn,...nm->...km", cos_section, signal, precision=highest)
    imag_first = -jnp.einsum("kn,...nm->...km", sin_section, signal, precision=highest)
    real_turn = real_first * cos_twist + imag_first * sin_twist
    imag_turn = imag_first * cos_twist - real_first * sin_twist
    real_out = exact_dot(real_turn, cos_last) + exact_dot(imag_turn, sin_last)
    imag_out = exact_dot(imag_turn, cos_last) - exact_dot(real_turn, sin_last)
    return (real_out, imag_out)


def inverse_transform(real_spec, imag_spec, tables):
    cos_section, sin_section, cos_twist, sin_twist, cos_last, sin_last = tables
    real_turn = exact_dot(real_spec, cos_last) - exact_dot(imag_spec, sin_last)
    imag_turn = exact_dot(imag_spec, cos_last) + exact_dot(real_spec, sin_last)
    real_first = real_turn * cos_twist - imag_turn * sin_twist
    imag_first = imag_turn * cos_twist + real_turn * sin_twist
    signal = jnp.einsum("kn,...km->...nm", cos_section, real_first, precision=highest) - jnp.einsum(
        "kn,...km->...nm", sin_section, imag_first, precision=highest
    )
    return signal / (cos_twist.shape[0] * cos_twist.shape[1])


def multiply(real_one, imag_one, real_two, imag_two):
    return (real_one * real_two - imag_one * imag_two, real_one * imag_two + imag_one * real_two)


def multiply_conj(real_one, imag_one, real_two, imag_two):
    return (real_one * real_two + imag_one * imag_two, imag_one * real_two - real_one * imag_two)


def to_channels(rows_in):
    return lax.all_to_all(rows_in.T, "seq", split_axis=0, concat_axis=1, tiled=True)


def to_rows(columns):
    return lax.all_to_all(columns, "seq", split_axis=1, concat_axis=0, tiled=True).T


def gather_all(pieces):
    shapes = [piece.shape for piece in pieces]
    flat = jnp.concatenate([piece.astype(jnp.bfloat16).reshape(-1) for piece in pieces])
    whole = lax.all_gather(flat, ("dp", "seq"), axis=0, tiled=False)
    result, start = [], 0
    for shape in shapes:
        size = math.prod(shape)
        result.append(whole[:, start : start + size].reshape((-1,) + shape[1:]))
        start += size
    return result


def per_device(
    token_ids,
    embed_table,
    gain_one,
    bias_one,
    in_weight,
    in_bias,
    short_taps,
    short_bias,
    freq_weight,
    freq_bias,
    inner_weight,
    inner_bias,
    filter_weight,
    skip_scale,
    out_weight,
    out_bias,
    gain_two,
    bias_two,
    up_weight,
    up_bias,
    down_weight,
    down_bias,
    cotangent,
):
    tokens = token_ids[0]
    row_count = tokens.shape[0]
    vocab, model_width = embed_table.shape
    seq_parts = lax.axis_size("seq")
    seq_index = lax.axis_index("seq")
    dp_index = lax.axis_index("dp")
    local_width = model_width // seq_parts
    length = row_count * seq_parts
    freq_rows = 2 * seq_parts
    low_rows = seq_index * local_width

    def own_channels(table):
        parts = table.reshape(table.shape[0], -1, model_width)
        return lax.dynamic_slice_in_dim(parts, low_rows, local_width, 2)

    in_full, out_full, up_full, down_full, filter_full, tokens_full = gather_all(
        (in_weight, out_weight, up_weight, down_weight, filter_weight, token_ids)
    )
    sequence = lax.dynamic_slice_in_dim(
        tokens_full.reshape(-1, length), dp_index, 1, 0
    )[0].astype(jnp.int32)
    cos_section, sin_section = angle_table(freq_rows, seq_parts, freq_rows)
    cos_twist, sin_twist = angle_table(freq_rows, row_count, freq_rows * row_count)
    cos_last, sin_last = angle_table(row_count, row_count, row_count)
    tables = (cos_section, sin_section, cos_twist, sin_twist, cos_last, sin_last)

    unit_one, inverse_one = normalize(embed_table)
    normed = (unit_one * gain_one + bias_one).astype(jnp.bfloat16)
    table = narrow_dot(normed, in_full) + in_bias
    local_table = own_channels(table)
    local_taps = own_channels(short_taps)
    local_bias = own_channels(short_bias[None])[0]
    local_skip = own_channels(skip_scale)[:, 0, :, None]
    ids = jnp.arange(vocab, dtype=jnp.int32)[:, None]
    padded = jnp.concatenate([jnp.full((2,), -1, jnp.int32), sequence])
    shifted = jnp.concatenate(
        [(padded[None, j : j + length] == ids).astype(jnp.float32) for j in range(3)], axis=0
    )
    weights = (local_taps[:, None] * local_table[None]).reshape(3 * vocab, 3 * local_width)
    mixed = rows_inner(weights, shifted, highest) + local_bias.reshape(-1, 1)
    gate_outer = mixed[:local_width]
    gate_inner = mixed[local_width : 2 * local_width]
    value_part = mixed[2 * local_width :]

    count = (freq_weight.shape[0] - 1) // 2
    position_phase = jnp.arange(length, dtype=jnp.float32) / length
    levels = 0.0001 + jnp.arange(count, dtype=jnp.float32) * ((count - 1 - 0.0001) / (count - 1))
    angles = 2.0 * math.pi * position_phase[None, :] * levels[:, None]
    features = jnp.concatenate([position_phase[None, :], jnp.cos(angles), -jnp.sin(angles)], axis=0)
    first_pre = rows_inner(freq_weight, features, highest) + freq_bias[:, None]
    first_act = jnp.sin(first_pre)
    second_pre = rows_inner(inner_weight, first_act, highest) + inner_bias[:, None]
    second_act = jnp.sin(second_pre)
    channel = (low_rows + jnp.arange(local_width, dtype=jnp.int32)).astype(jnp.float32) / (
        model_width - 1
    )
    decay_rate = slow_rate + (fast_rate - slow_rate) * channel
    decay = jnp.exp(-position_phase[None, :] * decay_rate[:, None]) + decay_shift
    local_filter = lax.dynamic_slice_in_dim(
        filter_full.reshape(2, model_width, -1), low_rows, local_width, 1
    ).astype(jnp.float32).reshape(2 * local_width, -1)
    kernels = exact_dot(local_filter, second_act).reshape(2, local_width, length) * decay

    def forth(signal):
        shape = signal.shape[:-1] + (seq_parts, row_count)
        return forward_transform(signal.reshape(shape), tables)

    def back(real_spec, imag_spec):
        result = inverse_transform(real_spec, imag_spec, tables)
        return result.reshape(result.shape[:-2] + (length,))

    kernel_real, kernel_imag = forth(kernels)
    value_real, value_imag = forth(value_part)
    first_conv = (
        back(*multiply(value_real, value_imag, kernel_real[0], kernel_imag[0]))
        + local_skip[0] * value_part
    )
    gated = gate_inner * first_conv
    gated_real, gated_imag = forth(gated)
    second_conv = (
        back(*multiply(gated_real, gated_imag, kernel_real[1], kernel_imag[1]))
        + local_skip[1] * gated
    )
    mixer = to_rows((gate_outer * second_conv).astype(jnp.bfloat16))

    onehot = (tokens[:, None] == ids[:, 0][None, :]).astype(jnp.float32)
    hidden = exact_dot(onehot, embed_table)
    residual = hidden + narrow_dot(mixer, out_full) + out_bias
    unit_two, inverse_two = normalize(residual)
    normed_two = (unit_two * gain_two + bias_two).astype(jnp.bfloat16)
    lifted = narrow_dot(normed_two, up_full) + up_bias
    normal_cdf = 0.5 * (1.0 + lax.erf(lifted * (1.0 / math.sqrt(2.0))))
    activated = (lifted * normal_cdf).astype(jnp.bfloat16)
    block_out = residual + narrow_dot(activated, down_full) + down_bias
    seed_low = cotangent[0]
    seed = seed_low.astype(jnp.float32)
    grad_down_bias = jnp.sum(seed, axis=0)
    grad_down = rows_inner(activated, seed_low)
    grad_activated = against_rows(seed_low, down_full)
    normal_pdf = jnp.exp(-0.5 * lifted * lifted) * (1.0 / math.sqrt(2.0 * math.pi))
    grad_lifted = grad_activated * (normal_cdf + lifted * normal_pdf)
    grad_up_bias = jnp.sum(grad_lifted, axis=0)
    lifted_low = grad_lifted.astype(jnp.bfloat16)
    grad_up = rows_inner(normed_two, lifted_low)
    grad_normed_two = against_rows(lifted_low, up_full)
    grad_gain_two = jnp.sum(grad_normed_two * unit_two, axis=0)
    grad_bias_two = jnp.sum(grad_normed_two, axis=0)
    grad_residual = seed + norm_back(grad_normed_two * gain_two, unit_two, inverse_two)
    grad_out_bias = jnp.sum(grad_residual, axis=0)
    residual_low = grad_residual.astype(jnp.bfloat16)
    grad_out = rows_inner(mixer, residual_low)
    grad_mixer = to_channels(against_rows(residual_low, out_full).astype(jnp.bfloat16)).astype(
        jnp.float32
    )
    embed_sum = rows_inner(onehot, grad_residual, highest)

    grad_outer = grad_mixer * second_conv
    grad_second = grad_mixer * gate_outer
    skip_second = jnp.sum(grad_second * gated, axis=1)
    back_real, back_imag = forth(grad_second)
    grad_gated = grad_second * local_skip[1] + back(
        *multiply_conj(back_real, back_imag, kernel_real[1], kernel_imag[1])
    )
    kernel_grad_two = back(*multiply_conj(back_real, back_imag, gated_real, gated_imag))
    grad_inner_gate = grad_gated * first_conv
    grad_first = grad_gated * gate_inner
    skip_first = jnp.sum(grad_first * value_part, axis=1)
    early_real, early_imag = forth(grad_first)
    grad_value = grad_first * local_skip[0] + back(
        *multiply_conj(early_real, early_imag, kernel_real[0], kernel_imag[0])
    )
    kernel_grad_one = back(*multiply_conj(early_real, early_imag, value_real, value_imag))
    grad_mixed = jnp.concatenate([grad_outer, grad_inner_gate, grad_value], axis=0)
    id_sums = against_rows(shifted, grad_mixed, highest).reshape(3, vocab, 3, local_width)
    local_sums = jnp.sum(id_sums * local_taps[:, None], axis=0)
    local_taps_grad = jnp.sum(id_sums * local_table[None], axis=1)
    local_short_bias = jnp.sum(id_sums[2], axis=0, keepdims=True)
    local_small = jnp.concatenate(
        [
            local_sums,
            local_taps_grad,
            local_short_bias,
            jnp.pad(jnp.stack([skip_first, skip_second])[:, None], ((0, 0), (0, 2), (0, 0))),
        ],
        axis=0,
    )
    wide_small = lax.dynamic_update_slice_in_dim(
        jnp.zeros((local_small.shape[0], 3, model_width), jnp.float32), local_small, low_rows, 2
    )

    raw_grads = (jnp.stack([kernel_grad_one, kernel_grad_two]) * decay).reshape(
        2 * local_width, length
    )
    grad_local_filter = against_rows(raw_grads, second_act, highest).reshape(2, local_width, -1)
    grad_second_act = rows_inner(local_filter, raw_grads, highest)
    grad_second_pre = grad_second_act * jnp.cos(second_pre)
    grad_inner_weight = against_rows(first_act, grad_second_pre, highest)
    grad_inner_bias = jnp.sum(grad_second_pre, axis=1)
    grad_first_pre = exact_dot(inner_weight, grad_second_pre) * jnp.cos(first_pre)
    grad_freq_weight = against_rows(features, grad_first_pre, highest)
    grad_freq_bias = jnp.sum(grad_first_pre, axis=1)
    sum_filter = lax.psum_scatter(grad_local_filter, "dp", scatter_dimension=0, tiled=False)

    devices = lax.axis_size("dp") * seq_parts
    up_rows = model_width // devices
    pieces = jnp.concatenate(
        [
            grad_up.reshape(devices, -1, model_width),
            grad_down.reshape(devices, -1, model_width),
            grad_out.reshape(devices, -1, model_width),
        ],
        axis=1,
    )
    summed = lax.psum_scatter(pieces, ("dp", "seq"), scatter_dimension=0, tiled=False)
    up_size = up_rows * up_weight.shape[1] // model_width
    sum_up = summed[:up_size].reshape(up_weight.shape)
    sum_down = summed[up_size : up_size + down_weight.shape[0]]
    sum_out = summed[up_size + down_weight.shape[0] :]

    (
        wide_small,
        embed_sum,
        sum_freq_weight,
        sum_freq_bias,
        sum_inner_weight,
        sum_inner_bias,
        sum_out_bias,
        sum_gain_two,
        sum_bias_two,
        sum_up_bias,
        sum_down_bias,
    ) = lax.psum(
        (
            wide_small,
            embed_sum,
            grad_freq_weight,
            grad_freq_bias,
            grad_inner_weight,
            grad_inner_bias,
            grad_out_bias,
            grad_gain_two,
            grad_bias_two,
            grad_up_bias,
            grad_down_bias,
        ),
        ("dp", "seq"),
    )
    total_ids = wide_small[:vocab].reshape(vocab, 3 * model_width)
    sum_taps = wide_small[vocab : vocab + 3].reshape(3, 3 * model_width)
    sum_short_bias = wide_small[vocab + 3].reshape(3 * model_width)
    sum_skip = wide_small[vocab + 4 :, 0]
    sum_in_bias = jnp.sum(total_ids, axis=0)
    own_row = (dp_index * seq_parts + seq_index) * up_rows
    own_normed = lax.dynamic_slice_in_dim(normed, own_row, up_rows, 1).astype(jnp.float32)
    sum_in = rows_inner(own_normed, total_ids, highest)
    grad_normed = against_rows(total_ids, in_full.astype(jnp.float32), highest)
    sum_gain_one = jnp.sum(grad_normed * unit_one, axis=0)
    sum_bias_one = jnp.sum(grad_normed, axis=0)
    sum_embed = embed_sum + norm_back(grad_normed * gain_one, unit_one, inverse_one)
    return (
        block_out[None],
        sum_embed,
        sum_gain_one,
        sum_bias_one,
        sum_in,
        sum_in_bias,
        sum_taps,
        sum_short_bias,
        sum_freq_weight,
        sum_freq_bias,
        sum_inner_weight,
        sum_inner_bias,
        sum_filter,
        sum_skip,
        sum_out,
        sum_out_bias,
        sum_gain_two,
        sum_bias_two,
        sum_up,
        sum_up_bias,
        sum_down,
        sum_down_bias,
    )


F32, BF16 = jnp.float32, jnp.bfloat16
ROWS, PARTS, LOCAL, WIDTH, HIDDEN, SPLIT, IDS = 128, 16, 48, 768, 3072, 768, 16
GROUPS, LANE_CH = 3, 16
BINS = PARTS + 1
SPEC = BINS * LANE_CH
LENGTH = ROWS * PARTS


def tables_of(feature_count):
    b = np.arange(ROWS)
    grid = 2 * np.pi * ((b[:, None] * b[None, :]) % ROWS) / ROWS
    cos, sin = np.cos(grid), np.sin(grid)
    forth = np.block([[cos, -sin], [sin, cos]])
    high = forth.astype(ml_dtypes.bfloat16)
    low = (forth - high.astype(np.float64)).astype(ml_dtypes.bfloat16)
    mats = np.stack([high, low, high.T, low.T])
    k = np.arange(BINS)
    turn = 2 * np.pi * k[:, None] * b[None, :] / (2 * LENGTH)
    scale = np.where((k == 0) | (k == PARTS), 1.0, 2.0)[:, None] / (2 * LENGTH)
    twist = np.zeros((72, ROWS))
    twist[0:17], twist[17:34] = np.cos(turn), np.sin(turn)
    twist[34:51], twist[51:68] = np.cos(turn) * scale, np.sin(turn) * scale
    count = (feature_count - 1) // 2
    phase = np.arange(LENGTH, dtype=np.float32) / np.float32(LENGTH)
    levels = np.float32(0.0001) + np.arange(count, dtype=np.float32) * np.float32(
        (count - 1 - 0.0001) / (count - 1)
    )
    angle = np.float32(2.0 * math.pi) * phase[None, :] * levels[:, None]
    feats = np.zeros((40, LENGTH), np.float32)
    feats[0] = phase
    feats[1 : 1 + count] = np.cos(angle.astype(np.float64))
    feats[1 + count : 1 + 2 * count] = -np.sin(angle.astype(np.float64))
    feats[1 + 2 * count] = 1.0
    return mats, twist.astype(np.float32), feats


def times_turn(value, quarter_count, k, m):
    re, im = value
    c, s = math.cos(math.pi * k / m), math.sin(math.pi * k / m)
    if im is None:
        return (re * c, re * (-s))
    return (re * c + im * s, im * c - re * s)


def real_spectrum(xs):
    m = len(xs)
    if m == 1:
        return [(xs[0], None), (xs[0], None)]
    even, odd = real_spectrum(xs[0::2]), real_spectrum(xs[1::2])
    bins = [None] * (m + 1)
    bins[0] = (even[0][0] + odd[0][0], None)
    bins[m] = (even[0][0] - odd[0][0], None)
    half = m // 2
    bins[half] = (even[half][0], -odd[half][0])
    for k in range(1, half):
        er, ei = even[k]
        tr, ti = times_turn(odd[k], None, k, m)
        bins[k] = (er + tr, ei + ti)
        bins[m - k] = (er - tr, ti - ei)
    return bins


def real_signal(bins):
    m = len(bins) - 1
    if m == 1:
        return [bins[0][0] + bins[1][0]]
    half = m // 2
    even, odd = [None] * (half + 1), [None] * (half + 1)
    even[0] = (bins[0][0] + bins[m][0], None)
    odd[0] = (bins[0][0] - bins[m][0], None)
    even[half] = (bins[half][0], None)
    odd[half] = (-bins[half][1], None)
    for k in range(1, half):
        (ar, ai), (br, bi) = bins[k], bins[m - k]
        even[k] = (ar + br, ai - bi)
        dr, di = ar - br, ai + bi
        c, s = math.cos(math.pi * k / m), math.sin(math.pi * k / m)
        odd[k] = (dr * c - di * s, di * c + dr * s)
    first, second = real_signal(even), real_signal(odd)
    out = [None] * m
    out[0::2], out[1::2] = first, second
    return out


def sin_cos(x):
    n = jnp.floor(x * (1.0 / math.pi) + 0.5)
    r = x - n * 3.140625
    r = r - n * 9.67025756835937500000e-4
    r = r - n * 6.2771141529083251953e-7
    r = r - n * 1.2154201256553420762e-10
    flip = 1.0 - 2.0 * (n - 2.0 * jnp.floor(n * 0.5))
    q = r * r
    s = -2.50507477628578072866e-8
    s = s * q + 2.75573136213857245213e-6
    s = s * q - 1.98412698295895385996e-4
    s = s * q + 8.33333333332211858878e-3
    s = s * q - 1.66666666666666307295e-1
    s = (s * q) * r + r
    c = 2.08757008419747316778e-9
    c = c * q - 2.75573141792967388112e-7
    c = c * q + 2.48015872888517045348e-5
    c = c * q - 1.38888888888730564116e-3
    c = c * q + 4.16666666666665929218e-2
    c = c * q - 0.5
    c = c * q + 1.0
    return s * flip, c * flip


def dot32(a, b, ca, cb, precision=lax.Precision.HIGH):
    return lax.dot_general(
        a, b, (((ca,), (cb,)), ((), ())), precision=precision, preferred_element_type=F32
    )


def dot16(a, b, ca, cb):
    return lax.dot_general(a, b, (((ca,), (cb,)), ((), ())), preferred_element_type=F32)


def start_push(src, dst, send, recv, dp, seq):
    pltpu.make_async_remote_copy(
        src_ref=src,
        dst_ref=dst,
        send_sem=send,
        recv_sem=recv,
        device_id=(dp, seq),
        device_id_type=pl.DeviceIdType.MESH,
    ).start()


def wait_for(ref, sem):
    pltpu.make_async_copy(ref, ref, sem).wait()


def step_kernel(*refs):
    it = iter(refs)

    def take(count):
        return [next(it) for _ in range(count)]

    sources = take(len(INPUTS))
    sinks = take(len(OUTPUTS))
    v = SimpleNamespace(**dict(zip(SCRATCH, take(len(SCRATCH)))))
    sem_s, sem_r, sem_l, sem_o = take(4)
    src = SimpleNamespace(**dict(zip(INPUTS, sources)))
    out = SimpleNamespace(**dict(zip(OUTPUTS, sinks)))
    tok_v, emb_v, par_v, inw_v, mlp_v, filt_v = v.tok, v.emb, v.par, v.inw, v.mlp, v.filt
    outw_v, upw_v, downw_v, mats_v, twist_v, feats_v = v.outw, v.upw, v.downw, v.mats, v.twist, v.feats
    dp, seq = lax.axis_index("dp"), lax.axis_index("seq")
    me = dp * PARTS + seq
    z, yc = lax.div(seq, 4), lax.rem(seq, 4)
    y, core = lax.div(yc, 2), lax.rem(yc, 2)
    chip = dp * 2 + y
    twin = seq + 1 - 2 * core
    other_core = 1 - core
    other_dp = 1 - dp

    def tile(index, size):
        return pl.ds(index * size if isinstance(index, int) else pl.multiple_of(index * size, size), size)

    def everyone(k):
        d = lax.rem(me + k, 2 * PARTS)
        return d, lax.div(d, PARTS), lax.rem(d, PARTS)

    def of_seq(k):
        return lax.rem(seq + k, PARTS)

    def of_plane(k):
        xx, yy = lax.rem(dp + lax.div(k, 2), 2), lax.rem(y + lax.rem(k, 2), 2)
        return xx * 2 + yy, xx, z * 4 + yy * 2 + core

    def of_line(k):
        zz = lax.rem(z + k, 4)
        return zz, zz * 4 + yc

    def of_eight(k):
        j = lax.rem(dp * 4 + yc + k, 8)
        return j, lax.div(j, 4), z * 4 + lax.rem(j, 4)

    def loop(low, high, body):
        def step(k, carry):
            body(k)
            return carry

        lax.fori_loop(low, high, step, 0)

    firsts = np.cumsum([0] + list(FAMILIES.values())).tolist()
    fam = SimpleNamespace(**dict(zip(FAMILIES, zip(range(len(FAMILIES)), firsts))))

    def s_of(family):
        return sem_s.at[family[0]]

    def r_of(family, index=0):
        return sem_r.at[family[1] + index]

    def push(family, source, target, dp_to, seq_to, index=0):
        start_push(source, target, s_of(family), r_of(family, index), dp_to, seq_to)

    def arrived(family, ref, index=0):
        wait_for(ref, r_of(family, index))

    barrier = pltpu.get_barrier_semaphore()

    def greet(k):
        _, d, s = everyone(k)
        pl.semaphore_signal(barrier, inc=1, device_id=(d, s), device_id_type=pl.DeviceIdType.MESH)

    loop(1, 2 * PARTS, greet)
    loads = []

    def load(source, target):
        copy = pltpu.make_async_copy(source, target, sem_l.at[len(loads)])
        copy.start()
        loads.append(copy)

    def load_row(source, row):
        target = par_v.at[row] if len(source.shape) == 1 else par_v.at[row : row + 1, :]
        pltpu.make_async_copy(source, target, sem_l.at[LOADS]).start()

    def wait_load(*which):
        for i in which:
            loads[i].wait()

    load(src.embed_table, emb_v)
    load(src.gain_one, par_v.at[0])
    load(src.bias_one, par_v.at[1])
    load(src.in_weight, inw_v)
    load(src.token_ids, tok_v)
    load(src.filter_weight, filt_v)
    LOAD_WEIGHTS = len(loads)
    load(src.up_weight, upw_v)
    load(src.out_weight, outw_v)
    load(src.cotangent, v.seed_all.at[chip])
    load(src.down_weight, downw_v)
    LOAD_NET = len(loads)
    load(src.freq_weight, mlp_v.at[0:33, :])
    load(src.freq_bias, mlp_v.at[33])
    load(src.inner_weight, mlp_v.at[40:104, :])
    load(src.inner_bias, mlp_v.at[104])
    load(src.feats, feats_v)
    LOAD_TAIL = len(loads)
    load(src.mats, mats_v)
    load(src.twist, twist_v)
    for p in range(3):
        at = pl.ds(p * WIDTH, WIDTH)
        load_row(src.in_bias.at[at], 2 + p)
        load_row(src.short_bias.at[at], 14 + p)
        for t in range(3):
            load_row(src.short_taps.at[t : t + 1, at], 5 + 3 * t + p)
    for t in range(2):
        load_row(src.skip_scale.at[t : t + 1, :], 17 + t)
    load(src.out_bias, par_v.at[19])
    load_row(src.gain_two, 20)
    load_row(src.bias_two, 21)
    load_row(src.down_bias, 22)
    for r in range(4):
        load_row(src.up_bias.at[pl.ds(r * WIDTH, WIDTH)], 23 + r)
    LOAD_END = len(loads)

    wait_load(*range(LOAD_WEIGHTS))
    lanes16 = lax.broadcasted_iota(jnp.int32, (IDS, WIDTH), 0)
    embed = jnp.concatenate([emb_v[...], jnp.zeros((4, WIDTH), F32)], axis=0)
    center = embed - jnp.mean(embed, axis=-1, keepdims=True)
    inverse_one = lax.rsqrt(jnp.mean(center * center, axis=-1, keepdims=True) + epsilon)
    unit_one = center * inverse_one
    normed = (unit_one * par_v[0:1, :] + par_v[1:2, :]).astype(BF16).astype(F32)
    normed = jnp.where(lanes16 < 12, normed, 0.0)
    normed_t = v.normed_t
    normed_t[...] = normed.T
    in_low = inw_v[...].astype(BF16).astype(F32)
    partial = dot32(normed_t[tile(me, 24), :], in_low, 0, 0, None)
    p_send, p_recv = v.p_send, v.p_recv
    for i in range(PARTS):
        block = [partial[:, p * WIDTH + i * LOCAL : p * WIDTH + (i + 1) * LOCAL] for p in range(3)]
        p_send[i] = jnp.concatenate(block + [jnp.zeros((IDS, 256 - 3 * LOCAL), F32)], axis=1).astype(BF16)
    filt_all, tok_all = v.filt_all, v.tok_all
    filt_all[dp] = filt_v[...].astype(BF16)
    tok_all[seq] = tok_v[...]
    p_recv[seq] = p_send[seq]
    mlp_v[34:40, :] = jnp.zeros((6, 64), F32)
    mlp_v[105:112, :] = jnp.zeros((7, 64), F32)

    pl.semaphore_wait(barrier, 2 * PARTS - 1)

    def push_p(k):
        s = of_seq(k)
        push(fam.p, p_send.at[s], p_recv.at[seq], dp, s)

    loop(1, PARTS, push_p)
    wait_load(*range(LOAD_WEIGHTS, LOAD_NET))
    up_send, up_all, out_all, seed_all = v.up_send, v.up_all, v.out_all, v.seed_all
    out_all[core, chip, z] = outw_v[...].astype(BF16)

    def push_out(k):
        zz, s = of_line(k)
        mine = out_all.at[core, chip, z]
        push(fam.outz, mine, mine, dp, s)

    loop(1, 4, push_out)

    def push_tok(k):
        s = of_seq(k)
        push(fam.tok, tok_v, tok_all.at[seq], dp, s)

    loop(1, PARTS, push_tok)
    push(fam.filt, filt_all.at[dp], filt_all.at[dp], other_dp, seq)


    def shard_of(q, c, zz):
        return (q // 2) * PARTS + zz * 4 + (q % 2) * 2 + c

    for q in range(4):
        cut = [
            upw_v[:, 96 * shard_of(q, c, zz) : 96 * (shard_of(q, c, zz) + 1)]
            for c in range(2)
            for zz in range(4)
        ]
        up_send[q] = jnp.concatenate(cut, axis=1).astype(BF16)

    def push_up(k):
        q, d, s = of_plane(k)
        push(fam.up, up_send.at[q], up_all.at[core, z, chip], d, s)

    across = lax.rem(z + 2, 4)
    beside = z + 1 - 2 * lax.rem(z, 2)
    beside_across = lax.rem(beside + 2, 4)

    def to_twin(family, source, target=None):
        push(family, source, source if target is None else target, dp, twin)

    def relay(family, onward, ref, block, zz):
        start_push(ref.at[block], ref.at[block], s_of(onward), r_of(family, block), dp, zz * 4 + yc)

    def spread_start(family, ref):
        @pl.when(z > 0)
        def _():
            relay(family, family, ref, z, z - 1)

        @pl.when(z < 3)
        def _():
            relay(family, family, ref, z, z + 1)

    def spread_near(family, onward, twins, ref):
        @pl.when(z > 0)
        def _():
            arrived(family, ref.at[0], z - 1)

            @pl.when(z < 3)
            def _():
                relay(family, onward, ref, z - 1, z + 1)

            to_twin(twins, ref.at[z - 1])

        @pl.when(z < 3)
        def _():
            arrived(family, ref.at[0], z + 1)

            @pl.when(z > 0)
            def _():
                relay(family, onward, ref, z + 1, z - 1)

            to_twin(twins, ref.at[z + 1])

    def spread_far(family, onward, twins, ref):
        arrived(family, ref.at[0], across)

        @pl.when(z == 1)
        def _():
            relay(family, onward, ref, across, 0)

        @pl.when(z == 2)
        def _():
            relay(family, onward, ref, across, 3)

        to_twin(twins, ref.at[across])

    def spread_last(family, twins, ref):
        @pl.when(lax.rem(z, 3) == 0)
        def _():
            arrived(family, ref.at[0], 3 - z)
            to_twin(twins, ref.at[3 - z])

    def to_line(family, source, target, zz, index):
        push(family, source, target, dp, zz * 4 + yc, index)

    loop(1, 4, push_up)
    down_all = v.down_all
    down_all[core, z] = downw_v[...].astype(BF16)
    spread_start(fam.down, down_all.at[core])
    to_twin(fam.downt, down_all.at[core, z])
    up_all[core, z, chip] = up_send[chip]
    act1, cos1, act2, cos2 = v.act1, v.cos1, v.act2, v.cos2
    wait_load(*range(LOAD_NET, LOAD_TAIL))
    mlp = mlp_v[...]
    freq_t = mlp[0:40].T
    inner_bias = mlp[104:112].T[:, 0:1]
    inner = mlp[40:104]

    def network(i):
        at = tile(i, 512)
        s1, c1 = sin_cos(dot32(freq_t, feats_v[:, at], 1, 0))
        act1[0:64, at] = s1
        cos1[:, at] = c1
        act1[64:72, at] = jnp.where(
            lax.broadcasted_iota(jnp.int32, (8, 512), 0) == 0, 1.0, 0.0
        ).astype(F32)
        s2, c2 = sin_cos(dot32(inner, s1, 0, 0) + inner_bias)
        act2[:, at] = s2
        cos2[:, at] = c2

    loop(0, 4, network)
    def gather_first(family, ref, k):
        _, d, s = of_plane(k)
        push(family, ref.at[chip], ref.at[chip], d, s, 0)

    def gather_second(family, ref, k):
        arrived(family, ref.at[0], 0)
        q, _, _ = of_plane(k)
        _, d, s = of_plane(3 - k)
        push(family, ref.at[chip], ref.at[chip], d, s, 1)
        push(family, ref.at[q], ref.at[q], d, s, 1)


    wait_load(*range(LOAD_TAIL, LOAD_END))
    wait_for(par_v.at[0:24], sem_l.at[LOADS])
    par_t = v.par_t
    for i in range(WIDTH // 128):
        par_t[128 * i : 128 * (i + 1), :] = par_v[:, 128 * i : 128 * (i + 1)].T
    own_par = par_t[tile(seq, LOCAL), :]

    kern, hi_ref, lo_ref = v.kern, v.hi, v.lo
    spec_k1, spec_k2, spec_v, spec_g = v.spec_k1, v.spec_k2, v.spec_v, v.spec_g
    arrived(fam.filt, filt_all.at[0])
    filt = jnp.concatenate([filt_all[0], filt_all[1]], axis=0).astype(F32)
    for i in range(LENGTH // 256):
        both = dot32(filt, act2[:, 256 * i : 256 * (i + 1)], 1, 0)
        for h in range(2):
            for f in range(2):
                kern[f, 2 * i + h] = both[f * LOCAL : (f + 1) * LOCAL, 128 * h : 128 * (h + 1)]
    lane = lax.broadcasted_iota(jnp.int32, (LANE_CH, ROWS), 1).astype(F32)

    def decay_of(g):
        row = lax.broadcasted_iota(jnp.int32, (LANE_CH, ROWS), 0) + (seq * LOCAL + g * LANE_CH)
        rate = slow_rate + (fast_rate - slow_rate) * (row.astype(F32) * (1.0 / (WIDTH - 1)))
        return lambda a: jnp.exp((lane + float(a * ROWS)) * (rate * (-1.0 / LENGTH))) + decay_shift

    turn = [0]

    def put(row0, k, re, im):
        rows = pl.ds(row0 + k * LANE_CH, LANE_CH)
        for part, value in ((0, re), (1, im)):
            at = pl.ds(part * ROWS, ROWS)
            high = value.astype(BF16)
            hi_ref[turn[0], rows, at] = high
            lo_ref[turn[0], rows, at] = (value - high.astype(F32)).astype(BF16)

    def forth(row0, values):
        for k, (re, im) in enumerate(real_spectrum(values)):
            c, s = twist_v[k : k + 1, :], twist_v[17 + k : 18 + k, :]
            if im is None:
                put(row0, k, re * c, re * (-s))
            else:
                put(row0, k, re * c + im * s, im * c - re * s)

    def dft(rows, which):
        high, low = hi_ref[turn[0], 0:rows, :], lo_ref[turn[0], 0:rows, :]
        m_high, m_low = mats_v[which], mats_v[which + 1]
        return dot16(high, m_high, 1, 0) + dot16(low, m_high, 1, 0) + dot16(high, m_low, 1, 0)

    def put_product(row0, spec, other, conj):
        a_re, a_im = spec[:, 0:ROWS], spec[:, ROWS:]
        b_re, b_im = other[:, 0:ROWS], other[:, ROWS:]
        if conj:
            re, im = a_re * b_re + a_im * b_im, a_im * b_re - a_re * b_im
        else:
            re, im = a_re * b_re - a_im * b_im, a_re * b_im + a_im * b_re
        rows = pl.ds(row0, SPEC)
        for part, value in ((0, re), (1, im)):
            at = pl.ds(part * ROWS, ROWS)
            high = value.astype(BF16)
            hi_ref[turn[0], rows, at] = high
            lo_ref[turn[0], rows, at] = (value - high.astype(F32)).astype(BF16)

    def back(turned, row0):
        bins = []
        for k in range(BINS):
            part = turned[row0 + k * LANE_CH : row0 + (k + 1) * LANE_CH]
            re, im = part[:, 0:ROWS], part[:, ROWS:]
            c, s = twist_v[34 + k : 35 + k, :], twist_v[51 + k : 52 + k, :]
            if k in (0, PARTS):
                bins.append((re * c - im * s, None))
            else:
                bins.append((re * c - im * s, im * c + re * s))
        return real_signal(bins)

    def kernel_spectra(g):
        turn[0] = g
        at = tile(g, LANE_CH)
        decay = decay_of(g)
        damp = [decay(a) for a in range(PARTS)]
        forth(0, [kern[0, a, at, :] * damp[a] for a in range(PARTS)])
        forth(SPEC, [kern[1, a, at, :] * damp[a] for a in range(PARTS)])
        spec = dft(2 * SPEC, 0)
        spec_k1[g] = spec[0:SPEC]
        spec_k2[g] = spec[SPEC:]

    kernel_spectra(0)
    kernel_spectra(1)

    arrived(fam.p, p_recv.at[0 : PARTS - 1])
    table = p_recv[0].astype(F32)
    for s in range(1, PARTS):
        table = table + p_recv[s].astype(F32)
    px_send, px_recv = v.px_send, v.px_recv
    px_send[...] = table
    push(fam.px, px_send, px_recv, other_dp, seq)
    arrived(fam.up, up_send.at[0:3])
    spread_start(fam.upz, up_all.at[core])
    to_twin(fam.upt, up_all.at[core, z])
    arrived(fam.outz, out_all.at[0, 0, 0:3])
    gather_first(fam.outp, out_all.at[core], 2 - core)
    to_twin(fam.outt, out_all.at[core, chip])
    kernel_spectra(2)
    spread_near(fam.down, fam.downf, fam.downt, down_all.at[core])


    table_t, onehot, mix = v.table_t, v.onehot, v.mix
    arrived(fam.px, px_recv)
    wide_t = (px_send[...] + px_recv[...]).T
    table_t[...] = jnp.concatenate(
        [wide_t[p * LOCAL : (p + 1) * LOCAL] + own_par[:, 2 + p : 3 + p] for p in range(3)], axis=0
    )

    arrived(fam.tok, tok_all.at[0 : PARTS - 1])
    id_rows = lax.broadcasted_iota(jnp.int32, (IDS, ROWS), 0)
    for a in range(PARTS):
        now = tok_all[a]
        if a == 0:
            long = jnp.concatenate([jnp.full((1, ROWS), -1, jnp.int32), now], axis=1)
        else:
            long = jnp.concatenate([tok_all[a - 1], now], axis=1)
        for t in range(3):
            moved = long[:, ROWS - 2 + t : 2 * ROWS - 2 + t]
            onehot[t * IDS : (t + 1) * IDS, a * ROWS : (a + 1) * ROWS] = (
                id_rows == moved
            ).astype(F32)

    def taps_of(t):
        return jnp.concatenate(
            [own_par[:, 5 + 3 * t + p : 6 + 3 * t + p] for p in range(3)], axis=0
        )

    short = jnp.concatenate([taps_of(t) * table_t[...] for t in range(3)], axis=1)
    short_bias = jnp.concatenate([own_par[:, 14 + p : 15 + p] for p in range(3)], axis=0)
    for i in range(LENGTH // 256):
        both = dot32(short, onehot[:, 256 * i : 256 * (i + 1)], 1, 0) + short_bias
        for h in range(2):
            for p in range(3):
                mix[p, 2 * i + h] = both[p * LOCAL : (p + 1) * LOCAL, 128 * h : 128 * (h + 1)]

    first_s, gated_s, second_s = v.first, v.gated, v.second
    mix_send, mix_recv = v.mix_send, v.mix_recv
    gm_send, gm_recv = v.gm_send, v.gm_recv

    def exchange(family, send, recv):
        def one(k):
            s = of_seq(k)
            push(family, send.at[s], recv.at[seq], dp, s)

        loop(1, PARTS, one)

    def operator(g):
        turn[0] = g
        at = tile(g, LANE_CH)
        skips = par_t[pl.ds(pl.multiple_of(seq * LOCAL + g * LANE_CH, LANE_CH), LANE_CH), :]
        skip0, skip1 = skips[:, 17:18], skips[:, 18:19]
        forth(0, [mix[2, a, at, :] for a in range(PARTS)])
        spec = dft(SPEC, 0)
        spec_v[g] = spec
        put_product(0, spec, spec_k1[g], False)
        signal = back(dft(SPEC, 2), 0)
        gated = []
        for a in range(PARTS):
            conv = signal[a] + skip0 * mix[2, a, at, :]
            first_s[a, at, :] = conv
            gate = mix[1, a, at, :] * conv
            gated_s[a, at, :] = gate
            gated.append(gate)
        forth(0, gated)
        spec = dft(SPEC, 0)
        spec_g[g] = spec
        put_product(0, spec, spec_k2[g], False)
        signal = back(dft(SPEC, 2), 0)
        for a in range(PARTS):
            conv = signal[a] + skip1 * gated_s[a, at, :]
            second_s[a, at, :] = conv
            mix_send[a, at, :] = (mix[0, a, at, :] * conv).astype(BF16)


    gather_second(fam.outp, out_all.at[core], 2 - core)
    gather_first(fam.seed, seed_all, 2 - core)
    for g in range(GROUPS):
        operator(g)
    exchange(fam.mix, mix_send, mix_recv)
    spread_near(fam.upz, fam.upf, fam.upt, up_all.at[core])
    mix_recv[seq] = mix_send[seq]

    own_onehot = (id_rows == tok_v[...]).astype(F32)
    resid, unit2, inv2, n2_all = v.resid, v.unit2, v.inv2, v.n2_all
    resid[...] = dot32(own_onehot, embed, 0, 0) + par_v[19:20, :]
    arrived(fam.outp, out_all.at[0, 0:2], 1)

    def forward_out(k):
        q, _, _ = of_plane(k)
        to_twin(fam.outt, out_all.at[core, q])

    loop(1, 4, forward_out)
    w_up, w_out = v.w_up, v.w_out
    arrived(fam.outt, out_all.at[0])

    def place_out(i):
        q, zz = lax.div(i, 8) * 2 + lax.rem(i, 2), lax.rem(lax.div(i, 2), 4)
        both = jnp.concatenate(
            [out_all[0, q, zz].astype(F32), out_all[1, q, zz].astype(F32)], axis=0
        )
        w_out[tile(i, 48), :] = both.astype(BF16)

    loop(0, 16, place_out)
    arrived(fam.mix, mix_recv.at[0 : PARTS - 1])


    mixer_t = mix_recv[...].reshape(WIDTH, ROWS)
    residual = resid[...] + dot16(mixer_t, w_out[...], 0, 0)
    resid[...] = residual
    center = residual - jnp.mean(residual, axis=-1, keepdims=True)
    inv = lax.rsqrt(jnp.mean(center * center, axis=-1, keepdims=True) + epsilon)
    inv2[...] = inv
    unit = center * inv
    unit2[...] = unit
    n2_all[chip] = (unit * par_v[20:21, :] + par_v[21:22, :]).astype(BF16)

    def push_n2(k, q):
        _, d, s = of_plane(k)
        push(fam.n2, n2_all.at[q], n2_all.at[q], d, s, q)

    push_n2(1, chip)
    push_n2(2, chip)
    gather_second(fam.seed, seed_all, 2 - core)
    spread_far(fam.upz, fam.upf, fam.upt, up_all.at[core])
    spread_far(fam.down, fam.downf, fam.downt, down_all.at[core])

    up_bias = jnp.zeros((1, SPLIT), F32)
    for q in range(4):
        cut = []
        for c in range(2):
            for zz in range(4):
                first = 96 * shard_of(q, c, zz)
                row, lane0 = first // WIDTH, first % WIDTH
                cut.append(par_v[23 + row : 24 + row, lane0 : lane0 + 96])
        up_bias = jnp.where(chip == q, jnp.concatenate(cut, axis=1), up_bias)

    spread_last(fam.upz, fam.upt, up_all.at[core])
    arrived(fam.upt, up_all.at[0])

    def place_up(i):
        q, zz = lax.div(i, 8) * 2 + lax.rem(i, 2), lax.rem(lax.div(i, 2), 4)
        both = jnp.concatenate(
            [up_all[0, zz, q].astype(F32), up_all[1, zz, q].astype(F32)], axis=0
        )
        w_up[tile(i, 48), :] = both.astype(BF16)

    loop(0, 16, place_up)
    act_all, gl_all, po_all, gn_all, slope = v.act_all, v.gl_all, v.po_all, v.gn_all, v.slope
    gn_recv, po_recv = v.gn_recv, v.po_recv

    def feed(k):
        q, _, _ = of_plane(k)
        lifted = dot16(n2_all[q], w_up[...], 1, 0) + up_bias
        cdf = 0.5 * (1.0 + lax.erf(lifted * (1.0 / math.sqrt(2.0))))
        pdf = jnp.exp(-0.5 * lifted * lifted) * (1.0 / math.sqrt(2.0 * math.pi))
        act_all[q] = (lifted * cdf).astype(BF16)
        slope[q] = cdf + lifted * pdf

    feed(0)
    first_k = 2 - core
    first_q, _, _ = of_plane(first_k)
    arrived(fam.n2, n2_all.at[0], first_q)
    push_n2(3 - first_k, first_q)
    feed(first_k)
    second_q, _, _ = of_plane(3 - first_k)
    arrived(fam.n2, n2_all.at[0], second_q)
    feed(3 - first_k)
    last_q, _, _ = of_plane(3)
    arrived(fam.n2, n2_all.at[0], last_q)
    feed(3)
    arrived(fam.seed, seed_all.at[0:2], 1)

    sd_x, sd_y, sd_t, sd_z = v.sd_x, v.sd_y, v.sd_t, v.sd_z
    su_x, su_y, su_t, su_z, su_p, su_r = v.su_x, v.su_y, v.su_t, v.su_z, v.su_p, v.su_r
    so_x, so_y, so_t, so_p, so_u, so_z = v.so_x, v.so_y, v.so_t, v.so_p, v.so_u, v.so_z
    acts = act_all[...].reshape(4 * ROWS, SPLIT)
    seeds = seed_all[...].reshape(4 * ROWS, WIDTH)
    for c in range(2):
        half = acts[:, c * 384 : (c + 1) * 384]
        sd_x[c] = dot16(half, seeds, 0, 0).astype(BF16).reshape(4, 96, WIDTH)
    to_twin(fam.sdt, sd_x.at[other_core], sd_y)

    def add_sd(zz):
        sd_t[zz] = (sd_x[core, zz].astype(F32) + sd_y[zz].astype(F32)).astype(BF16)

    def add_su(zz):
        for q in range(4):
            su_t[zz, q] = (su_x[core, zz, q].astype(F32) + su_y[zz, q].astype(F32)).astype(BF16)

    def fold_send(family, sums, landing, block, zz, side):
        to_line(family, sums.at[block], landing.at[side, block], zz, side * 4 + block)

    def fold_add(family, sums, landing, block, side):
        arrived(family, landing.at[side, block], side * 4 + block)
        sums[block] = (sums[block].astype(F32) + landing[side, block].astype(F32)).astype(BF16)

    def fold_start(family, sums, landing, blocks):
        @pl.when(z == 0)
        def _():
            for far in blocks:
                fold_send(family, sums, landing, far, 1, 0)

        @pl.when(z == 3)
        def _():
            for far in blocks:
                fold_send(family, sums, landing, 3 - far, 2, 1)

    def fold_middle(family, sums, landing):
        @pl.when(z == 1)
        def _():
            for block in (3, 2):
                fold_add(family, sums, landing, block, 0)
                fold_send(family, sums, landing, block, 2, 0)

        @pl.when(z == 2)
        def _():
            for block in (0, 1):
                fold_add(family, sums, landing, block, 1)
                fold_send(family, sums, landing, block, 1, 1)

    def fold_end(family, sums, landing):
        @pl.when(z == 2)
        def _():
            fold_add(family, sums, landing, 3, 0)
            fold_send(family, sums, landing, 3, 3, 0)

        @pl.when(z == 1)
        def _():
            fold_add(family, sums, landing, 0, 1)
            fold_send(family, sums, landing, 0, 0, 1)

    def fold_total(family, sums, landing, total):
        total[...] = sums[z].astype(F32)

        @pl.when(z > 0)
        def _():
            arrived(family, landing.at[0, z], z)
            total[...] = total[...] + landing[0, z].astype(F32)

        @pl.when(z < 3)
        def _():
            arrived(family, landing.at[1, z], 4 + z)
            total[...] = total[...] + landing[1, z].astype(F32)

    spread_last(fam.down, fam.downt, down_all.at[core])
    arrived(fam.downt, down_all.at[0])

    def feed_back(k, bias_sum):
        q, d, s = of_plane(lax.rem(k, 4))
        grad_act = dot16(seed_all[q], down_all[...].reshape(SPLIT, WIDTH), 1, 1)
        grad_lifted = grad_act * slope[q]
        gl_all[q] = grad_lifted.astype(BF16)
        gn_all[q] = dot16(gl_all[q], w_up[...], 1, 1).astype(BF16)

        @pl.when(k != 4)
        def _():
            push(fam.gn, gn_all.at[q], gn_recv.at[chip], d, s)

        return bias_sum + jnp.sum(grad_lifted, axis=0, keepdims=True)

    grad_up_bias = lax.fori_loop(1, 3, feed_back, jnp.zeros((1, SPLIT), F32))
    arrived(fam.sdt, sd_y)
    loop(0, 4, add_sd)
    fold_start(fam.sd, sd_t, sd_z, (3, 2))
    grad_up_bias = lax.fori_loop(3, 5, feed_back, grad_up_bias)
    gn_recv[chip] = gn_all[chip]
    units = n2_all[...].reshape(4 * ROWS, WIDTH)
    lows = gl_all[...].reshape(4 * ROWS, SPLIT)
    for x in range(2):
        part = dot16(units[:, x * 384 : (x + 1) * 384], lows, 0, 0)
        for i in range(16):
            su_x[i % 2, i // 4, x * 2 + (i // 2) % 2] = part[24 * i : 24 * (i + 1)].astype(BF16)
    to_twin(fam.sut, su_x.at[other_core], su_y)
    arrived(fam.sut, su_y)
    loop(0, 4, add_su)
    fold_start(fam.su, su_t, su_z, (3, 2))


    def outputs_part(k):
        q, _, _ = of_plane(k)
        po_all[q] = dot16(act_all[q], down_all[...].reshape(SPLIT, WIDTH), 1, 0).astype(BF16)

    loop(0, 4, outputs_part)

    fold_middle(fam.sd, sd_t, sd_z)

    arrived(fam.gn, gn_all.at[0:3])
    grad_n2 = gn_recv[0].astype(F32)
    for q in range(1, 4):
        grad_n2 = grad_n2 + gn_recv[q].astype(F32)
    unit, inv = unit2[...], inv2[...]
    seed = seed_all[chip].astype(F32)
    scaled = grad_n2 * par_v[20:21, :]
    grad_res = seed + inv * (
        scaled
        - jnp.mean(scaled, axis=-1, keepdims=True)
        - unit * jnp.mean(scaled * unit, axis=-1, keepdims=True)
    )
    gres = v.gres
    gres[...] = grad_res.astype(BF16)
    gm_send[...] = dot16(w_out[...], gres[...], 1, 1).astype(BF16).reshape(PARTS, LOCAL, ROWS)
    exchange(fam.gm, gm_send, gm_recv)
    gm_recv[seq] = gm_send[seq]

    def sum_first(family, sums, landing, k):
        q, d, s = of_plane(k)
        push(family, sums.at[q], landing.at[0], d, s, 0)
        q, _, _ = of_plane(3)
        push(family, sums.at[q], landing.at[1], d, s, 0)

    def sum_second(family, sums, landing, k):
        arrived(family, landing.at[0:2], 0)
        q, d, s = of_plane(3 - k)
        sums[q] = (sums[q].astype(F32) + landing[1].astype(F32)).astype(BF16)
        push(family, sums.at[q], landing.at[2], d, s, 1)

    sum_first(fam.po, po_all, po_recv, 2 - core)
    b_x, b_y, b_p, b_t, b_z, b_f = v.b_x, v.b_y, v.b_p, v.b_t, v.b_z, v.b_f
    b_x[0:12, :] = dot32(own_onehot, grad_res, 1, 0)[0:12]
    b_x[12:13, :] = jnp.sum(grad_res, axis=0, keepdims=True)
    b_x[13:14, :] = jnp.sum(grad_n2 * unit, axis=0, keepdims=True)
    b_x[14:15, :] = jnp.sum(grad_n2, axis=0, keepdims=True)
    b_x[15:16, :] = jnp.sum(seed, axis=0, keepdims=True)
    for q in range(4):
        b_x[16 + q : 17 + q, :] = jnp.where(chip == q, grad_up_bias, 0.0)
    b_x[20:24, :] = jnp.zeros((4, WIDTH), F32)
    to_twin(fam.bt, b_x, b_y)
    for x in range(2):
        part = dot16(mixer_t[x * 384 : (x + 1) * 384], gres[...], 1, 0)
        for i in range(16):
            so_x[i % 2, x * 2 + (i // 2) % 2, i // 4] = part[24 * i : 24 * (i + 1)].astype(BF16)
    to_twin(fam.sot, so_x.at[other_core], so_y)

    def push_b(k):
        q, d, s = of_plane(k)
        mine = b_p.at[chip]
        push(fam.b, mine, mine, d, s)

    def add_so(zz):
        for q in range(4):
            so_t[q, zz] = (so_x[core, q, zz].astype(F32) + so_y[q, zz].astype(F32)).astype(BF16)

    grad_mix, raw, q_s = v.grad_mix, v.raw, v.q_s

    def operator_back(g):
        turn[0] = g
        at = tile(g, LANE_CH)
        skips = par_t[pl.ds(pl.multiple_of(seq * LOCAL + g * LANE_CH, LANE_CH), LANE_CH), :]
        skip0, skip1 = skips[:, 17:18], skips[:, 18:19]
        decay = decay_of(g)

        def rows_at(first, count=LANE_CH):
            return pl.ds(first + g * LANE_CH, count)

        seconds, total = [], jnp.zeros((LANE_CH, ROWS), F32)
        for a in range(PARTS):
            upstream = gm_recv[a, at, :].astype(F32)
            lanes = slice(a * ROWS, (a + 1) * ROWS)
            grad_mix[rows_at(0), lanes] = upstream * second_s[a, at, :]
            grad_second = upstream * mix[0, a, at, :]
            total = total + grad_second * gated_s[a, at, :]
            seconds.append(grad_second)
        q_s[rows_at(0), 49:50] = jnp.sum(total, axis=1, keepdims=True)
        forth(0, seconds)
        spec = dft(SPEC, 0)
        put_product(0, spec, spec_k2[g], True)
        put_product(SPEC, spec, spec_g[g], True)
        turned = dft(2 * SPEC, 2)
        signal = back(turned, 0)
        cross = back(turned, SPEC)
        firsts, total = [], jnp.zeros((LANE_CH, ROWS), F32)
        for a in range(PARTS):
            lanes = slice(a * ROWS, (a + 1) * ROWS)
            raw[rows_at(LOCAL), lanes] = cross[a] * decay(a)
            grad_second = gm_recv[a, at, :].astype(F32) * mix[0, a, at, :]
            grad_gated = skip1 * grad_second + signal[a]
            grad_mix[rows_at(LOCAL), lanes] = grad_gated * first_s[a, at, :]
            grad_first = grad_gated * mix[1, a, at, :]
            total = total + grad_first * mix[2, a, at, :]
            grad_mix[rows_at(2 * LOCAL), lanes] = skip0 * grad_first
            firsts.append(grad_first)
        q_s[rows_at(0), 48:49] = jnp.sum(total, axis=1, keepdims=True)
        forth(0, firsts)
        spec = dft(SPEC, 0)
        put_product(0, spec, spec_k1[g], True)
        put_product(SPEC, spec, spec_v[g], True)
        turned = dft(2 * SPEC, 2)
        signal = back(turned, 0)
        cross = back(turned, SPEC)
        for a in range(PARTS):
            lanes = slice(a * ROWS, (a + 1) * ROWS)
            raw[rows_at(0), lanes] = cross[a] * decay(a)
            grad_mix[rows_at(2 * LOCAL), lanes] = grad_mix[rows_at(2 * LOCAL), lanes] + signal[a]

    def sums_of_rows():
        arrived(fam.bt, b_y)
        for c in range(2):

            @pl.when(core == c)
            def _():
                at = slice(c * 384, (c + 1) * 384)
                b_p[chip] = (b_x[:, at] + b_y[:, at]).astype(BF16)

        loop(1, 4, push_b)

    arrived(fam.sot, so_y)
    loop(0, 4, add_so)
    sum_first(fam.so, so_t, so_p, 2 - core)
    sums_of_rows()
    arrived(fam.gm, gm_recv.at[0 : PARTS - 1])
    fold_end(fam.sd, sd_t, sd_z)
    fold_middle(fam.su, su_t, su_z)
    fold_start(fam.su, su_t, su_z, (1,))
    fold_start(fam.sd, sd_t, sd_z, (1,))
    for g in range(GROUPS):
        operator_back(g)
    fold_end(fam.su, su_t, su_z)
    sum_second(fam.so, so_t, so_p, 2 - core)
    sum_second(fam.po, po_all, po_recv, 2 - core)
    arrived(fam.b, b_p.at[0:3])
    b_t[...] = (
        (b_p[0].astype(F32) + b_p[1].astype(F32)) + (b_p[2].astype(F32) + b_p[3].astype(F32))
    ).astype(BF16)
    b_z[z] = b_t[...]

    def push_b2(k):
        zz, s = of_line(k)
        push(fam.b2, b_t, b_z.at[z], dp, s)

    loop(1, 4, push_b2)

    zx_send, zx_recv, z_send, z_recv = v.zx_send, v.zx_recv, v.z_send, v.z_recv
    by_id = dot32(grad_mix[...], onehot[...], 1, 1)
    sums = sum(taps_of(t) * by_id[:, t * IDS : (t + 1) * IDS] for t in range(3))
    taps_grad = [
        jnp.sum(table_t[...] * by_id[:, t * IDS : (t + 1) * IDS], axis=1, keepdims=True)
        for t in range(3)
    ]
    bias_grad = jnp.sum(by_id[:, 2 * IDS : 3 * IDS], axis=1, keepdims=True)
    columns = jnp.concatenate([sums[:, 0:12]] + taps_grad + [bias_grad], axis=1)
    skip_cols = jnp.concatenate(
        [q_s[:, 48:50], jnp.zeros((LOCAL, 14), F32)], axis=1
    )
    zx_send[...] = jnp.concatenate(
        [columns, skip_cols, jnp.zeros((64, IDS), F32)], axis=0
    ).T
    push(fam.zx, zx_send, zx_recv, other_dp, seq)

    f_send, f_recv, m_send, m_recv, m2_send, m2_recv = (v.f_send, v.f_recv, v.m_send, v.m_recv, v.m2_send, v.m2_recv)
    grad_filter = dot32(raw[...], act2[...], 1, 1)
    f_send[...] = grad_filter
    there = f_send.at[tile(other_dp, LOCAL), :]
    push(fam.f, there, f_recv, other_dp, seq)
    grad_second_pre = dot32(filt, raw[...], 0, 0) * cos2[...]
    grad_inner = dot32(act1[...], grad_second_pre, 1, 1)
    grad_first_pre = dot32(inner, grad_second_pre, 1, 0) * cos1[...]
    grad_freq = dot32(feats_v[...], grad_first_pre, 1, 1)
    m_send[...] = jnp.concatenate(
        [
            jnp.concatenate([grad_freq, jnp.zeros((40, 64), F32)], axis=0),
            jnp.concatenate([grad_inner, jnp.zeros((8, 64), F32)], axis=0),
        ],
        axis=1,
    ).astype(BF16)
    j_me = dp * 4 + yc
    m_recv[j_me] = m_send[...]

    def push_m(k):
        j, d, s = of_eight(k)
        push(fam.m, m_send, m_recv.at[j_me], d, s)

    loop(1, 8, push_m)

    arrived(fam.zx, zx_recv)
    z_send[...] = (zx_send[...] + zx_recv[...]).astype(BF16)
    z_recv[seq] = z_send[...]

    def push_z(k):
        s = of_seq(k)
        push(fam.z, z_send, z_recv.at[seq], dp, s)

    loop(1, PARTS, push_z)
    arrived(fam.so, so_p.at[0], 1)
    for zz in range(4):
        part = so_t[chip, zz].astype(F32) + so_p[0, zz].astype(F32) + so_p[2, zz].astype(F32)
        so_u[zz] = part.astype(BF16)
    so_z[z] = so_u[z]

    def push_so2(k):
        zz, s = of_line(k)
        push(fam.so2, so_u.at[zz], so_z.at[z], dp, s)

    loop(1, 4, push_so2)
    fold_total(fam.su, su_t, su_z, v.su_f)
    su_p[...] = v.su_f[...].astype(BF16)
    su_r[chip] = su_p[chip]

    def push_su2(k):
        q, d, s = of_plane(k)
        push(fam.su2, su_p.at[q], su_r.at[chip], d, s)

    loop(1, 4, push_su2)


    arrived(fam.m, m_recv.at[0:7])
    totals = m_recv[0].astype(F32)
    for j in range(1, 8):
        totals = totals + m_recv[j].astype(F32)
    m2_send[...] = totals.astype(BF16)
    m2_recv[z] = m2_send[...]

    def push_m2(k):
        zz, s = of_line(k)
        push(fam.m2, m2_send, m2_recv.at[z], dp, s)

    loop(1, 4, push_m2)

    wide, gt_all = v.wide, v.gt_all
    arrived(fam.z, z_recv.at[0 : PARTS - 1])
    for p in range(4):
        for i in range(PARTS):
            wide[:, p * WIDTH + i * LOCAL : p * WIDTH + (i + 1) * LOCAL] = z_recv[i][
                :, p * LOCAL : (p + 1) * LOCAL
            ].astype(F32)
    by_ids = jnp.where(
        lax.broadcasted_iota(jnp.int32, (IDS, 3 * WIDTH), 0) < 12, wide[:, 0 : 3 * WIDTH], 0.0
    )
    own_gt = dot32(in_low, by_ids, 1, 1)
    gt_all[me] = jnp.concatenate(
        [own_gt[8 * t : 8 * (t + 1)] for t in range(3)] + [jnp.zeros((8, 80), F32)], axis=1
    )

    def push_gt(k):
        _, d, s = everyone(k)
        mine = gt_all.at[me]
        push(fam.gt, mine, mine, d, s)

    loop(1, 2 * PARTS, push_gt)

    stores = []

    def store(source, target):
        copy = pltpu.make_async_copy(source, target, sem_o.at[len(stores)])
        copy.start()
        stores.append(copy)

    o_in, o_wide, o_rows = v.o_in, v.o_wide, v.o_rows
    o_in[...] = dot32(normed_t[tile(me, 24), :], by_ids, 1, 0)
    o_wide[...] = jnp.sum(by_ids, axis=0, keepdims=True)
    o_rows[2:4, :] = wide[0:2, 3 * WIDTH :]
    store(o_in, out.in_weight)
    store(o_wide.at[0], out.in_bias)
    store(wide.at[12:15, 0 : 3 * WIDTH], out.short_taps)
    store(wide.at[15, pl.ds(0, 3 * WIDTH)], out.short_bias)
    store(o_rows.at[2:4, :], out.skip_scale)

    arrived(fam.po, po_recv.at[0], 1)
    block = resid[...] + par_v[22:23, :] + po_all[chip].astype(F32)
    block = block + po_recv[0].astype(F32) + po_recv[2].astype(F32)
    resid[...] = block
    store(resid, out.block)

    fold_total(fam.sd, sd_t, sd_z, downw_v)
    store(downw_v, out.down_weight)
    arrived(fam.f, f_recv)
    f_recv[...] = f_send[tile(dp, LOCAL), :] + f_recv[...]
    store(f_recv, out.filter_weight)

    arrived(fam.su2, su_r.at[0:3])
    for q in range(4):
        part = su_r[q].astype(F32)
        for c in range(2):
            for zz in range(4):
                first, place = 96 * shard_of(q, c, zz), 384 * c + 96 * zz
                upw_v[:, first : first + 96] = part[:, place : place + 96]
    store(upw_v, out.up_weight)

    arrived(fam.b2, b_z.at[0:3])
    b_f[core] = (b_z[0].astype(F32) + b_z[1].astype(F32)) + (b_z[2].astype(F32) + b_z[3].astype(F32))
    to_twin(fam.bf, b_f.at[core])
    arrived(fam.so2, so_z.at[0:3])
    part = so_z[0].astype(F32)
    for zz in range(1, 4):
        part = part + so_z[zz].astype(F32)
    outw_v[...] = part
    store(outw_v, out.out_weight)
    arrived(fam.m2, m2_recv.at[0:3])
    totals = m2_recv[0].astype(F32)
    for zz in range(1, 4):
        totals = totals + m2_recv[zz].astype(F32)
    mlp_v[0:40, :] = totals[0:40, 0:64]
    mlp_v[40:112, :] = totals[0:72, 64:128]
    store(mlp_v.at[0:33, :], out.freq_weight)
    store(mlp_v.at[33], out.freq_bias)
    store(mlp_v.at[40:104, :], out.inner_weight)
    store(mlp_v.at[104], out.inner_bias)
    arrived(fam.bf, b_f.at[0])
    totals = jnp.concatenate([b_f[0], b_f[1]], axis=1)
    o_rows[4:8, :] = totals[12:16]
    o_up = v.o_up
    for q in range(4):
        for c in range(2):
            for zz in range(4):
                first, place = 96 * shard_of(q, c, zz), 384 * c + 96 * zz
                o_up[:, first : first + 96] = totals[16 + q : 17 + q, place : place + 96]
    store(o_rows.at[4], out.out_bias)
    store(o_rows.at[5], out.gain_two)
    store(o_rows.at[6], out.bias_two)
    store(o_rows.at[7], out.down_bias)
    store(o_up.at[0], out.up_bias)

    arrived(fam.gt, gt_all.at[0 : 2 * PARTS - 1])
    gts = gt_all[...]
    grad_normed = jnp.concatenate([gts[:, :, IDS * t : IDS * (t + 1)] for t in range(3)], axis=1)
    grad_normed = grad_normed.reshape(WIDTH, IDS).T
    o_rows[0:1, :] = jnp.sum(grad_normed * unit_one, axis=0, keepdims=True)
    o_rows[1:2, :] = jnp.sum(grad_normed, axis=0, keepdims=True)
    scaled = grad_normed * par_v[0:1, :]
    grad_embed = inverse_one * (
        scaled
        - jnp.mean(scaled, axis=-1, keepdims=True)
        - unit_one * jnp.mean(scaled * unit_one, axis=-1, keepdims=True)
    )
    emb_v[...] = totals[0:12] + grad_embed[0:12]
    store(o_rows.at[0], out.gain_one)
    store(o_rows.at[1], out.bias_one)
    store(emb_v, out.embed_table)

    for family, ref in (
        (fam.p, p_send.at[0 : PARTS - 1]), (fam.tok, tok_all.at[0 : PARTS - 1]), (fam.filt, filt_all.at[0]),
        (fam.px, px_send), (fam.outz, out_all.at[0, 0, 0:3]), (fam.outp, out_all.at[0, 0:3]),
        (fam.outt, out_all.at[0]), (fam.up, up_send.at[0:3]),
        (fam.upt, up_all.at[0]), (fam.seed, seed_all.at[0:3]),
        (fam.downt, down_all.at[0]), (fam.mix, mix_send.at[0 : PARTS - 1]),
        (fam.gm, gm_send.at[0 : PARTS - 1]), (fam.n2, n2_all.at[0:3]), (fam.gn, gn_all.at[0:3]),
        (fam.po, po_all.at[0:3]), (fam.sdt, sd_y), (fam.sut, su_y), (fam.sot, so_y), (fam.sd, sd_t.at[0:3]),
        (fam.su, su_t.at[0:3]), (fam.su2, su_p.at[0:3]), (fam.so, so_t.at[0:3]), (fam.so2, so_u.at[0:3]),
        (fam.bt, b_x), (fam.b, b_p.at[0:3]), (fam.b2, b_z.at[0:3]), (fam.bf, b_f.at[0]),
        (fam.m, m_recv.at[0:7]), (fam.m2, m2_recv.at[0:3]), (fam.z, z_recv.at[0 : PARTS - 1]),
        (fam.zx, zx_send), (fam.f, f_recv), (fam.gt, gt_all.at[0 : 2 * PARTS - 1]),
    ):
        wait_for(ref, s_of(family))
    for family, onward, ref in (
        (fam.upz, fam.upf, up_all.at[0]),
        (fam.down, fam.downf, down_all.at[0]),
    ):

        @pl.when(lax.rem(z, 3) == 0)
        def _():
            wait_for(ref.at[0], s_of(family))

        @pl.when(lax.rem(z, 3) != 0)
        def _():
            wait_for(ref.at[0:2], s_of(family))
            wait_for(ref.at[0:3], s_of(onward))

    for copy in stores:
        copy.wait()


def copy_kernel(*refs):
    count = len(OUTPUTS)
    for source, target in zip(refs[:count], refs[count:]):
        target[...] = source[...]


FAMILIES = dict(
    p=1, tok=1, filt=1, px=1, outz=1, outp=2, outt=1, up=1, upz=4, upf=0, upt=1, down=4, downf=0, downt=1, seed=2, mix=1,
    gm=1, n2=4, gn=1, po=2, sdt=1, sd=8, sut=1, su=8, su2=1, sot=1, so=2, so2=1, bt=1, b=1, b2=1, bf=1,
    m=1, m2=1, z=1, zx=1, f=1, gt=1,
)
LOADS = 18
INPUTS = dict(
    token_ids=0, embed_table=0, gain_one=0, bias_one=0, in_weight=0, in_bias=0, short_taps=0, short_bias=0,
    freq_weight=0, freq_bias=0, inner_weight=0, inner_bias=0, filter_weight=0, skip_scale=0, out_weight=0,
    out_bias=0, gain_two=0, bias_two=0, up_weight=0, up_bias=0, down_weight=0, down_bias=0, cotangent=0,
    mats=0, twist=0, feats=0,
)
OUTPUTS = dict(
    block=(ROWS, WIDTH), embed_table=(12, WIDTH), gain_one=(WIDTH,),
    bias_one=(WIDTH,), in_weight=(24, 3 * WIDTH), in_bias=(3 * WIDTH,),
    short_taps=(3, 3 * WIDTH), short_bias=(3 * WIDTH,), freq_weight=(33, 64),
    freq_bias=(64,), inner_weight=(64, 64), inner_bias=(64,),
    filter_weight=(LOCAL, 64), skip_scale=(2, WIDTH), out_weight=(24, WIDTH),
    out_bias=(WIDTH,), gain_two=(WIDTH,), bias_two=(WIDTH,),
    up_weight=(24, HIDDEN), up_bias=(HIDDEN,), down_weight=(96, WIDTH),
    down_bias=(WIDTH,),
)
SPECTRUM = (GROUPS, SPEC, 2 * ROWS)
SCRATCH = dict(
    tok=((1, ROWS), jnp.int32), emb=((12, WIDTH), F32), par=((32, WIDTH), F32),
    inw=((24, 3 * WIDTH), F32), mlp=((112, 64), F32), filt=((LOCAL, 64), F32),
    outw=((24, WIDTH), F32), upw=((24, HIDDEN), F32), downw=((96, WIDTH), F32),
    mats=((4, 256, 256), BF16), twist=((72, ROWS), F32), feats=((40, LENGTH), F32),
    normed_t=((WIDTH, IDS), F32), p_send=((PARTS, IDS, 256), BF16),
    p_recv=((PARTS, IDS, 256), BF16), px_send=((IDS, 256), F32), px_recv=((IDS, 256), F32),
    filt_all=((2, LOCAL, 64), BF16), tok_all=((PARTS, 1, ROWS), jnp.int32),
    up_send=((4, 24, SPLIT), BF16), up_all=((2, 4, 4, 24, SPLIT), BF16),
    out_all=((2, 4, 4, 24, WIDTH), BF16), seed_all=((4, ROWS, WIDTH), BF16),
    down_all=((2, 4, 96, WIDTH), BF16), w_up=((WIDTH, SPLIT), BF16), w_out=((WIDTH, WIDTH), BF16),
    act1=((72, LENGTH), F32), cos1=((64, LENGTH), F32), act2=((64, LENGTH), F32),
    cos2=((64, LENGTH), F32), kern=((2, PARTS, LOCAL, ROWS), F32), par_t=((WIDTH, 32), F32),
    table_t=((3 * LOCAL, IDS), F32), onehot=((3 * IDS, LENGTH), F32),
    mix=((3, PARTS, LOCAL, ROWS), F32),
    hi=((GROUPS, 2 * SPEC, 2 * ROWS), BF16), lo=((GROUPS, 2 * SPEC, 2 * ROWS), BF16),
    spec_k1=(SPECTRUM, F32), spec_k2=(SPECTRUM, F32), spec_v=(SPECTRUM, F32),
    spec_g=(SPECTRUM, F32),
    first=((PARTS, LOCAL, ROWS), F32), gated=((PARTS, LOCAL, ROWS), F32),
    second=((PARTS, LOCAL, ROWS), F32),
    mix_send=((PARTS, LOCAL, ROWS), BF16), mix_recv=((PARTS, LOCAL, ROWS), BF16),
    gm_send=((PARTS, LOCAL, ROWS), BF16), gm_recv=((PARTS, LOCAL, ROWS), BF16),
    resid=((ROWS, WIDTH), F32), unit2=((ROWS, WIDTH), F32), inv2=((ROWS, 1), F32),
    n2_all=((4, ROWS, WIDTH), BF16), act_all=((4, ROWS, SPLIT), BF16),
    gl_all=((4, ROWS, SPLIT), BF16), slope=((4, ROWS, SPLIT), F32), po_all=((4, ROWS, WIDTH), BF16),
    po_recv=((3, ROWS, WIDTH), BF16), gn_all=((4, ROWS, WIDTH), BF16),
    gn_recv=((4, ROWS, WIDTH), BF16), gres=((ROWS, WIDTH), BF16),
    sd_x=((2, 4, 96, WIDTH), BF16), sd_y=((4, 96, WIDTH), BF16), sd_t=((4, 96, WIDTH), BF16),
    sd_z=((2, 4, 96, WIDTH), BF16),
    su_x=((2, 4, 4, 24, SPLIT), BF16), su_y=((4, 4, 24, SPLIT), BF16),
    su_t=((4, 4, 24, SPLIT), BF16), su_z=((2, 4, 4, 24, SPLIT), BF16), su_f=((4, 24, SPLIT), F32), su_p=((4, 24, SPLIT), BF16),
    su_r=((4, 24, SPLIT), BF16),
    so_x=((2, 4, 4, 24, WIDTH), BF16), so_y=((4, 4, 24, WIDTH), BF16),
    so_t=((4, 4, 24, WIDTH), BF16), so_p=((3, 4, 24, WIDTH), BF16), so_u=((4, 24, WIDTH), BF16),
    so_z=((4, 24, WIDTH), BF16),
    b_x=((24, WIDTH), F32), b_y=((24, WIDTH), F32), b_p=((4, 24, 384), BF16),
    b_t=((24, 384), BF16), b_z=((4, 24, 384), BF16), b_f=((2, 24, 384), F32),
    grad_mix=((3 * LOCAL, LENGTH), F32), raw=((2 * LOCAL, LENGTH), F32), q_s=((LOCAL, 128), F32),
    z_send=((IDS, 256), BF16), z_recv=((PARTS, IDS, 256), BF16), zx_send=((IDS, 256), F32),
    zx_recv=((IDS, 256), F32), wide=((IDS, 4 * WIDTH), F32), gt_all=((32, 8, 128), F32),
    m_send=((80, 128), BF16), m_recv=((8, 80, 128), BF16), m2_send=((80, 128), BF16),
    m2_recv=((4, 80, 128), BF16), f_send=((2 * LOCAL, 64), F32), f_recv=((LOCAL, 64), F32),
    o_in=((24, 3 * WIDTH), F32), o_wide=((1, 3 * WIDTH), F32), o_rows=((8, WIDTH), F32),
    o_up=((1, HIDDEN), F32),
)


def fits(mesh_shape, args):
    return (
        mesh_shape["dp"] == 2
        and mesh_shape["seq"] == PARTS
        and args[0].shape == (1, ROWS)
        and args[1].shape == (12, WIDTH)
        and args[4].shape == (24, 3 * WIDTH)
        and args[8].shape == (33, 64)
        and args[18].shape == (24, HIDDEN)
    )


def fast_device(*args):
    given = SimpleNamespace(**dict(zip(INPUTS, args)))
    tables = tables_of(given.freq_weight.shape[0])
    given.mats, given.twist, given.feats = (jnp.asarray(table) for table in tables)
    given.cotangent = given.cotangent[0]
    anywhere, near = (pl.BlockSpec(memory_space=space) for space in (pl.ANY, pltpu.VMEM))
    shapes = [jax.ShapeDtypeStruct(shape, F32) for shape in OUTPUTS.values()]
    counts = (len(FAMILIES), sum(FAMILIES.values()), LOADS + 1, len(shapes))
    made = pl.pallas_call(
        step_kernel,
        out_shape=shapes,
        in_specs=[anywhere] * len(INPUTS),
        out_specs=[anywhere] * len(shapes),
        scratch_shapes=[pltpu.VMEM(shape, kind) for shape, kind in SCRATCH.values()]
        + [pltpu.SemaphoreType.DMA((count,)) for count in counts],
        compiler_params=pltpu.CompilerParams(
            collective_id=0, has_side_effects=True, vmem_limit_bytes=60 * 1024 * 1024
        ),
    )(*(getattr(given, name) for name in INPUTS))
    made = pl.pallas_call(
        copy_kernel,
        out_shape=shapes,
        in_specs=[near] * len(shapes),
        out_specs=[near] * len(shapes),
    )(*made)
    return (made[0][None], *made[1:])


def solution(mesh):
    in_specs = (
        P("dp", "seq"),
        P(),
        P(),
        P(),
        P(("dp", "seq"), None),
        P(),
        P(),
        P(),
        P(),
        P(),
        P(),
        P(),
        P(("dp", "seq"), None),
        P(),
        P(("dp", "seq"), None),
        P(),
        P(),
        P(),
        P(("dp", "seq"), None),
        P(),
        P(("dp", "seq"), None),
        P(),
        P("dp", "seq", None),
    )
    out_specs = (
        P("dp", "seq", None),
        P(),
        P(),
        P(),
        P(("dp", "seq"), None),
        P(),
        P(),
        P(),
        P(),
        P(),
        P(),
        P(),
        P(("dp", "seq"), None),
        P(),
        P(("dp", "seq"), None),
        P(),
        P(),
        P(),
        P(("dp", "seq"), None),
        P(),
        P(("dp", "seq"), None),
        P(),
    )

    def either(*args):
        return (fast_device if fits(mesh.shape, args) else per_device)(*args)

    return jax.shard_map(
        either, mesh=mesh, in_specs=in_specs, out_specs=out_specs, check_vma=False
    )
```
